32 devices in a mesh: row: 8 (over z, x), col: 4 (over y, core).
Axes of the slice: x: 2, y: 2, z: 4, core: 2. Of those that a mesh axis runs over, the one named last changes fastest.
Arguments:
- tokens: bfloat16 [25216, 768], P(('row', 'col')), may hold values from -6 to 6
- cotangent: bfloat16 [25216, 768], P(('row', 'col')), may hold values from -6 to 6
- routes: int32 [25216, 2], P(('row', 'col')), may hold values from 0 to 3, all different within a row; in each aligned block of 394 rows (0 to 393, 394 to 787, ...) at most 256 rows name the same one
- norm1_gain: bfloat16 [768], P('row'), may hold values from 0.5 to 1.5
- norm1_shift: bfloat16 [768], P('row'), may hold values from -1.75 to 1.75
- attn_in: bfloat16 [768, 3, 768], P('row', None, 'col'), may hold values from -0.21875 to 0.21875
- attn_bias: bfloat16 [2, 768], P(None, 'col'), may hold values from -3 to 3
- attn_proj: bfloat16 [768, 768], P('row', 'col'), may hold values from -0.875 to 0.875
- proj_bias: bfloat16 [768], P('col'), may hold values from -1.75 to 1.75
- norm2_gain: bfloat16 [768], P('row'), may hold values from 0.5 to 1.5
- norm2_shift: bfloat16 [768], P('row'), may hold values from -1.75 to 1.75
- router: bfloat16 [768, 4], P('row', 'col'), may hold values from -0.15625 to 0.15625
- expert_in: bfloat16 [4, 768, 3072], P(None, 'row', 'col'), may hold values from -0.21875 to 0.21875
- expert_in_bias: bfloat16 [4, 3072], P('col', 'row'), may hold values from -3 to 3
- expert_out: bfloat16 [4, 3072, 768], P(None, 'col', 'row'), may hold values from -0.4375 to 0.4375
- expert_out_bias: bfloat16 [4, 768], P('col', 'row'), may hold values from -6 to 6
Outputs:
- output: bfloat16 [25216, 768], P(('row', 'col'))
- input_grad: bfloat16 [25216, 768], P(('row', 'col'))
- grad_norm1_gain: float32 [768], P('row')
- grad_norm1_shift: float32 [768], P('row')
- grad_attn_in: float32 [768, 3, 768], P('row', None, 'col')
- grad_attn_bias: float32 [2, 768], P(None, 'col')
- grad_attn_proj: float32 [768, 768], P('row', 'col')
- grad_proj_bias: float32 [768], P('col')
- grad_norm2_gain: float32 [768], P('row')
- grad_norm2_shift: float32 [768], P('row')
- grad_router: float32 [768, 4], P('row', 'col')
- grad_expert_in: float32 [4, 768, 3072], P(None, 'row', 'col')
- grad_expert_in_bias: float32 [4, 3072], P('col', 'row')
- grad_expert_out: float32 [4, 3072, 768], P(None, 'col', 'row')
- grad_expert_out_bias: float32 [4, 768], P('col', 'row')
The draws below stay inside these ranges and needn't reach their ends.
Inputs may be any that keep to these rules, and one draw needn't show every extreme that they name: `routes`: each row names two different experts. In each aligned block of 394 rows (one device's micro-batch), no expert is named by more than 256 rows.
All inputs are finite; a program needn't handle non-finite values.
Results may differ from the reference program's by a relative error of at most 0.03.
Values may be sent and summed in bfloat16 or wider, within the bound.
A program may use at most 256 MiB of HBM per device.

```python
import math
import jax
import jax.numpy as jnp
import numpy as np
from jax import lax

D = 768
HEADS = 12
HEAD_DIM = 64
FF = 3072
SEQ = 197
IMG_MB = 2
EXPERTS = 4
TOK_DEV = 788
TOKENS = 25216
CAP = 256


def shard_levels(stream_key, extent, pieces, low, top_value):
    level, own = 1.0, jax.random.fold_in(stream_key, 6)
    for axis_at, shards_of in pieces:
        draws = jnp.exp(jax.random.uniform(jax.random.fold_in(own, axis_at), (shards_of,), jnp.float32, low / len(pieces), top_value / len(pieces)))
        level = level * jnp.repeat(draws, extent[axis_at] // shards_of).reshape([-1 if axis == axis_at else 1 for axis in range(len(extent))])
    return level


def routed_block(rng, own, number, rows, count, top, limit, slope):
    sequence = jax.random.permutation(rng, count)
    heavy_load, usual = shares(count, rows * top, limit, slope, True), shares(count, rows * top, limit, slope, False)
    places = jnp.arange(count)

    def named(sizes, turn):
        used = int((sizes > 0).sum())
        fixed = max(1, used // 4)
        moved = fixed + (places - fixed + turn * (used - fixed)) % max(1, count - fixed)
        return jnp.zeros((count,), jnp.int32).at[sequence[jnp.where(places < fixed, places, moved)]].set(jnp.asarray(sizes, jnp.int32))

    sizes = jnp.where(number % 4 == 0, named(heavy_load, number // 4), named(usual, number - number // 4 - 1))
    mixed = jax.random.permutation(jax.random.fold_in(own, 3), count)
    donor, sink = mixed[0:count // 2 * 2:2], mixed[1:count // 2 * 2:2]
    room = jnp.minimum(sizes[donor] - 1, limit - sizes[sink]) // 2
    room = jnp.where((donor == sequence[0]) | (sink == sequence[0]) | (sizes[sink] == 0), 0, jnp.maximum(room, 0))
    moved = jax.random.randint(jax.random.fold_in(own, 4), (count // 2,), 0, 1 << 20) % (room + 1)
    sizes = sizes.at[donor].add(-moved).at[sink].add(moved)
    labels = jnp.searchsorted(jnp.cumsum(sizes), jnp.arange(rows * top), side="right").astype(jnp.int32)
    table = labels.reshape(top, rows).T
    table = table[jax.random.permutation(jax.random.fold_in(own, 1), rows)]
    turn = jax.random.randint(jax.random.fold_in(own, 2), (rows, 1), 0, top)
    return jnp.take_along_axis(table, (jnp.arange(top)[None, :] + turn) % top, axis=1)


def shares(number_of, total, most, lean, full):
    weights = [(1 << 20) // math.isqrt(rank ** lean) + 1 for rank in range(1, number_of + 1)]
    largest = most if full else min(most, max(-(-total // number_of), total * weights[0] // sum(weights)))
    least = 1 if total - largest >= number_of - 1 else 0
    holding, spare = [largest] + [least] * (number_of - 1), total - largest - least * (number_of - 1)
    while spare > 0:
        candidates = [i for i in range(1, number_of) if holding[i] < largest] or [i for i in range(1, number_of) if holding[i] < most]
        mass, remaining = sum([weights[i] for i in candidates]), spare
        for i in candidates:
            extra = min(most - holding[i], max(1, remaining * weights[i] // mass), spare)
            holding[i] = holding[i] + extra
            spare = spare - extra
    return np.array(holding)


def noise(key, shape, spread, reach, cuts=(), kind=jnp.bfloat16):
    values = jax.random.normal(key, shape, jnp.float32) * spread
    if len(cuts) > 0:
        values = shard_levels(key, shape, cuts, -0.22, 0.18) * values
    return jnp.clip(values, min=-reach, max=reach).astype(kind)


def setup_inputs(seed: int = 0) -> dict:
    streams_of = jax.random.split(jax.random.key(seed), 17)
    tokens = noise(streams_of[0], (TOKENS, D), 1.0, 6.0, ((0, 32),))
    cotangent = noise(streams_of[1], (TOKENS, D), 1.0, 6.0, ((0, 32),))
    routes_keys = jax.random.split(jax.random.fold_in(streams_of[2], 1), TOKENS // (IMG_MB * SEQ))
    routes_turns = jax.random.permutation(jax.random.fold_in(streams_of[2], 3), TOKENS // (IMG_MB * SEQ))
    routes = jax.vmap(lambda own, number: routed_block(jax.random.fold_in(streams_of[2], 2), own, number, IMG_MB * SEQ, EXPERTS, 2, CAP, 1))(routes_keys, routes_turns).reshape((TOKENS, 2))
    norm1_gain = jnp.clip(1.0 + 0.1 * jax.random.normal(streams_of[3], (D,), jnp.float32), 0.5, 1.5).astype(jnp.bfloat16)
    norm1_shift = noise(streams_of[4], (D,), 0.3, 1.75, ((0, 8),))
    attn_in = noise(streams_of[5], (D, 3, D), D ** -0.5, 0.21875, ((0, 8), (2, 4)))
    attn_bias = noise(streams_of[6], (2, D), 0.5, 3.0, ((1, 4),))
    attn_proj = noise(streams_of[7], (D, D), (D // 16) ** -0.5, 0.875, ((0, 8), (1, 4)))
    proj_bias = noise(streams_of[8], (D,), 0.3, 1.75, ((0, 4),))
    norm2_gain = jnp.clip(1.0 + 0.1 * jax.random.normal(streams_of[9], (D,), jnp.float32), 0.5, 1.5).astype(jnp.bfloat16)
    norm2_shift = noise(streams_of[10], (D,), 0.3, 1.75, ((0, 8),))
    router = noise(streams_of[11], (D, EXPERTS), (2 * D) ** -0.5, 0.15625, ((0, 8), (1, 4)))
    expert_in = noise(streams_of[12], (EXPERTS, D, FF), D ** -0.5, 0.21875, ((1, 8), (2, 4)))
    expert_in_bias = noise(streams_of[13], (EXPERTS, FF), 0.5, 3.0, ((0, 4), (1, 8)))
    expert_out = noise(streams_of[14], (EXPERTS, FF, D), (max(1, FF // (EXPERTS * EXPERTS))) ** -0.5, 0.4375, ((1, 4), (2, 8)))
    expert_out_bias = noise(streams_of[15], (EXPERTS, D), 1.0, 6.0, ((0, 4), (1, 8)))
    return dict(tokens=tokens, cotangent=cotangent, routes=routes, norm1_gain=norm1_gain, norm1_shift=norm1_shift, attn_in=attn_in, attn_bias=attn_bias, attn_proj=attn_proj, proj_bias=proj_bias, norm2_gain=norm2_gain, norm2_shift=norm2_shift, router=router, expert_in=expert_in, expert_in_bias=expert_in_bias, expert_out=expert_out, expert_out_bias=expert_out_bias)


epsilon = 1e-06

@jax.custom_vjp
def low(v):
    return lax.optimization_barrier(v.astype(jnp.bfloat16)).astype(jnp.float32)

@jax.custom_vjp
def low_back(v):
    return v

def low_keep(v):
    return (low(v), None)

def low_pass(kept, grad):
    return (grad,)

def back_keep(v):
    return (v, None)

def back_low(kept, grad):
    return (low(grad),)
low.defvjp(low_keep, low_pass)
low_back.defvjp(back_keep, back_low)

def matmul(left, right):
    return jnp.dot(left, right, precision=lax.Precision.HIGHEST)

def rounded(values):
    return low(low_back(values))

def norm_rows(row_vals, norm_gain, norm_shift):
    centred = row_vals - lax.optimization_barrier(jnp.mean(row_vals, axis=-1, keepdims=True))
    variance = lax.optimization_barrier(jnp.mean(centred * centred, axis=-1, keepdims=True))
    return centred * lax.rsqrt(variance + epsilon) * norm_gain + norm_shift

def block_forward(row_vals, route_rows, params):
    gain_one, shift_one, qkv_weight, qv_bias, proj_weight, proj_bias, gain_two, shift_two, router_weight, first_w, first_bias, second_w, second_bias = params
    images = row_vals.shape[0] // SEQ
    head_shape = (images, SEQ, HEADS, HEAD_DIM)
    scaling = HEAD_DIM ** (-0.5)
    entry1 = low(norm_rows(row_vals, gain_one, shift_one))
    projected = jnp.einsum('td,dje->tje', entry1, qkv_weight, precision=lax.Precision.HIGHEST)
    query_rows = rounded((projected[:, 0] + qv_bias[0]) * scaling).reshape(head_shape)
    key_rows = rounded(projected[:, 1]).reshape(head_shape)
    value_rows = rounded(projected[:, 2] + qv_bias[1]).reshape(head_shape)
    scores = low_back(jnp.einsum('ishd,ijhd->ihsj', query_rows, key_rows, precision=lax.Precision.HIGHEST))
    attn_probs = low(jax.nn.softmax(scores, axis=-1))
    attn_mixed = rounded(jnp.einsum('ihsj,ijhd->ishd', attn_probs, value_rows, precision=lax.Precision.HIGHEST).reshape(-1, D))
    resid = row_vals + low_back(matmul(attn_mixed, proj_weight) + proj_bias)
    entry2 = low(norm_rows(resid, gain_two, shift_two))
    router_probs = jax.nn.softmax(matmul(entry2, router_weight), axis=-1)
    chosen = (route_rows[:, :, None] == jnp.arange(EXPERTS, dtype=jnp.int32)[None, None, :]).astype(jnp.float32)
    gate_values = lax.optimization_barrier(jnp.sum(chosen * router_probs[:, None, :], axis=-1))
    combine = lax.optimization_barrier(jnp.sum(gate_values[:, :, None] * chosen, axis=1))

    def expert_step(running, packed):
        w_one, b_one, w_two, b_two, weight_col = packed
        entry_rows = low_back(entry2)
        hidden = low_back(matmul(entry_rows, w_one) + b_one)
        active = low(jax.nn.gelu(hidden, approximate=False))
        result = rounded(matmul(active, w_two) + b_two)
        return (running + weight_col[:, None] * result, None)
    mixture, unused = lax.scan(jax.checkpoint(expert_step), jnp.zeros_like(resid), (first_w, first_bias, second_w, second_bias, combine.T))
    return resid + mixture

def reference(tokens, cotangent, routes, norm1_gain, norm1_shift, attn_in, attn_bias, attn_proj, proj_bias, norm2_gain, norm2_shift, router, expert_in, expert_in_bias, expert_out, expert_out_bias):
    weights = tuple((weight_arr.astype(jnp.float32) for weight_arr in (norm1_gain, norm1_shift, attn_in, attn_bias, attn_proj, proj_bias, norm2_gain, norm2_shift, router, expert_in, expert_in_bias, expert_out, expert_out_bias)))
    inputs = tokens.astype(jnp.float32)
    route_blocks = routes.reshape(-1, TOK_DEV, 2)

    def forward(row_inputs, params):
        blocks = row_inputs.reshape(-1, TOK_DEV, D)

        def runner(packed):
            return block_forward(packed[0], packed[1], params)
        return lax.map(jax.checkpoint(runner), (blocks, route_blocks)).reshape(-1, D)
    output, pullback = jax.vjp(forward, inputs, weights)
    grad_inputs, gradients = pullback(cotangent.astype(jnp.float32))
    return (output.astype(jnp.bfloat16), grad_inputs.astype(jnp.bfloat16), gradients[0], gradients[1], gradients[2], gradients[3], gradients[4], gradients[5], gradients[6], gradients[7], gradients[8], gradients[9], gradients[10], gradients[11], gradients[12])
```

```python
import functools
import math

import jax
import jax.numpy as jnp
from jax import lax
from jax.experimental import pallas as pl
from jax.experimental.pallas import tpu as pltpu
from jax.sharding import PartitionSpec as P

D = 768
HEADS = 12
HEAD_DIM = 64
SEQ = 197
IMG_MB = 2
MICRO = 2
IMAGES = IMG_MB * MICRO
IMG = (SEQ + 15) // 16 * 16
BLK = IMG_MB * IMG
ROWS = IMAGES * IMG
SCALE = HEAD_DIM ** (-0.5)
SMALL = 16
epsilon = 1e-06

MESH = pl.DeviceIdType.MESH
F32 = jnp.float32
BF16 = jnp.bfloat16
NT = (((1,), (1,)), ((), ()))
TN = (((0,), (0,)), ((), ()))


def dot_nn(a, b):
    return jnp.dot(a, b, preferred_element_type=F32)


def dot_nt(a, b):
    return lax.dot_general(a, b, NT, preferred_element_type=F32)


def dot_tn(a, b):
    return lax.dot_general(a, b, TN, preferred_element_type=F32)


def norm_rows(vals):
    centred = vals - jnp.mean(vals, axis=-1, keepdims=True)
    inv_std = lax.rsqrt(jnp.mean(centred * centred, axis=-1, keepdims=True) + epsilon)
    return centred * inv_std, inv_std


def ring_place(r, R):
    half = lax.rem(r, 2)
    return lax.div(r, 2) * (1 - half) + half * (R - 1 - lax.div(r, 2))


def ring_at(p, R):
    p = lax.rem(p + 2 * R, R)
    back = lax.div(p, R // 2)
    return (1 - back) * (2 * p) + back * (2 * (R - 1 - p) + 1)


def col_core(c):
    return c + 1 - 2 * lax.rem(c, 2)


def col_y(c):
    return c + 2 - 4 * lax.div(c, 2)


def col_diag(c):
    return 3 - c


def col_at(c, k):
    low = lax.rem(lax.rem(c, 2) + lax.rem(k, 2), 2)
    high = lax.rem(lax.div(c, 2) + lax.div(k, 2), 2)
    return low + 2 * high


def remote(src, dst, send, recv, dev):
    return pltpu.make_async_remote_copy(
        src_ref=src, dst_ref=dst, send_sem=send, recv_sem=recv, device_id=dev, device_id_type=MESH
    )


def greet(devs):
    bar = pltpu.get_barrier_semaphore()
    for dev in devs:
        pl.semaphore_signal(bar, inc=1, device_id=dev, device_id_type=MESH)
    pl.semaphore_wait(bar, len(devs))

def norm_forward(row_vals, norm_gain, norm_shift):
    centred = row_vals - jnp.mean(row_vals, axis=-1, keepdims=True)
    inv_std = lax.rsqrt(jnp.mean(centred * centred, axis=-1, keepdims=True) + epsilon)
    normed = centred * inv_std
    return (normed * norm_gain + norm_shift, normed, inv_std)


def norm_backward(grad_rows, normed, inv_std, norm_gain):
    scaled = grad_rows * norm_gain
    inner = (
        scaled
        - jnp.mean(scaled, axis=-1, keepdims=True)
        - normed * jnp.mean(scaled * normed, axis=-1, keepdims=True)
    )
    return (inv_std * inner, jnp.sum(grad_rows * normed, axis=0), jnp.sum(grad_rows, axis=0))


def gelu_exact(values):
    return jax.nn.gelu(values, approximate=False)


def shards(
    tokens,
    cotangent,
    routes,
    norm1_gain,
    norm1_shift,
    attn_in,
    attn_bias,
    attn_proj,
    proj_bias,
    norm2_gain,
    norm2_shift,
    router,
    expert_in,
    expert_in_bias,
    expert_out,
    expert_out_bias,
):
    experts_all = expert_in.shape[0]
    rows_mb = IMG_MB * SEQ
    capacity = (2 * rows_mb * 13 // (10 * experts_all) + 7) // 8 * 8
    scaling = HEAD_DIM ** (-0.5)
    head_shape = (IMG_MB, SEQ, HEADS, HEAD_DIM)
    stacked = jnp.stack([jnp.swapaxes(expert_in, 1, 2), expert_out])
    owned_cols = lax.all_to_all(stacked, "col", split_axis=1, concat_axis=2, tiled=True)
    norm_pack = jnp.stack([norm1_gain, norm1_shift, norm2_gain, norm2_shift])
    qkv_rows, proj_rows, router_rows, norm_full, owned, first_bias, second_bias = (
        lax.all_gather(attn_in, "row", axis=0, tiled=True),
        lax.all_gather(attn_proj, "row", axis=0, tiled=True),
        lax.all_gather(router, "row", axis=0, tiled=True),
        lax.all_gather(norm_pack, "row", axis=1, tiled=True),
        lax.all_gather(owned_cols, "row", axis=3, tiled=True),
        lax.all_gather(expert_in_bias, "row", axis=1, tiled=True),
        lax.all_gather(expert_out_bias, "row", axis=1, tiled=True),
    )
    qkv_full, proj_full, router_full, qv_bias, out_bias_vec = (
        lax.all_gather(qkv_rows, "col", axis=2, tiled=True),
        lax.all_gather(proj_rows, "col", axis=1, tiled=True),
        lax.all_gather(router_rows, "col", axis=1, tiled=True),
        lax.all_gather(attn_bias, "col", axis=1, tiled=True),
        lax.all_gather(proj_bias, "col", axis=0, tiled=True),
    )
    norms_wide = norm_full.astype(jnp.float32)
    gain_one, shift_one, gain_two, shift_two = (
        norms_wide[0],
        norms_wide[1],
        norms_wide[2],
        norms_wide[3],
    )
    qv_bias_wide = qv_bias.astype(jnp.float32)
    out_bias_wide = out_bias_vec.astype(jnp.float32)
    first_w = owned[0]
    second_w = owned[1]
    first_bias_wide = first_bias.astype(jnp.float32)[:, None, :]
    second_bias_wide = second_bias.astype(jnp.float32)[:, None, :]
    router_wide = router_full.astype(jnp.float32)
    expert_ids = jnp.arange(experts_all, dtype=jnp.int32)
    column_scale = jnp.array([scaling, 1.0, 1.0], jnp.float32)[None, :, None]
    exp_dev = owned.shape[1]
    acc_qkv = jnp.zeros(qkv_full.shape, jnp.float32)
    acc_proj = jnp.zeros(proj_full.shape, jnp.float32)
    acc_router = jnp.zeros(router_full.shape, jnp.float32)
    acc_qv = jnp.zeros(qv_bias.shape, jnp.float32)
    acc_out_bias = jnp.zeros(out_bias_vec.shape, jnp.float32)
    acc_norms = jnp.zeros(norm_full.shape, jnp.float32)
    acc_experts = (
        jnp.zeros((2, exp_dev, owned.shape[2], expert_in.shape[1]), jnp.float32),
        jnp.zeros(expert_in_bias.shape, jnp.float32),
        jnp.zeros(expert_out_bias.shape, jnp.float32),
    )
    outputs = []
    input_grads = []
    for batch_index in range(MICRO):
        offset = batch_index * rows_mb
        row_vals = tokens[offset : offset + rows_mb].astype(jnp.float32)
        grad_out = cotangent[offset : offset + rows_mb].astype(jnp.float32)
        route_mb = routes[offset : offset + rows_mb]
        normed_out1, normed1, inv_std1 = norm_forward(row_vals, gain_one, shift_one)
        entry1 = normed_out1.astype(jnp.bfloat16)
        projected = jnp.einsum("td,dje->tje", entry1, qkv_full, preferred_element_type=jnp.float32)
        query_rows = (
            ((projected[:, 0] + qv_bias_wide[0]) * scaling).astype(jnp.bfloat16).reshape(head_shape)
        )
        key_rows = projected[:, 1].astype(jnp.bfloat16).reshape(head_shape)
        value_rows = (projected[:, 2] + qv_bias_wide[1]).astype(jnp.bfloat16).reshape(head_shape)
        scores = jnp.einsum(
            "ishd,ijhd->ihsj", query_rows, key_rows, preferred_element_type=jnp.float32
        )
        row_peak = jnp.max(scores, axis=-1, keepdims=True)
        exp_scores = jnp.exp(scores - row_peak)
        totals = jnp.sum(exp_scores, axis=-1, keepdims=True)
        attn_probs = exp_scores / totals
        log_totals = row_peak + jnp.log(totals)
        attn_mixed = (
            jnp.einsum(
                "ihsj,ijhd->ishd",
                attn_probs.astype(jnp.bfloat16),
                value_rows,
                preferred_element_type=jnp.float32,
            )
            .reshape(rows_mb, D)
            .astype(jnp.bfloat16)
        )
        branch = jnp.dot(attn_mixed, proj_full, preferred_element_type=jnp.float32) + out_bias_wide
        resid = row_vals + branch
        normed_out2, normed2, inv_std2 = norm_forward(resid, gain_two, shift_two)
        entry2 = normed_out2.astype(jnp.bfloat16)
        logits = jnp.dot(entry2, router_full, preferred_element_type=jnp.float32)
        router_probs = jax.nn.softmax(logits, axis=-1)
        chosen = route_mb[:, :, None] == expert_ids[None, None, :]
        gate_values = jnp.sum(jnp.where(chosen, router_probs[:, None, :], 0.0), axis=-1)
        route_flags = chosen.reshape(2 * rows_mb, experts_all).astype(jnp.int32)
        before = jnp.cumsum(route_flags, axis=0) - route_flags
        target = route_mb.reshape(-1) * capacity + jnp.sum(before * route_flags, axis=-1)
        outgoing = (
            jnp.zeros((experts_all * capacity, D), jnp.bfloat16)
            .at[target]
            .set(jnp.repeat(entry2, 2, axis=0))
        )
        arrived = lax.all_to_all(
            outgoing.reshape(experts_all, capacity, D),
            "col",
            split_axis=0,
            concat_axis=1,
            tiled=True,
        )
        pre_act = (
            jnp.einsum("erd,efd->erf", arrived, first_w, preferred_element_type=jnp.float32)
            + first_bias_wide
        )
        active = gelu_exact(pre_act).astype(jnp.bfloat16)
        result = (
            jnp.einsum("erf,efd->erd", active, second_w, preferred_element_type=jnp.float32)
            + second_bias_wide
        ).astype(jnp.bfloat16)
        returned = lax.all_to_all(result, "col", split_axis=1, concat_axis=0, tiled=True).reshape(
            experts_all * capacity, D
        )
        picked = returned[target].reshape(rows_mb, 2, D).astype(jnp.float32)
        outputs.append(
            (resid + jnp.sum(gate_values[:, :, None] * picked, axis=1)).astype(jnp.bfloat16)
        )
        grad_gates = jnp.sum(grad_out[:, None, :] * picked, axis=-1)
        grad_sent = (
            (gate_values[:, :, None] * grad_out[:, None, :])
            .astype(jnp.bfloat16)
            .reshape(2 * rows_mb, D)
        )
        grad_outgoing = (
            jnp.zeros((experts_all * capacity, D), jnp.bfloat16).at[target].set(grad_sent)
        )
        grad_result = lax.all_to_all(
            grad_outgoing.reshape(experts_all, capacity, D),
            "col",
            split_axis=0,
            concat_axis=1,
            tiled=True,
        )
        grad_active = jnp.einsum(
            "erd,efd->erf", grad_result, second_w, preferred_element_type=jnp.float32
        )
        grad_pre = jax.vjp(gelu_exact, pre_act)[1](grad_active)[0].astype(jnp.bfloat16)
        weight_terms = jnp.stack(
            [
                jnp.einsum("erf,erd->efd", grad_pre, arrived, preferred_element_type=jnp.float32),
                jnp.einsum("erf,erd->efd", active, grad_result, preferred_element_type=jnp.float32),
            ]
        )
        in_bias_terms = jnp.sum(grad_pre.astype(jnp.float32), axis=1)
        out_bias_terms = jnp.sum(grad_result.astype(jnp.float32), axis=1)
        weight_piece, in_bias_piece, out_bias_piece = (
            lax.psum_scatter(
                weight_terms.astype(jnp.bfloat16), "row", scatter_dimension=3, tiled=True
            ).astype(jnp.float32),
            lax.psum_scatter(
                in_bias_terms.astype(jnp.bfloat16), "row", scatter_dimension=1, tiled=True
            ).astype(jnp.float32),
            lax.psum_scatter(
                out_bias_terms.astype(jnp.bfloat16), "row", scatter_dimension=1, tiled=True
            ).astype(jnp.float32),
        )
        acc_experts = (
            acc_experts[0] + weight_piece,
            acc_experts[1] + in_bias_piece,
            acc_experts[2] + out_bias_piece,
        )
        grad_entry = jnp.einsum(
            "erf,efd->erd", grad_pre, first_w, preferred_element_type=jnp.float32
        ).astype(jnp.bfloat16)
        grad_back = lax.all_to_all(
            grad_entry, "col", split_axis=1, concat_axis=0, tiled=True
        ).reshape(experts_all * capacity, D)
        grad_entry2 = jnp.sum(grad_back[target].reshape(rows_mb, 2, D).astype(jnp.float32), axis=1)
        grad_probs = jnp.sum(jnp.where(chosen, grad_gates[:, :, None], 0.0), axis=1)
        grad_logits = router_probs * (
            grad_probs - jnp.sum(router_probs * grad_probs, axis=-1, keepdims=True)
        )
        grad_entry2 = grad_entry2 + jnp.dot(
            grad_logits, router_wide.T, precision=lax.Precision.HIGHEST
        )
        acc_router = acc_router + jnp.dot(
            entry2.astype(jnp.float32).T, grad_logits, precision=lax.Precision.HIGHEST
        )
        grad_norm2, gain_two_grad, shift_two_grad = norm_backward(
            grad_entry2, normed2, inv_std2, gain_two
        )
        grad_resid = grad_out + grad_norm2
        grad_branch = grad_resid.astype(jnp.bfloat16)
        acc_proj = acc_proj + jnp.einsum(
            "td,te->de", attn_mixed, grad_branch, preferred_element_type=jnp.float32
        )
        acc_out_bias = acc_out_bias + jnp.sum(grad_branch.astype(jnp.float32), axis=0)
        grad_mixed = (
            jnp.einsum("te,de->td", grad_branch, proj_full, preferred_element_type=jnp.float32)
            .astype(jnp.bfloat16)
            .reshape(head_shape)
        )
        scores_again = jnp.einsum(
            "ishd,ijhd->ihsj", query_rows, key_rows, preferred_element_type=jnp.float32
        )
        probs_again = jnp.exp(scores_again - log_totals)
        grad_weights = jnp.einsum(
            "ishd,ijhd->ihsj", grad_mixed, value_rows, preferred_element_type=jnp.float32
        )
        grad_values = jnp.einsum(
            "ihsj,ishd->ijhd",
            probs_again.astype(jnp.bfloat16),
            grad_mixed,
            preferred_element_type=jnp.float32,
        )
        inner_sum = jnp.sum(probs_again * grad_weights, axis=-1, keepdims=True)
        grad_scores = (probs_again * (grad_weights - inner_sum)).astype(jnp.bfloat16)
        grad_query = jnp.einsum(
            "ihsj,ijhd->ishd", grad_scores, key_rows, preferred_element_type=jnp.float32
        )
        grad_keys = jnp.einsum(
            "ihsj,ishd->ijhd", grad_scores, query_rows, preferred_element_type=jnp.float32
        )
        grad_qkv = jnp.stack(
            [
                grad_query.reshape(rows_mb, D),
                grad_keys.reshape(rows_mb, D),
                grad_values.reshape(rows_mb, D),
            ],
            axis=1,
        ).astype(jnp.bfloat16)
        acc_qkv = (
            acc_qkv
            + jnp.einsum("td,tje->dje", entry1, grad_qkv, preferred_element_type=jnp.float32)
            * column_scale
        )
        grad_sums = jnp.sum(grad_qkv.astype(jnp.float32), axis=0)
        acc_qv = acc_qv + jnp.stack([grad_sums[0] * scaling, grad_sums[2]])
        grad_entry1 = jnp.sum(
            jnp.einsum("tje,dje->tjd", grad_qkv, qkv_full, preferred_element_type=jnp.float32)
            * column_scale,
            axis=1,
        )
        grad_norm1, gain_one_grad, shift_one_grad = norm_backward(
            grad_entry1, normed1, inv_std1, gain_one
        )
        input_grads.append((grad_resid + grad_norm1).astype(jnp.bfloat16))
        acc_norms = acc_norms + jnp.stack(
            [gain_one_grad, shift_one_grad, gain_two_grad, shift_two_grad]
        )
    qkv_grad, proj_grad, router_grad, qv_grad, out_bias_grad = (
        lax.psum_scatter(acc_qkv, "col", scatter_dimension=2, tiled=True),
        lax.psum_scatter(acc_proj, "col", scatter_dimension=1, tiled=True),
        lax.psum_scatter(acc_router, "col", scatter_dimension=1, tiled=True),
        lax.psum_scatter(acc_qv, "col", scatter_dimension=1, tiled=True),
        lax.psum_scatter(acc_out_bias, "col", scatter_dimension=0, tiled=True),
    )
    qv_grad, out_bias_grad = lax.psum((qv_grad, out_bias_grad), "row")
    qkv_grad, proj_grad, router_grad, norm_grad = (
        lax.psum_scatter(
            qkv_grad.astype(jnp.bfloat16), "row", scatter_dimension=0, tiled=True
        ).astype(jnp.float32),
        lax.psum_scatter(
            proj_grad.astype(jnp.bfloat16), "row", scatter_dimension=0, tiled=True
        ).astype(jnp.float32),
        lax.psum_scatter(
            router_grad.astype(jnp.bfloat16), "row", scatter_dimension=0, tiled=True
        ).astype(jnp.float32),
        lax.psum_scatter(
            acc_norms.astype(jnp.bfloat16), "row", scatter_dimension=1, tiled=True
        ).astype(jnp.float32),
    )
    expert_stack, in_bias_grad, out_bias_expert = acc_experts
    norm_grad = lax.psum(norm_grad, "col")
    expert_blocks = lax.all_to_all(
        expert_stack.astype(jnp.bfloat16), "col", split_axis=2, concat_axis=1, tiled=True
    ).astype(expert_stack.dtype)
    return (
        jnp.concatenate(outputs, axis=0),
        jnp.concatenate(input_grads, axis=0),
        norm_grad[0],
        norm_grad[1],
        qkv_grad,
        qv_grad,
        proj_grad,
        out_bias_grad,
        norm_grad[2],
        norm_grad[3],
        router_grad,
        jnp.swapaxes(expert_blocks[0], 1, 2),
        in_bias_grad,
        expert_blocks[1],
        out_bias_expert,
    )

def ring_event(buf_of, sends, recvs, flow, step, r, c, pos, R):
    right, left = ring_at(pos + 1, R), ring_at(pos - 1, R)
    hops = R // 2
    from_left, from_right = ring_at(pos - step, R), ring_at(pos + step, R)
    if step > 0:
        a, b = buf_of(from_left), buf_of(from_right)
        remote(a, a, sends.at[flow, 0, step - 1], recvs.at[flow, 0, step - 1], (right, c)).wait_recv()
        remote(b, b, sends.at[flow, 1, step - 1], recvs.at[flow, 1, step - 1], (left, c)).wait_recv()
    a, b = buf_of(from_left), buf_of(from_right)
    if step == hops - 1:
        a, b = a.at[0], b.at[1]
    remote(a, a, sends.at[flow, 0, step], recvs.at[flow, 0, step], (right, c)).start()
    remote(b, b, sends.at[flow, 1, step], recvs.at[flow, 1, step], (left, c)).start()


def ring_finish(buf_of, sends, recvs, flow, r, c, pos, R):
    right, left = ring_at(pos + 1, R), ring_at(pos - 1, R)
    hops = R // 2
    far = buf_of(ring_at(pos + hops, R))
    remote(far.at[0], far.at[0], sends.at[flow, 0, hops - 1], recvs.at[flow, 0, hops - 1], (right, c)).wait_recv()
    remote(far.at[1], far.at[1], sends.at[flow, 1, hops - 1], recvs.at[flow, 1, hops - 1], (left, c)).wait_recv()
    own = buf_of(r)
    for step in range(hops):
        a, b = (own, own) if step < hops - 1 else (own.at[0], own.at[1])
        remote(a, a, sends.at[flow, 0, step], recvs.at[flow, 0, step], (right, c)).wait_send()
        remote(b, b, sends.at[flow, 1, step], recvs.at[flow, 1, step], (left, c)).wait_send()


def front_kernel(
    R, C, E,
    tok, cot, pack, wexp, rt, upper,
    wbuf, e2_all, cot_all, info_all, wg_out, qkv, mixed, probs, resid, rprob, sm_out,
    wg, entry1, e2, wp, brow, info, mix_tmp,
    ring_s, ring_r, fan_s, fan_r, a2a_s, a2a_r, flow_s, flow_r, cot_s, cot_r, e2_s, e2_r, inf_s, inf_r, loc,
):
    r, c = lax.axis_index("row"), lax.axis_index("col")
    pos = ring_place(r, R)
    hops = R // 2
    right, left = ring_at(pos + 1, R), ring_at(pos - 1, R)
    core, ypeer, diag = col_core(c), col_y(c), col_diag(c)
    greet([(right, c), (left, c), (r, core), (r, ypeer), (r, diag)])
    HALF = 64
    TAIL = pack.shape[0] - HALF
    HB = D // R

    own_pack = pltpu.make_async_copy(pack, wg.at[c, r], loc.at[0])
    own_pack.start()
    remote(pack, wg.at[c, r], ring_s.at[0, 0], ring_r.at[0, 0], (right, c)).start()
    remote(pack, wg.at[c, r], ring_s.at[1, 0], ring_r.at[1, 0], (left, c)).start()
    remote(pack, wg.at[c, r], fan_s.at[0, 0], fan_r.at[0, 0], (r, core)).start()
    remote(pack, wg.at[c, r], fan_s.at[1, 0], fan_r.at[1, 0], (r, ypeer)).start()
    own_exp = pltpu.make_async_copy(wexp.at[c], wbuf.at[c, r], loc.at[1])
    own_exp.start()
    peers = [core, ypeer, diag]
    for n, peer in enumerate(peers):
        remote(wexp.at[peer], wbuf.at[c, r], a2a_s.at[n], a2a_r.at[n], (r, peer)).start()
    own_cot = pltpu.make_async_copy(cot, cot_all.at[c], loc.at[2])
    own_cot.start()

    fan_rows = [r]
    for s in range(1, hops + 1):
        o_l, o_r = ring_at(pos - s, R), ring_at(pos + s, R)
        if s < hops:
            a, b = wg.at[c, o_l], wg.at[c, o_r]
            remote(a, a, ring_s.at[0, s - 1], ring_r.at[0, s - 1], (right, c)).wait_recv()
            remote(b, b, ring_s.at[1, s - 1], ring_r.at[1, s - 1], (left, c)).wait_recv()
            if s == hops - 1:
                a2, b2 = a.at[pl.ds(0, HALF)], b.at[pl.ds(HALF, TAIL)]
            else:
                a2, b2 = a, b
            remote(a2, a2, ring_s.at[0, s], ring_r.at[0, s], (right, c)).start()
            remote(b2, b2, ring_s.at[1, s], ring_r.at[1, s], (left, c)).start()
            new = [o_l, o_r]
        else:
            far = wg.at[c, o_l]
            a2, b2 = far.at[pl.ds(0, HALF)], far.at[pl.ds(HALF, TAIL)]
            remote(a2, a2, ring_s.at[0, s - 1], ring_r.at[0, s - 1], (right, c)).wait_recv()
            remote(b2, b2, ring_s.at[1, s - 1], ring_r.at[1, s - 1], (left, c)).wait_recv()
            new = [o_l]
        for o in new:
            j = len(fan_rows)
            fan_rows.append(o)
            blk = wg.at[c, o]
            remote(blk, blk, fan_s.at[0, j], fan_r.at[0, j], (r, core)).start()
            remote(blk, blk, fan_s.at[1, j], fan_r.at[1, j], (r, ypeer)).start()
    own_pack.wait()
    own_exp.wait()

    def fan_wait(g, n):
        for j, o in enumerate(fan_rows):
            blk = wg.at[g, o]
            remote(blk, blk, fan_s.at[n, j], fan_r.at[n, j], (r, core)).wait_recv()

    def fan_relay():
        for j, o in enumerate(fan_rows):
            blk = wg.at[ypeer, o]
            remote(blk, blk, fan_s.at[1, j], fan_r.at[1, j], (r, ypeer)).wait_recv()
            remote(blk, blk, fan_s.at[2, j], fan_r.at[2, j], (r, core)).start()

    own_small = jnp.zeros((SMALL, D), F32)
    for o in range(R):
        own_small = own_small + wg[c, o, HB : HB + SMALL, :].astype(F32)
    gain1, shift1 = own_small[0:1], own_small[1:2]
    gain2, shift2 = own_small[2:3], own_small[3:4]

    def first(i, _):
        rows = pl.ds(pl.multiple_of(i * IMG, 16), IMG)
        normed, _u = norm_rows(tok[rows, :].astype(F32))
        entry1[rows, :] = (normed * gain1 + shift1).astype(BF16)
        return 0

    lax.fori_loop(0, IMAGES, first, 0)

    def flow_buf(k):
        f = col_at(c, k)
        return lambda o: wbuf.at[f, o]

    W3 = 3 * (D // C)
    WH = D // C
    lane = lax.broadcasted_iota(jnp.int32, (1, W3), 1)
    col_scale = jnp.where(lane < WH, SCALE, 1.0).astype(F32)
    keep = lax.broadcasted_iota(jnp.int32, (1, IMG), 1) < SEQ
    heads = WH // HEAD_DIM

    order = [c, core, ypeer, diag]
    for k in range(C):
        g = order[k]
        if k == 1:
            fan_wait(core, 0)
            a2a = wbuf.at[core, r]
            remote(a2a, a2a, a2a_s.at[0], a2a_r.at[0], (r, core)).wait_recv()
        if k == 2:
            fan_relay()
            remote(cot, cot_all.at[c], cot_s.at[0], cot_r.at[0], (r, core)).start()
            remote(cot, cot_all.at[c], cot_s.at[1], cot_r.at[1], (r, ypeer)).start()
        if k == 3:
            fan_wait(diag, 2)
        small = wg[g, 0, HB : HB + SMALL, :].astype(F32)
        bq, bv = small[4:5, :WH], small[5:6, :WH]
        bias = jnp.concatenate([bq, jnp.zeros_like(bq), bv], axis=1)

        def image(i, _, k=k, g=g, bias=bias):
            rows = pl.ds(pl.multiple_of(i * IMG, 16), IMG)
            w = wg[g, :, 0:HB, 0:W3].reshape(D, W3)
            y = dot_nn(entry1[rows, :], w)
            z = ((y + bias) * col_scale).astype(BF16)
            qkv[g, rows, :] = z
            outs = []
            for h in range(heads):
                q = z[:, h * HEAD_DIM : (h + 1) * HEAD_DIM]
                kk = z[:, WH + h * HEAD_DIM : WH + (h + 1) * HEAD_DIM]
                v = z[:, 2 * WH + h * HEAD_DIM : 2 * WH + (h + 1) * HEAD_DIM]
                s = dot_nt(q, kk)
                s = jnp.where(keep, s, -1e30)
                peak = jnp.max(s, axis=-1, keepdims=True)
                ex = jnp.exp(s - peak)
                p = (ex / jnp.sum(ex, axis=-1, keepdims=True)).astype(BF16)
                probs[g, i, h] = p
                outs.append(dot_nn(p, v))
            mixed[g, rows, :] = jnp.concatenate(outs, axis=1).astype(BF16)
            return 0

        lax.fori_loop(0, IMAGES, image, 0)
        if k == 0:
            for n in range(2):
                pass
        ring_event(flow_buf(0), flow_s, flow_r, 0, k, r, c, pos, R)
        if k >= 1:
            ring_event(flow_buf(1), flow_s, flow_r, 1, k - 1, r, c, pos, R)
    ring_event(flow_buf(1), flow_s, flow_r, 1, hops - 1, r, c, pos, R)
    for n in (1, 2):
        a2a = wbuf.at[peers[n], r]
        remote(a2a, a2a, a2a_s.at[n], a2a_r.at[n], (r, peers[n])).wait_recv()
    ring_event(flow_buf(2), flow_s, flow_r, 2, 0, r, c, pos, R)
    ring_event(flow_buf(3), flow_s, flow_r, 3, 0, r, c, pos, R)
    send_wg = pltpu.make_async_copy(wg, wg_out, loc.at[3])
    send_wg.start()

    rtr = []
    pb = []
    for g in range(C):
        wp[:, g * WH : (g + 1) * WH] = wg[g, :, 0:HB, W3:].reshape(D, WH)
        pb.append(wg[g, 0, HB : HB + SMALL, :].astype(F32)[6:7, :WH])
        acc = jnp.zeros((1, D), F32)
        for o in range(R):
            acc = acc + wg[g, o, HB : HB + SMALL, :].astype(F32)[7:8]
        rtr.append(acc)
    pbias = jnp.concatenate(pb, axis=1)
    router_t = jnp.concatenate(rtr + [jnp.zeros((8 - C, D), F32)], axis=0)
    sm_out[0:SMALL, :] = own_small
    sm_out[SMALL : SMALL + 8, :] = router_t
    router_b = router_t.astype(BF16)

    def second(i, _):
        rows = pl.ds(pl.multiple_of(i * IMG, 16), IMG)
        acc = tok[rows, :].astype(F32) + pbias
        for g in range(C):
            acc = acc + dot_nn(mixed[g, rows, :], wp[g * WH : (g + 1) * WH, :])
        resid[rows, :] = acc
        normed, _u = norm_rows(acc)
        e2[rows, :] = (normed * gain2 + shift2).astype(BF16)
        return 0

    def e2_copy(n, h, who, peer):
        part = pl.ds(h * BLK, BLK)
        src = e2.at[part] if n < 2 else e2_all.at[who, part]
        return remote(src, e2_all.at[who, part], e2_s.at[n, h], e2_r.at[n, h], (r, peer))

    exp_id = lax.broadcasted_iota(jnp.int32, (8, BLK), 0)
    locals_ = []
    for h in range(MICRO):
        lax.fori_loop(h * IMG_MB, (h + 1) * IMG_MB, second, 0)
        e2_copy(1, h, c, ypeer).start()
        e2_copy(0, h, c, core).start()
        part = pl.ds(h * BLK, BLK)
        cp = pltpu.make_async_copy(e2.at[part], e2_all.at[c, part], loc.at[4 + h])
        cp.start()
        locals_.append(cp)
        blk = e2[h * BLK : (h + 1) * BLK, :]
        logits = jnp.where(exp_id < E, dot_nt(router_b, blk), -1e30)
        ex = jnp.exp(logits - jnp.max(logits, axis=0, keepdims=True))
        prob = ex / jnp.sum(ex, axis=0, keepdims=True)
        rprob[h] = prob
        named = rt[h]
        member = (named[0:1] == exp_id.astype(F32)) | (named[1:2] == exp_id.astype(F32))
        flags = jnp.where(member, 1.0, 0.0)
        rank = dot_nn(flags.astype(BF16), upper[...])
        info[h, 0:8, :] = jnp.where(member, rank, -1.0)
        info[h, 8:16, :] = jnp.where(member, prob, 0.0)
        ring_event(flow_buf(2), flow_s, flow_r, 2, 1 + h, r, c, pos, R)
        ring_event(flow_buf(3), flow_s, flow_r, 3, 1 + h, r, c, pos, R)
    cp = pltpu.make_async_copy(info, info_all.at[c], loc.at[6])
    cp.start()
    locals_.append(cp)
    for n, peer in enumerate(peers):
        remote(info, info_all.at[c], inf_s.at[n], inf_r.at[n], (r, peer)).start()
    remote(cot, cot_all.at[ypeer], cot_s.at[1], cot_r.at[1], (r, ypeer)).wait_recv()
    relay_cot = remote(cot_all.at[ypeer], cot_all.at[ypeer], cot_s.at[2], cot_r.at[2], (r, core))
    relay_cot.start()
    for h in range(MICRO):
        e2_copy(1, h, ypeer, ypeer).wait_recv()
        e2_copy(2, h, ypeer, core).start()
    ring_event(flow_buf(2), flow_s, flow_r, 2, 3, r, c, pos, R)
    ring_event(flow_buf(3), flow_s, flow_r, 3, 3, r, c, pos, R)

    for n, (who, src) in enumerate([(core, cot), (None, None), (diag, cot_all.at[diag])]):
        if n != 1:
            remote(src, cot_all.at[who], cot_s.at[n], cot_r.at[n], (r, core)).wait_recv()
    for n in range(3):
        remote(cot, cot_all.at[c], cot_s.at[n], cot_r.at[n], (r, core)).wait_send()
    for h in range(MICRO):
        e2_copy(0, h, core, core).wait_recv()
        e2_copy(2, h, diag, core).wait_recv()
        for n in range(3):
            e2_copy(n, h, c, core).wait_send()
    for n, peer in enumerate(peers):
        cp = remote(info, info_all.at[peer], inf_s.at[n], inf_r.at[n], (r, peer))
        cp.wait_recv()
        cp.wait_send()
    for n, peer in enumerate(peers):
        remote(wexp.at[peer], wbuf.at[c, r], a2a_s.at[n], a2a_r.at[n], (r, peer)).wait_send()
    for j in range(R):
        for n in range(3):
            blk = wg.at[c, 0]
            remote(blk, blk, fan_s.at[n, j], fan_r.at[n, j], (r, core)).wait_send()
    for s in range(hops):
        a, b = wg.at[c, 0], wg.at[c, 0]
        if s == hops - 1:
            a, b = a.at[pl.ds(0, HALF)], b.at[pl.ds(HALF, TAIL)]
        remote(a, a, ring_s.at[0, s], ring_r.at[0, s], (right, c)).wait_send()
        remote(b, b, ring_s.at[1, s], ring_r.at[1, s], (left, c)).wait_send()
    for k in range(C):
        ring_finish(flow_buf(k), flow_s, flow_r, k, r, c, pos, R)
    own_cot.wait()
    send_wg.wait()
    for cp in locals_:
        cp.wait()


def front(R, C, E, tok, cot, pack, wexp, rt, upper):
    WH = D // C
    HB = D // R
    hops = R // 2
    vm = pl.BlockSpec(memory_space=pltpu.VMEM)
    hbm = pl.BlockSpec(memory_space=pl.ANY)
    sem = pltpu.SemaphoreType.DMA
    heads = WH // HEAD_DIM
    return pl.pallas_call(
        functools.partial(front_kernel, R, C, E),
        name="front",
        out_shape=(
            jax.ShapeDtypeStruct((C, R, 2, HB, D), BF16),
            jax.ShapeDtypeStruct((C, ROWS, D), BF16),
            jax.ShapeDtypeStruct((C, ROWS, D), BF16),
            jax.ShapeDtypeStruct((C, MICRO, 16, BLK), F32),
            jax.ShapeDtypeStruct((C, R, HB + SMALL, D), BF16),
            jax.ShapeDtypeStruct((C, ROWS, 3 * WH), BF16),
            jax.ShapeDtypeStruct((C, ROWS, WH), BF16),
            jax.ShapeDtypeStruct((C, IMAGES, heads, IMG, IMG), BF16),
            jax.ShapeDtypeStruct((ROWS, D), F32),
            jax.ShapeDtypeStruct((MICRO, 8, BLK), F32),
            jax.ShapeDtypeStruct((SMALL + 8, D), F32),
        ),
        in_specs=[vm, hbm, vm, hbm, vm, vm],
        out_specs=(hbm, hbm, hbm, hbm, hbm, vm, vm, vm, vm, vm, vm),
        scratch_shapes=[
            pltpu.VMEM((C, R, HB + SMALL, D), BF16),
            pltpu.VMEM((ROWS, D), BF16),
            pltpu.VMEM((ROWS, D), BF16),
            pltpu.VMEM((D, D), BF16),
            pltpu.VMEM((8, 3 * WH), F32),
            pltpu.VMEM((MICRO, 16, BLK), F32),
            pltpu.VMEM((8, D), F32),
            sem((2, hops)), sem((2, hops)),
            sem((3, R)), sem((3, R)),
            sem((3,)), sem((3,)),
            sem((C, 2, hops)), sem((C, 2, hops)),
            sem((3,)), sem((3,)),
            sem((3, MICRO)), sem((3, MICRO)),
            sem((3,)), sem((3,)),
            sem((8,)),
        ],
        compiler_params=pltpu.CompilerParams(
            collective_id=1, has_side_effects=True, vmem_limit_bytes=56 << 20
        ),
    )(tok, cot, pack, wexp, rt, upper)

def reduce_event(parts, rbuf, sends, recvs, slot, step, r, c, pos, R):
    right, left = ring_at(pos + 1, R), ring_at(pos - 1, R)
    hops = R // 2
    to_right, to_left = ring_at(pos + hops - step, R), ring_at(pos - hops + step, R)
    for d, (dest, peer) in enumerate(((to_right, right), (to_left, left))):
        if step > 0:
            got = rbuf(d, step - 1)
            if step == 1:
                got, mine = got.at[d], parts.at[dest, d]
            else:
                mine = parts.at[dest]
            remote(got, got, sends.at[slot, d, step - 1], recvs.at[slot, d, step - 1], (peer, c)).wait_recv()
            mine[...] = (mine[...].astype(F32) + got[...].astype(F32)).astype(BF16)
        src, dst = parts.at[dest], rbuf(d, step)
        if step == 0:
            src, dst = src.at[d], dst.at[d]
        remote(src, dst, sends.at[slot, d, step], recvs.at[slot, d, step], (peer, c)).start()


def reduce_finish(parts, rbuf, sends, recvs, slot, r, c, pos, R):
    hops = R // 2
    total = parts[r].astype(F32)
    for d in range(2):
        got = rbuf(d, hops - 1)
        remote(got, got, sends.at[slot, d, hops - 1], recvs.at[slot, d, hops - 1], (r, c)).wait_recv()
        total = total + got[...].astype(F32)
    for d in range(2):
        for step in range(hops):
            src, dst = parts.at[r], rbuf(d, step)
            if step == 0:
                src, dst = src.at[d], dst.at[d]
            remote(src, dst, sends.at[slot, d, step], recvs.at[slot, d, step], (r, c)).wait_send()
    return total


def expert_kernel(
    R, C, CAP,
    e2_all, cot_all, info_all, wbuf, sm,
    ge_parts, mix_parts, mix_out, gg_all, dexp, raw, bias_out,
    wv, eb, gb, info, X, XT, GR, GRT, RES, GE, act, gh, stage, rbuf, corebuf, fin, ggs,
    w_sem, eb_sem, loc, red_s, red_r, fin_s, fin_r, core_s, core_r, ge_s, ge_r, mx_s, mx_r, gg_s, gg_r,
):
    r, c = lax.axis_index("row"), lax.axis_index("col")
    pos = ring_place(r, R)
    hops = R // 2
    HB = D // R
    right, left = ring_at(pos + 1, R), ring_at(pos - 1, R)
    core, ypeer, diag = col_core(c), col_y(c), col_diag(c)
    greet([(right, c), (left, c), (r, core), (r, ypeer), (r, diag)])
    NB = C * MICRO
    TR = NB * CAP

    def weights(k):
        return pltpu.make_async_copy(wbuf.at[col_at(c, k)], wv.at[k % 2], w_sem.at[k % 2])

    weights(0).start()
    get_info = pltpu.make_async_copy(info_all, info, loc.at[0])
    get_info.start()

    def fetch(b, slot, which):
        s, h = lax.div(b, MICRO), lax.rem(b, MICRO)
        src, dst = (e2_all, eb) if which == 0 else (cot_all, gb)
        return pltpu.make_async_copy(
            src.at[s, pl.ds(pl.multiple_of(h * BLK, 16), BLK)], dst.at[slot], eb_sem.at[which, slot]
        )

    slot_id = lax.broadcasted_iota(jnp.int32, (CAP, BLK), 0).astype(F32)

    def pick(b):
        s, h = lax.div(b, MICRO), lax.rem(b, MICRO)
        code = info[s, h, pl.ds(c, 1), :]
        gate = info[s, h, pl.ds(8 + c, 1), :]
        hot = jnp.where(slot_id == code, 1.0, 0.0)
        gate_slot = jnp.sum(hot * gate, axis=1, keepdims=True)
        return hot, gate_slot

    fetch(0, 0, 0).start()
    fetch(0, 0, 1).start()
    get_info.wait()

    def gather(b, bias):
        slot = lax.rem(b, 2)

        @pl.when(b + 1 < NB)
        def _():
            fetch(b + 1, 1 - slot, 0).start()
            fetch(b + 1, 1 - slot, 1).start()

        fetch(b, slot, 0).wait()
        fetch(b, slot, 1).wait()
        hot, gate_slot = pick(b)
        hot = hot.astype(BF16)
        rows = pl.ds(pl.multiple_of(b * CAP, 16), CAP)
        x = dot_nn(hot, eb[slot])
        X[rows, :] = x.astype(BF16)
        XT[:, rows] = x.T.astype(BF16)
        g = gate_slot * dot_nn(hot, gb[slot])
        g16 = g.astype(BF16)
        GR[rows, :] = g16
        g32 = g16.astype(F32)
        GRT[:, rows] = g32.T.astype(BF16)
        return bias + jnp.sum(g32, axis=0, keepdims=True)

    bias_out[...] = jnp.zeros_like(bias_out)
    bias_out[0:1, :] = lax.fori_loop(0, NB, gather, jnp.zeros((1, D), F32))

    def red(k, step):
        reduce_event(stage.at[k], lambda d, s: rbuf.at[k, d, s], red_s, red_r, k, step, r, c, pos, R)

    def red_end(k):
        total = reduce_finish(stage.at[k], lambda d, s: rbuf.at[k, d, s], red_s, red_r, k, r, c, pos, R)
        fin[k] = total.astype(BF16)
        if k == 0:
            cp = pltpu.make_async_copy(fin.at[0], dexp.at[c], loc.at[1])
        else:
            cp = remote(fin.at[1], dexp.at[c], fin_s.at[0], fin_r.at[0], (r, core))
        cp.start()
        return cp

    events = {
        (1, 0): [(0, 0)], (1, 2): [(0, 1)],
        (2, 0): [(0, 2), (1, 0)], (2, 2): [(0, 3), (1, 1)],
        (3, 0): [(1, 2)], (3, 2): [(1, 3)],
    }
    ends = []

    def pump(k, phase):
        for ev in events.get((k, phase), []):
            red(*ev)

    MT = 512 if TR % 512 == 0 else CAP
    DT = D // 2
    raws = []
    for k in range(C):
        f = col_at(c, k)
        if k + 1 < C:
            weights(k + 1).start()
        weights(k).wait()
        b1 = sm[pl.ds(9 + f, 1), :]

        def ffn(m, bias, k=k, b1=b1):
            rows = pl.ds(pl.multiple_of(m * MT, 16), MT)
            win = wv[k % 2, :, 0].reshape(D, D)
            wout = wv[k % 2, :, 1].reshape(D, D)
            hid = dot_nn(X[rows, :], win) + b1
            cdf = 0.5 * (1.0 + lax.erf(hid * (2.0 ** -0.5)))
            a16 = (hid * cdf).astype(BF16)
            act[rows, :] = a16
            slope = cdf + hid * (jnp.exp(-0.5 * hid * hid) * ((2.0 * math.pi) ** -0.5))
            ga = dot_nn(GR[rows, :], wout)
            g16 = (ga * slope).astype(BF16)
            gh[rows, :] = g16
            res = dot_nt(a16, wout)
            gen = dot_nt(g16, win)
            if k == 0:
                RES[rows, :] = res
                GE[rows, :] = gen
            else:
                RES[rows, :] = RES[rows, :] + res
                GE[rows, :] = GE[rows, :] + gen
            return bias + jnp.sum(g16.astype(F32), axis=0, keepdims=True)

        pump(k, 0)
        bsum = lax.fori_loop(0, TR // MT // 2, ffn, jnp.zeros((1, D), F32))
        pump(k, 1)
        bsum = lax.fori_loop(TR // MT // 2, TR // MT, ffn, bsum)
        pump(k, 2)
        bias_out[pl.ds(1 + f, 1), :] = bsum

        def dwin(j, _, k=k):
            rows = pl.ds(pl.multiple_of(j * DT, 16), DT)
            blocks = pl.ds(j * (R // 2), R // 2)
            stage[k, blocks, 0] = dot_nn(XT[rows, :], gh[...]).astype(BF16).reshape(R // 2, HB, D)
            stage[k, blocks, 1] = dot_nn(GRT[rows, :], act[...]).astype(BF16).reshape(R // 2, HB, D)
            return 0

        lax.fori_loop(0, 2, dwin, 0)
        if k >= 2:
            cp = pltpu.make_async_copy(stage.at[k], raw.at[k - 2], loc.at[k])
            cp.start()
            raws.append(cp)
        if k == 3:
            ends.append(red_end(0))

    b2 = sm[8:9, :]
    order = [diag, ypeer, core, c]
    NBLK = NB // 2
    holds = [(X, 0), (X, 2 * BLK), (GR, 0), (GR, 2 * BLK)]
    holds_m = [(act, 0), (act, 2 * BLK), (gh, 0), (gh, 2 * BLK)]
    fetch(order[0] * MICRO, 0, 1).start()
    n = 0
    sends = []
    for o, s in enumerate(order):
        for h in range(MICRO):
            b = s * MICRO + h
            slot = n % 2
            if n + 1 < NB:
                nxt = order[(n + 1) // MICRO] * MICRO + (n + 1) % MICRO
                fetch(nxt, 1 - slot, 1).start()
            fetch(b, slot, 1).wait()
            ge_ref, ge_at = holds[o]
            mx_ref, mx_at = holds_m[o]
            ge_blk = ge_ref.at[pl.ds(ge_at + h * BLK, BLK)]
            mx_blk = mx_ref.at[pl.ds(mx_at + h * BLK, BLK)]
            hot, gate_slot = pick(b)
            hot_t = hot.T.astype(BF16)
            rows = pl.ds(pl.multiple_of(b * CAP, 16), CAP)
            res = (RES[rows, :] + b2).astype(BF16).astype(F32)
            g = dot_nn(hot.astype(BF16), gb[slot])
            gg = jnp.sum(g * res, axis=1, keepdims=True)
            gg_row = jnp.sum(hot * gg, axis=0, keepdims=True)
            mine = lax.broadcasted_iota(jnp.int32, (8, BLK), 0) == c
            ggs[o, h] = jnp.where(mine, gg_row, 0.0)
            ge = dot_nn(hot_t, GE[rows, :].astype(BF16))
            mx = dot_nn(hot_t, (gate_slot * res).astype(BF16))
            part = pl.ds(h * BLK, BLK)
            if o == 1:
                for t in range(2):
                    cb = corebuf.at[t, h]
                    remote(cb, cb, core_s.at[t, h], core_r.at[t, h], (r, core)).wait_recv()
                ge = ge + corebuf[0, h].astype(F32)
                mx = mx + corebuf[1, h].astype(F32)
            ge_blk[...] = ge.astype(BF16)
            mx_blk[...] = mx.astype(BF16)
            if o == 0:
                cps = [
                    remote(ge_blk, corebuf.at[0, h], core_s.at[0, h], core_r.at[0, h], (r, core)),
                    remote(mx_blk, corebuf.at[1, h], core_s.at[1, h], core_r.at[1, h], (r, core)),
                ]
            elif o == 1:
                cps = [
                    remote(ge_blk, ge_parts.at[2, part], ge_s.at[1, h], ge_r.at[1, h], (r, ypeer)),
                    pltpu.make_async_copy(mx_blk, mix_out.at[part], loc.at[4 + h]),
                ]
            elif o == 2:
                cps = [
                    remote(ge_blk, ge_parts.at[1, part], ge_s.at[0, h], ge_r.at[0, h], (r, core)),
                    remote(mx_blk, mix_parts.at[1, part], mx_s.at[h], mx_r.at[h], (r, core)),
                ]
            else:
                cps = [
                    pltpu.make_async_copy(ge_blk, ge_parts.at[0, part], loc.at[6 + h]),
                    pltpu.make_async_copy(mx_blk, mix_parts.at[0, part], loc.at[8 + h]),
                ]
            for cp in cps:
                cp.start()
            sends.append((o, cps))
            n += 1
        if o < 3:
            peer = order[o]
            cp = remote(ggs.at[o], gg_all.at[c], gg_s.at[o], gg_r.at[o], (r, peer))
        else:
            cp = pltpu.make_async_copy(ggs.at[3], gg_all.at[c], loc.at[10])
        cp.start()
        sends.append((4 if o < 3 else 5, [cp]))
        if o == 2:
            ends.append(red_end(1))

    for o, cps in sends:
        for t, cp in enumerate(cps):
            if o == 3 or o == 5 or (o == 1 and t == 1):
                cp.wait()
            else:
                cp.wait_send()
    for h in range(MICRO):
        part = pl.ds(h * BLK, BLK)
        for n2, slot2 in enumerate((1, 2)):
            g_ref = ge_parts.at[slot2, part]
            remote(g_ref, g_ref, ge_s.at[n2, h], ge_r.at[n2, h], (r, core)).wait_recv()
        m_ref = mix_parts.at[1, part]
        remote(m_ref, m_ref, mx_s.at[h], mx_r.at[h], (r, core)).wait_recv()
    for o, peer in enumerate((diag, ypeer, core)):
        g_ref = gg_all.at[peer]
        remote(g_ref, g_ref, gg_s.at[o], gg_r.at[o], (r, peer)).wait_recv()
    ends[0].wait()
    ends[1].wait_send()
    d_ref = dexp.at[core]
    remote(d_ref, d_ref, fin_s.at[0], fin_r.at[0], (r, core)).wait_recv()
    for cp in raws:
        cp.wait()


def expert(R, C, CAP, e2_all, cot_all, info_all, wbuf, sm):
    HB = D // R
    hops = R // 2
    TR = C * MICRO * CAP
    vm = pl.BlockSpec(memory_space=pltpu.VMEM)
    hbm = pl.BlockSpec(memory_space=pl.ANY)
    sem = pltpu.SemaphoreType.DMA
    return pl.pallas_call(
        functools.partial(expert_kernel, R, C, CAP),
        name="expert",
        out_shape=(
            jax.ShapeDtypeStruct((3, ROWS, D), BF16),
            jax.ShapeDtypeStruct((2, ROWS, D), BF16),
            jax.ShapeDtypeStruct((ROWS, D), BF16),
            jax.ShapeDtypeStruct((C, MICRO, 8, BLK), F32),
            jax.ShapeDtypeStruct((C, 2, HB, D), BF16),
            jax.ShapeDtypeStruct((2, R, 2, HB, D), BF16),
            jax.ShapeDtypeStruct((8, D), F32),
        ),
        in_specs=[hbm, hbm, hbm, hbm, vm],
        out_specs=(hbm, hbm, hbm, hbm, hbm, hbm, vm),
        scratch_shapes=[
            pltpu.VMEM((2, R, 2, HB, D), BF16),
            pltpu.VMEM((2, BLK, D), BF16),
            pltpu.VMEM((2, BLK, D), BF16),
            pltpu.VMEM((C, MICRO, 16, BLK), F32),
            pltpu.VMEM((TR, D), BF16),
            pltpu.VMEM((D, TR), BF16),
            pltpu.VMEM((TR, D), BF16),
            pltpu.VMEM((D, TR), BF16),
            pltpu.VMEM((TR, D), F32),
            pltpu.VMEM((TR, D), F32),
            pltpu.VMEM((TR, D), BF16),
            pltpu.VMEM((TR, D), BF16),
            pltpu.VMEM((C, R, 2, HB, D), BF16),
            pltpu.VMEM((2, 2, hops, 2, HB, D), BF16),
            pltpu.VMEM((2, MICRO, BLK, D), BF16),
            pltpu.VMEM((2, 2, HB, D), BF16),
            pltpu.VMEM((C, MICRO, 8, BLK), F32),
            sem((2,)), sem((2, 2)), sem((11,)),
            sem((2, 2, hops)), sem((2, 2, hops)),
            sem((1,)), sem((1,)),
            sem((2, MICRO)), sem((2, MICRO)),
            sem((2, MICRO)), sem((2, MICRO)),
            sem((MICRO,)), sem((MICRO,)),
            sem((3,)), sem((3,)),
        ],
        compiler_params=pltpu.CompilerParams(
            collective_id=2, has_side_effects=True, vmem_limit_bytes=62 << 20
        ),
    )(e2_all, cot_all, info_all, wbuf, sm)

def back_kernel(
    R, C, E,
    tok, cot, ge_parts, mix_parts, mix_out, gg, info, rprob, resid, qkv, mixed, probs, wg_in, sm, raw, bias_in,
    out, input_grad, attn_grad, dexp, sums, mixy,
    wg, gp, stage, rbuf, wp, gbr, dres, gm, e1t, dz, ge1, gblk, corein, yin, apart, abuf, small, sbuf,
    loc, red_s, red_r, fin_s, fin_r, mix_s, mix_r, ag_s, ag_r, ar_s, ar_r, sm_s, sm_r,
):
    r, c = lax.axis_index("row"), lax.axis_index("col")
    pos = ring_place(r, R)
    hops = R // 2
    HB = D // R
    WH = D // C
    W3 = 3 * WH
    heads = WH // HEAD_DIM
    right, left = ring_at(pos + 1, R), ring_at(pos - 1, R)
    core, ypeer, diag = col_core(c), col_y(c), col_diag(c)

    copies = [
        pltpu.make_async_copy(raw, stage, loc.at[0]),
        pltpu.make_async_copy(ge_parts, gp, loc.at[1]),
        pltpu.make_async_copy(wg_in.at[:, :, pl.ds(0, HB)], wg, loc.at[2]),
    ]
    for cp in copies:
        cp.start()
    pairs = [(r, core), (r, ypeer)]
    step_bit = 1
    while step_bit < R:
        bit = lax.rem(lax.div(r, step_bit), 2)
        pairs.append((r + step_bit - 2 * step_bit * bit, c))
        step_bit *= 2
    greet([(right, c), (left, c), (r, core), (r, ypeer), (r, diag)] + pairs[2:])

    send_mix = remote(mix_out, mixy, mix_s.at[0], mix_r.at[0], (r, ypeer))
    copies[0].wait()

    def red(k, step):
        reduce_event(stage.at[k], lambda d, s: rbuf.at[k, d, s], red_s, red_r, k, step, r, c, pos, R)

    red(0, 0)
    red(1, 0)
    copies[1].wait()
    copies[2].wait()
    gain1, shift1 = sm[0:1], sm[1:2]
    gain2, shift2 = sm[2:3], sm[3:4]
    router_b = sm[SMALL : SMALL + 8].astype(BF16)
    router3 = jnp.concatenate([router_b, router_b, router_b], axis=0)
    for g in range(C):
        wp[:, g * WH : (g + 1) * WH] = wg[g, :, :, W3:].reshape(D, WH)
    small[...] = jnp.zeros_like(small)
    small[24:32, :] = bias_in[...]

    for h in range(MICRO):
        rp = rprob[h]
        p = gg[0, h]
        for e in range(1, E):
            p = p + gg[e, h]
        gl = rp * (p - jnp.sum(rp * p, axis=0, keepdims=True))
        hi = gl.astype(BF16)
        rest = gl - hi.astype(F32)
        mid = rest.astype(BF16)
        low = (rest - mid.astype(F32)).astype(BF16)
        gl3 = jnp.concatenate([hi.astype(F32), mid.astype(F32), low.astype(F32)], axis=0)
        gl3_t = gl3.T.astype(BF16)
        gl3 = gl3.astype(BF16)
        drt = jnp.zeros((24, D), F32)
        vecs = [jnp.zeros((1, D), F32) for _ in range(3)]
        for i in range(IMG_MB):
            at = h * BLK + i * IMG
            rows = slice(at, at + IMG)
            n2, inv2 = norm_rows(resid[rows, :])
            e2 = (n2 * gain2 + shift2).astype(BF16)
            drt = drt + dot_nn(gl3[:, i * IMG : (i + 1) * IMG], e2)
            ge2 = gp[0, rows, :].astype(F32) + gp[1, rows, :].astype(F32) + gp[2, rows, :].astype(F32)
            ge2 = ge2 + dot_nn(gl3_t[i * IMG : (i + 1) * IMG], router3)
            b = ge2 * gain2
            inner = b - jnp.mean(b, axis=-1, keepdims=True) - n2 * jnp.mean(b * n2, axis=-1, keepdims=True)
            gr = cot[rows, :].astype(F32) + inv2 * inner
            dres[rows, :] = gr
            g16 = gr.astype(BF16)
            gbr[rows, :] = g16
            vecs[0] = vecs[0] + jnp.sum(ge2 * n2, axis=0, keepdims=True)
            vecs[1] = vecs[1] + jnp.sum(ge2, axis=0, keepdims=True)
            vecs[2] = vecs[2] + jnp.sum(g16.astype(F32), axis=0, keepdims=True)
            for g in range(C):
                gm[g, rows, :] = dot_nt(g16, wp[g * WH : (g + 1) * WH, :]).astype(BF16)
            n1, _u = norm_rows(tok[rows, :].astype(F32))
            e1 = n1 * gain1 + shift1
            e1t[h * IMG_MB + i] = e1.T.astype(BF16)
        small[2:3, :] = small[2:3, :] + vecs[0]
        small[3:4, :] = small[3:4, :] + vecs[1]
        small[12:13, :] = small[12:13, :] + vecs[2]
        small[4:12, :] = small[4:12, :] + drt[0:8] + drt[8:16] + drt[16:24]
        red(0, 1 + h)
        red(1, 1 + h)
    send_mix.start()
    get_mix = pltpu.make_async_copy(mix_parts, gp.at[pl.ds(0, 2)], loc.at[3])
    get_mix.start()
    red(0, 3)
    red(1, 3)
    for g in range(C):
        dp = dot_tn(mixed[g], gbr[...]).astype(BF16)
        for g2 in range(C):
            gblk[g2, g * WH : (g + 1) * WH, W3:] = dp[:, g2 * WH : (g2 + 1) * WH]

    order = [diag, ypeer, core, c]
    sends = []
    for o in range(C):
        g = order[o]

        def image(i, vec, g=g):
            rows = pl.ds(pl.multiple_of(i * IMG, 16), IMG)
            z = qkv[g, rows, :]
            gmv = gm[g, rows, :]
            dq, dk, dv = [], [], []
            for h in range(heads):
                q = z[:, h * HEAD_DIM : (h + 1) * HEAD_DIM]
                kk = z[:, WH + h * HEAD_DIM : WH + (h + 1) * HEAD_DIM]
                v = z[:, 2 * WH + h * HEAD_DIM : 2 * WH + (h + 1) * HEAD_DIM]
                gmh = gmv[:, h * HEAD_DIM : (h + 1) * HEAD_DIM]
                p16 = probs[g, i, h]
                p = p16.astype(F32)
                w = dot_nt(gmh, v)
                ds = (p * (w - jnp.sum(p * w, axis=-1, keepdims=True))).astype(BF16)
                dq.append(dot_nn(ds, kk))
                dk.append(dot_tn(ds, q))
                dv.append(dot_tn(p16, gmh))
            d = jnp.concatenate(
                [v.astype(BF16).astype(F32) * SCALE for v in dq] + [v.astype(BF16).astype(F32) for v in dk + dv],
                axis=1,
            )
            dz[rows, :] = d.astype(BF16)
            w = wg[g, :, :, 0:W3].reshape(D, W3)
            part = dot_nt(d.astype(BF16), w)
            ge1[rows, :] = part if o == 0 else ge1[rows, :] + part
            return vec + jnp.sum(d, axis=0, keepdims=True)

        vec = lax.fori_loop(0, IMAGES, image, jnp.zeros((1, W3), F32))
        small[pl.ds(13 + g, 1), 0:W3] = vec
        for j in range(2):
            half = slice(j * (D // 2), (j + 1) * (D // 2))
            acc = jnp.zeros((D // 2, W3), F32)
            for i in range(IMAGES):
                acc = acc + dot_nn(e1t[i, half, :], dz[i * IMG : (i + 1) * IMG, :])
            gblk[g, half, 0:W3] = acc.astype(BF16)
        blk = gblk.at[g]
        if o == 0:
            cp = remote(blk, corein.at[0], ag_s.at[0], ag_r.at[0], (r, core))
            cp.start()
            sends.append(cp)
        elif o == 1:
            remote(blk, corein.at[0], ag_s.at[0], ag_r.at[0], (r, core)).wait_recv()
            blk[...] = (blk[...].astype(F32) + corein[0].astype(F32)).astype(BF16)
            cp = remote(blk, yin, ag_s.at[1], ag_r.at[1], (r, ypeer))
            cp.start()
            sends.append(cp)
        elif o == 2:
            cp = remote(blk, corein.at[1], ag_s.at[2], ag_r.at[2], (r, core))
            cp.start()
            sends.append(cp)
        if o == 0:
            for k in range(2):
                stage[k, r] = reduce_finish(
                    stage.at[k], lambda d, s, k=k: rbuf.at[k, d, s], red_s, red_r, k, r, c, pos, R
                ).astype(BF16)
                cp = remote(stage.at[k, r], dexp.at[c], fin_s.at[k], fin_r.at[k], (r, ypeer if k == 0 else diag))
                cp.start()
                sends.append(cp)

    remote(gblk.at[c], corein.at[1], ag_s.at[2], ag_r.at[2], (r, core)).wait_recv()
    remote(gblk.at[c], yin, ag_s.at[1], ag_r.at[1], (r, ypeer)).wait_recv()
    for o in range(R):
        rows = slice(o * HB, (o + 1) * HB)
        tot = gblk[c, rows, :].astype(F32) + corein[1, rows, :].astype(F32) + yin[rows, :].astype(F32)
        apart[o, 0] = tot[0 : HB // 2].astype(BF16)
        apart[o, 1] = tot[HB // 2 :].astype(BF16)

    def ring(step):
        reduce_event(apart, lambda d, s: abuf.at[d, s], ar_s, ar_r, 0, step, r, c, pos, R)

    ring(0)

    dg = jnp.zeros((1, D), F32)
    dsh = jnp.zeros((1, D), F32)
    for i in range(IMAGES):
        rows = slice(i * IMG, (i + 1) * IMG)
        n1, inv1 = norm_rows(tok[rows, :].astype(F32))
        a = ge1[rows, :]
        b = a * gain1
        inner = b - jnp.mean(b, axis=-1, keepdims=True) - n1 * jnp.mean(b * n1, axis=-1, keepdims=True)
        input_grad[rows, :] = (dres[rows, :] + inv1 * inner).astype(BF16)
        dg = dg + jnp.sum(a * n1, axis=0, keepdims=True)
        dsh = dsh + jnp.sum(a, axis=0, keepdims=True)
        if i == 1:
            ring(1)
    small[0:1, :] = dg
    small[1:2, :] = dsh

    for n, peer in enumerate(pairs):
        size = 24 if n < 2 else 32
        cp = remote(small.at[pl.ds(0, size)], sbuf.at[n, pl.ds(0, size)], sm_s.at[n], sm_r.at[n], peer)
        cp.start()
        cp.wait()
        small[0:size, :] = small[0:size, :] + sbuf[n, 0:size, :]
        if n == 1:
            ring(2)
        if n == 3:
            ring(3)
    sums[...] = small[...]

    send_mix.wait()
    get_far = pltpu.make_async_copy(mixy, gp.at[2], loc.at[1])
    get_far.start()
    get_mix.wait()
    get_far.wait()
    for i in range(IMAGES):
        rows = slice(i * IMG, (i + 1) * IMG)
        o = resid[rows, :] + gp[0, rows, :].astype(F32) + gp[1, rows, :].astype(F32) + gp[2, rows, :].astype(F32)
        out[rows, :] = o.astype(BF16)

    total = reduce_finish(apart, lambda d, s: abuf.at[d, s], ar_s, ar_r, 0, r, c, pos, R)
    attn_grad[...] = total.reshape(HB, D)
    for cp in sends:
        cp.wait_send()
    for k, peer in enumerate((ypeer, diag)):
        d_ref = dexp.at[peer]
        remote(d_ref, d_ref, fin_s.at[k], fin_r.at[k], (r, peer)).wait_recv()


def back(R, C, E, tok, cot, ge_parts, mix_parts, mix_out, gg, info, rprob, resid, qkv, mixed, probs, wg, sm, raw, bias):
    HB = D // R
    WH = D // C
    hops = R // 2
    vm = pl.BlockSpec(memory_space=pltpu.VMEM)
    hbm = pl.BlockSpec(memory_space=pl.ANY)
    sem = pltpu.SemaphoreType.DMA
    steps = 2 + int(math.log2(R))
    return pl.pallas_call(
        functools.partial(back_kernel, R, C, E),
        name="back",
        out_shape=(
            jax.ShapeDtypeStruct((ROWS, D), BF16),
            jax.ShapeDtypeStruct((ROWS, D), BF16),
            jax.ShapeDtypeStruct((HB, D), F32),
            jax.ShapeDtypeStruct((C, 2, HB, D), BF16),
            jax.ShapeDtypeStruct((32, D), F32),
            jax.ShapeDtypeStruct((ROWS, D), BF16),
        ),
        in_specs=[vm, vm, hbm, hbm, hbm, vm, hbm, vm, vm, vm, vm, vm, hbm, vm, hbm, vm],
        out_specs=(vm, vm, vm, hbm, vm, hbm),
        scratch_shapes=[
            pltpu.VMEM((C, R, HB, D), BF16),
            pltpu.VMEM((3, ROWS, D), BF16),
            pltpu.VMEM((2, R, 2, HB, D), BF16),
            pltpu.VMEM((2, 2, hops, 2, HB, D), BF16),
            pltpu.VMEM((D, D), BF16),
            pltpu.VMEM((ROWS, D), BF16),
            pltpu.VMEM((ROWS, D), F32),
            pltpu.VMEM((C, ROWS, WH), BF16),
            pltpu.VMEM((IMAGES, D, IMG), BF16),
            pltpu.VMEM((ROWS, 3 * WH), BF16),
            pltpu.VMEM((ROWS, D), F32),
            pltpu.VMEM((C, D, D), BF16),
            pltpu.VMEM((2, D, D), BF16),
            pltpu.VMEM((D, D), BF16),
            pltpu.VMEM((R, 2, HB // 2, D), BF16),
            pltpu.VMEM((2, hops, 2, HB // 2, D), BF16),
            pltpu.VMEM((32, D), F32),
            pltpu.VMEM((steps, 32, D), F32),
            sem((4,)),
            sem((2, 2, hops)), sem((2, 2, hops)),
            sem((2,)), sem((2,)),
            sem((1,)), sem((1,)),
            sem((3,)), sem((3,)),
            sem((1, 2, hops)), sem((1, 2, hops)),
            sem((steps,)), sem((steps,)),
        ],
        compiler_params=pltpu.CompilerParams(
            collective_id=3, has_side_effects=True, vmem_limit_bytes=62 << 20
        ),
    )(tok, cot, ge_parts, mix_parts, mix_out, gg, info, rprob, resid, qkv, mixed, probs, wg, sm, raw, bias)

def pad_rows(v):
    return jnp.pad(v.reshape(IMAGES, SEQ, D), ((0, 0), (0, IMG - SEQ), (0, 0))).reshape(ROWS, D)


def unpad_rows(v):
    return v.reshape(IMAGES, IMG, D)[:, :SEQ].reshape(IMAGES * SEQ, D)


def spread(v, at, n):
    wide = jnp.tile(v, (1, n))
    piece = lax.broadcasted_iota(jnp.int32, wide.shape, 1) // v.shape[1]
    return jnp.where(piece == at, wide, jnp.zeros_like(wide))


def prepare(R, C, tokens, cotangent, routes, norm1_gain, norm1_shift, attn_in, attn_bias, attn_proj,
            proj_bias, norm2_gain, norm2_shift, router, expert_in, expert_in_bias, expert_out, expert_out_bias):
    r = lax.axis_index("row")
    HB, WH = D // R, D // C
    norms = spread(jnp.stack([norm1_gain, norm1_shift, norm2_gain, norm2_shift]), r, R)
    thin = jnp.pad(jnp.concatenate([attn_bias, proj_bias[None]], axis=0), ((0, 0), (0, D - WH)))
    owned = spread(jnp.concatenate([router.T, expert_out_bias], axis=0), r, R)
    ff_rows = expert_in_bias.shape[1] * R // D
    inner = spread(expert_in_bias, r, R).reshape(ff_rows, D)
    smalls = jnp.concatenate([norms, thin, owned, inner], axis=0)
    smalls = jnp.pad(smalls, ((0, SMALL - smalls.shape[0]), (0, 0)))
    pack = jnp.concatenate([jnp.concatenate([attn_in.reshape(HB, 3 * WH), attn_proj], axis=1), smalls], axis=0)
    wexp = jnp.stack([expert_in, jnp.swapaxes(expert_out, 1, 2)], axis=1)
    named = routes.astype(F32).T.reshape(2, IMAGES, SEQ)
    named = jnp.pad(named, ((0, 6), (0, 0), (0, IMG - SEQ)), constant_values=-1.0)
    rt = jnp.swapaxes(named.reshape(8, MICRO, BLK), 0, 1)
    upper = (lax.broadcasted_iota(jnp.int32, (BLK, BLK), 0) < lax.broadcasted_iota(jnp.int32, (BLK, BLK), 1)).astype(BF16)
    return pad_rows(tokens), pad_rows(cotangent), pack, wexp, rt, upper

def rings(
    tokens, cotangent, routes, norm1_gain, norm1_shift, attn_in, attn_bias, attn_proj, proj_bias,
    norm2_gain, norm2_shift, router, expert_in, expert_in_bias, expert_out, expert_out_bias,
):
    R, C = lax.axis_size("row"), lax.axis_size("col")
    E = expert_in.shape[0]
    HB, WH = D // R, D // C
    W3 = 3 * WH
    rows_mb = IMG_MB * SEQ
    cap = (2 * rows_mb * 13 // (10 * E) + 7) // 8 * 8
    cap = (cap + 15) // 16 * 16
    tok, cot, pack, wexp, rt, upper = prepare(
        R, C, tokens, cotangent, routes, norm1_gain, norm1_shift, attn_in, attn_bias, attn_proj, proj_bias,
        norm2_gain, norm2_shift, router, expert_in, expert_in_bias, expert_out, expert_out_bias,
    )
    wbuf, e2_all, cot_all, info_all, wg, qkv, mixed, probs, resid, rprob, sm = front(
        R, C, E, tok, cot, pack, wexp, rt, upper
    )
    ge_parts, mix_parts, mix_out, gg, dexp_a, raw, bias = expert(R, C, cap, e2_all, cot_all, info_all, wbuf, sm)
    out, input_grad, attn_grad, dexp_b, sums, _ = back(
        R, C, E, tok, cot, ge_parts, mix_parts, mix_out, gg, info_all, rprob, resid, qkv, mixed, probs, wg, sm, raw, bias
    )
    r, c = lax.axis_index("row"), lax.axis_index("col")
    e = lax.broadcasted_iota(jnp.int32, (E, 1, 1, 1), 0)
    near = lax.div(e, 2) == lax.div(c, 2)
    dexp = jnp.where(near, dexp_a, dexp_b).astype(F32)
    norms = lax.dynamic_slice(sums, (0, r * HB), (4, HB))
    grad_router = lax.dynamic_slice(sums, (4 + c, r * HB), (1, HB)).reshape(HB, 1)
    grad_pb = lax.dynamic_slice(sums, (12, c * WH), (1, WH)).reshape(WH)
    group = lax.dynamic_slice(sums, (13 + c, 0), (1, W3)).reshape(3, WH)
    grad_ab = jnp.stack([group[0], group[2]])
    grad_eob = lax.dynamic_slice(sums, (24, r * HB), (1, HB))
    ff = expert_in_bias.shape[1]
    grad_eib = lax.dynamic_slice(sums[25 : 25 + ff * R // D].reshape(1, ff * R), (0, r * ff), (1, ff))
    return (
        unpad_rows(out),
        unpad_rows(input_grad),
        norms[0],
        norms[1],
        attn_grad[:, :W3].reshape(HB, 3, WH),
        grad_ab,
        attn_grad[:, W3:],
        grad_pb,
        norms[2],
        norms[3],
        grad_router,
        dexp[:, 0],
        grad_eib,
        jnp.swapaxes(dexp[:, 1], 1, 2),
        grad_eob,
    )


def solution(mesh):
    in_specs = (
        P(("row", "col"), None),
        P(("row", "col"), None),
        P(("row", "col"), None),
        P("row"),
        P("row"),
        P("row", None, "col"),
        P(None, "col"),
        P("row", "col"),
        P("col"),
        P("row"),
        P("row"),
        P("row", "col"),
        P(None, "row", "col"),
        P("col", "row"),
        P(None, "col", "row"),
        P("col", "row"),
    )
    out_specs = (
        P(("row", "col"), None),
        P(("row", "col"), None),
        P("row"),
        P("row"),
        P("row", None, "col"),
        P(None, "col"),
        P("row", "col"),
        P("col"),
        P("row"),
        P("row"),
        P("row", "col"),
        P(None, "row", "col"),
        P("col", "row"),
        P(None, "col", "row"),
        P("col", "row"),
    )
    body = rings if (mesh.shape["row"], mesh.shape["col"]) == (8, 4) else shards
    return jax.shard_map(body, mesh=mesh, in_specs=in_specs, out_specs=out_specs, check_vma=False)
```

```python
import functools
import math

import jax
import jax.numpy as jnp
from jax import lax
from jax.experimental import pallas as pl
from jax.experimental.pallas import tpu as pltpu
from jax.sharding import PartitionSpec as P

D = 768
HEADS = 12
HEAD_DIM = 64
SEQ = 197
IMG_MB = 2
MICRO = 2
IMAGES = IMG_MB * MICRO
IMG = (SEQ + 15) // 16 * 16
BLK = IMG_MB * IMG
ROWS = IMAGES * IMG
SCALE = HEAD_DIM ** (-0.5)
SMALL = 16
epsilon = 1e-06

MESH = pl.DeviceIdType.MESH
F32 = jnp.float32
BF16 = jnp.bfloat16
NT = (((1,), (1,)), ((), ()))
TN = (((0,), (0,)), ((), ()))


def dot_nn(a, b):
    return jnp.dot(a, b, preferred_element_type=F32)


def dot_nt(a, b):
    return lax.dot_general(a, b, NT, preferred_element_type=F32)


def dot_tn(a, b):
    return lax.dot_general(a, b, TN, preferred_element_type=F32)


def norm_rows(vals):
    centred = vals - jnp.mean(vals, axis=-1, keepdims=True)
    inv_std = lax.rsqrt(jnp.mean(centred * centred, axis=-1, keepdims=True) + epsilon)
    return centred * inv_std, inv_std


def ring_place(r, R):
    half = lax.rem(r, 2)
    return lax.div(r, 2) * (1 - half) + half * (R - 1 - lax.div(r, 2))


def ring_at(p, R):
    p = lax.rem(p + 2 * R, R)
    back = lax.div(p, R // 2)
    return (1 - back) * (2 * p) + back * (2 * (R - 1 - p) + 1)


def col_core(c):
    return c + 1 - 2 * lax.rem(c, 2)


def col_y(c):
    return c + 2 - 4 * lax.div(c, 2)


def col_diag(c):
    return 3 - c


def col_at(c, k):
    low = lax.rem(lax.rem(c, 2) + lax.rem(k, 2), 2)
    high = lax.rem(lax.div(c, 2) + lax.div(k, 2), 2)
    return low + 2 * high


def remote(src, dst, send, recv, dev):
    return pltpu.make_async_remote_copy(
        src_ref=src, dst_ref=dst, send_sem=send, recv_sem=recv, device_id=dev, device_id_type=MESH
    )


def greet(devs):
    bar = pltpu.get_barrier_semaphore()
    for dev in devs:
        pl.semaphore_signal(bar, inc=1, device_id=dev, device_id_type=MESH)
    pl.semaphore_wait(bar, len(devs))

def norm_forward(row_vals, norm_gain, norm_shift):
    centred = row_vals - jnp.mean(row_vals, axis=-1, keepdims=True)
    inv_std = lax.rsqrt(jnp.mean(centred * centred, axis=-1, keepdims=True) + epsilon)
    normed = centred * inv_std
    return (normed * norm_gain + norm_shift, normed, inv_std)


def norm_backward(grad_rows, normed, inv_std, norm_gain):
    scaled = grad_rows * norm_gain
    inner = (
        scaled
        - jnp.mean(scaled, axis=-1, keepdims=True)
        - normed * jnp.mean(scaled * normed, axis=-1, keepdims=True)
    )
    return (inv_std * inner, jnp.sum(grad_rows * normed, axis=0), jnp.sum(grad_rows, axis=0))


def gelu_exact(values):
    return jax.nn.gelu(values, approximate=False)


def shards(
    tokens,
    cotangent,
    routes,
    norm1_gain,
    norm1_shift,
    attn_in,
    attn_bias,
    attn_proj,
    proj_bias,
    norm2_gain,
    norm2_shift,
    router,
    expert_in,
    expert_in_bias,
    expert_out,
    expert_out_bias,
):
    experts_all = expert_in.shape[0]
    rows_mb = IMG_MB * SEQ
    capacity = (2 * rows_mb * 13 // (10 * experts_all) + 7) // 8 * 8
    scaling = HEAD_DIM ** (-0.5)
    head_shape = (IMG_MB, SEQ, HEADS, HEAD_DIM)
    stacked = jnp.stack([jnp.swapaxes(expert_in, 1, 2), expert_out])
    owned_cols = lax.all_to_all(stacked, "col", split_axis=1, concat_axis=2, tiled=True)
    norm_pack = jnp.stack([norm1_gain, norm1_shift, norm2_gain, norm2_shift])
    qkv_rows, proj_rows, router_rows, norm_full, owned, first_bias, second_bias = (
        lax.all_gather(attn_in, "row", axis=0, tiled=True),
        lax.all_gather(attn_proj, "row", axis=0, tiled=True),
        lax.all_gather(router, "row", axis=0, tiled=True),
        lax.all_gather(norm_pack, "row", axis=1, tiled=True),
        lax.all_gather(owned_cols, "row", axis=3, tiled=True),
        lax.all_gather(expert_in_bias, "row", axis=1, tiled=True),
        lax.all_gather(expert_out_bias, "row", axis=1, tiled=True),
    )
    qkv_full, proj_full, router_full, qv_bias, out_bias_vec = (
        lax.all_gather(qkv_rows, "col", axis=2, tiled=True),
        lax.all_gather(proj_rows, "col", axis=1, tiled=True),
        lax.all_gather(router_rows, "col", axis=1, tiled=True),
        lax.all_gather(attn_bias, "col", axis=1, tiled=True),
        lax.all_gather(proj_bias, "col", axis=0, tiled=True),
    )
    norms_wide = norm_full.astype(jnp.float32)
    gain_one, shift_one, gain_two, shift_two = (
        norms_wide[0],
        norms_wide[1],
        norms_wide[2],
        norms_wide[3],
    )
    qv_bias_wide = qv_bias.astype(jnp.float32)
    out_bias_wide = out_bias_vec.astype(jnp.float32)
    first_w = owned[0]
    second_w = owned[1]
    first_bias_wide = first_bias.astype(jnp.float32)[:, None, :]
    second_bias_wide = second_bias.astype(jnp.float32)[:, None, :]
    router_wide = router_full.astype(jnp.float32)
    expert_ids = jnp.arange(experts_all, dtype=jnp.int32)
    column_scale = jnp.array([scaling, 1.0, 1.0], jnp.float32)[None, :, None]
    exp_dev = owned.shape[1]
    acc_qkv = jnp.zeros(qkv_full.shape, jnp.float32)
    acc_proj = jnp.zeros(proj_full.shape, jnp.float32)
    acc_router = jnp.zeros(router_full.shape, jnp.float32)
    acc_qv = jnp.zeros(qv_bias.shape, jnp.float32)
    acc_out_bias = jnp.zeros(out_bias_vec.shape, jnp.float32)
    acc_norms = jnp.zeros(norm_full.shape, jnp.float32)
    acc_experts = (
        jnp.zeros((2, exp_dev, owned.shape[2], expert_in.shape[1]), jnp.float32),
        jnp.zeros(expert_in_bias.shape, jnp.float32),
        jnp.zeros(expert_out_bias.shape, jnp.float32),
    )
    outputs = []
    input_grads = []
    for batch_index in range(MICRO):
        offset = batch_index * rows_mb
        row_vals = tokens[offset : offset + rows_mb].astype(jnp.float32)
        grad_out = cotangent[offset : offset + rows_mb].astype(jnp.float32)
        route_mb = routes[offset : offset + rows_mb]
        normed_out1, normed1, inv_std1 = norm_forward(row_vals, gain_one, shift_one)
        entry1 = normed_out1.astype(jnp.bfloat16)
        projected = jnp.einsum("td,dje->tje", entry1, qkv_full, preferred_element_type=jnp.float32)
        query_rows = (
            ((projected[:, 0] + qv_bias_wide[0]) * scaling).astype(jnp.bfloat16).reshape(head_shape)
        )
        key_rows = projected[:, 1].astype(jnp.bfloat16).reshape(head_shape)
        value_rows = (projected[:, 2] + qv_bias_wide[1]).astype(jnp.bfloat16).reshape(head_shape)
        scores = jnp.einsum(
            "ishd,ijhd->ihsj", query_rows, key_rows, preferred_element_type=jnp.float32
        )
        row_peak = jnp.max(scores, axis=-1, keepdims=True)
        exp_scores = jnp.exp(scores - row_peak)
        totals = jnp.sum(exp_scores, axis=-1, keepdims=True)
        attn_probs = exp_scores / totals
        log_totals = row_peak + jnp.log(totals)
        attn_mixed = (
            jnp.einsum(
                "ihsj,ijhd->ishd",
                attn_probs.astype(jnp.bfloat16),
                value_rows,
                preferred_element_type=jnp.float32,
            )
            .reshape(rows_mb, D)
            .astype(jnp.bfloat16)
        )
        branch = jnp.dot(attn_mixed, proj_full, preferred_element_type=jnp.float32) + out_bias_wide
        resid = row_vals + branch
        normed_out2, normed2, inv_std2 = norm_forward(resid, gain_two, shift_two)
        entry2 = normed_out2.astype(jnp.bfloat16)
        logits = jnp.dot(entry2, router_full, preferred_element_type=jnp.float32)
        router_probs = jax.nn.softmax(logits, axis=-1)
        chosen = route_mb[:, :, None] == expert_ids[None, None, :]
        gate_values = jnp.sum(jnp.where(chosen, router_probs[:, None, :], 0.0), axis=-1)
        route_flags = chosen.reshape(2 * rows_mb, experts_all).astype(jnp.int32)
        before = jnp.cumsum(route_flags, axis=0) - route_flags
        target = route_mb.reshape(-1) * capacity + jnp.sum(before * route_flags, axis=-1)
        outgoing = (
            jnp.zeros((experts_all * capacity, D), jnp.bfloat16)
            .at[target]
            .set(jnp.repeat(entry2, 2, axis=0))
        )
        arrived = lax.all_to_all(
            outgoing.reshape(experts_all, capacity, D),
            "col",
            split_axis=0,
            concat_axis=1,
            tiled=True,
        )
        pre_act = (
            jnp.einsum("erd,efd->erf", arrived, first_w, preferred_element_type=jnp.float32)
            + first_bias_wide
        )
        active = gelu_exact(pre_act).astype(jnp.bfloat16)
        result = (
            jnp.einsum("erf,efd->erd", active, second_w, preferred_element_type=jnp.float32)
            + second_bias_wide
        ).astype(jnp.bfloat16)
        returned = lax.all_to_all(result, "col", split_axis=1, concat_axis=0, tiled=True).reshape(
            experts_all * capacity, D
        )
        picked = returned[target].reshape(rows_mb, 2, D).astype(jnp.float32)
        outputs.append(
            (resid + jnp.sum(gate_values[:, :, None] * picked, axis=1)).astype(jnp.bfloat16)
        )
        grad_gates = jnp.sum(grad_out[:, None, :] * picked, axis=-1)
        grad_sent = (
            (gate_values[:, :, None] * grad_out[:, None, :])
            .astype(jnp.bfloat16)
            .reshape(2 * rows_mb, D)
        )
        grad_outgoing = (
            jnp.zeros((experts_all * capacity, D), jnp.bfloat16).at[target].set(grad_sent)
        )
        grad_result = lax.all_to_all(
            grad_outgoing.reshape(experts_all, capacity, D),
            "col",
            split_axis=0,
            concat_axis=1,
            tiled=True,
        )
        grad_active = jnp.einsum(
            "erd,efd->erf", grad_result, second_w, preferred_element_type=jnp.float32
        )
        grad_pre = jax.vjp(gelu_exact, pre_act)[1](grad_active)[0].astype(jnp.bfloat16)
        weight_terms = jnp.stack(
            [
                jnp.einsum("erf,erd->efd", grad_pre, arrived, preferred_element_type=jnp.float32),
                jnp.einsum("erf,erd->efd", active, grad_result, preferred_element_type=jnp.float32),
            ]
        )
        in_bias_terms = jnp.sum(grad_pre.astype(jnp.float32), axis=1)
        out_bias_terms = jnp.sum(grad_result.astype(jnp.float32), axis=1)
        weight_piece, in_bias_piece, out_bias_piece = (
            lax.psum_scatter(
                weight_terms.astype(jnp.bfloat16), "row", scatter_dimension=3, tiled=True
            ).astype(jnp.float32),
            lax.psum_scatter(
                in_bias_terms.astype(jnp.bfloat16), "row", scatter_dimension=1, tiled=True
            ).astype(jnp.float32),
            lax.psum_scatter(
                out_bias_terms.astype(jnp.bfloat16), "row", scatter_dimension=1, tiled=True
            ).astype(jnp.float32),
        )
        acc_experts = (
            acc_experts[0] + weight_piece,
            acc_experts[1] + in_bias_piece,
            acc_experts[2] + out_bias_piece,
        )
        grad_entry = jnp.einsum(
            "erf,efd->erd", grad_pre, first_w, preferred_element_type=jnp.float32
        ).astype(jnp.bfloat16)
        grad_back = lax.all_to_all(
            grad_entry, "col", split_axis=1, concat_axis=0, tiled=True
        ).reshape(experts_all * capacity, D)
        grad_entry2 = jnp.sum(grad_back[target].reshape(rows_mb, 2, D).astype(jnp.float32), axis=1)
        grad_probs = jnp.sum(jnp.where(chosen, grad_gates[:, :, None], 0.0), axis=1)
        grad_logits = router_probs * (
            grad_probs - jnp.sum(router_probs * grad_probs, axis=-1, keepdims=True)
        )
        grad_entry2 = grad_entry2 + jnp.dot(
            grad_logits, router_wide.T, precision=lax.Precision.HIGHEST
        )
        acc_router = acc_router + jnp.dot(
            entry2.astype(jnp.float32).T, grad_logits, precision=lax.Precision.HIGHEST
        )
        grad_norm2, gain_two_grad, shift_two_grad = norm_backward(
            grad_entry2, normed2, inv_std2, gain_two
        )
        grad_resid = grad_out + grad_norm2
        grad_branch = grad_resid.astype(jnp.bfloat16)
        acc_proj = acc_proj + jnp.einsum(
            "td,te->de", attn_mixed, grad_branch, preferred_element_type=jnp.float32
        )
        acc_out_bias = acc_out_bias + jnp.sum(grad_branch.astype(jnp.float32), axis=0)
        grad_mixed = (
            jnp.einsum("te,de->td", grad_branch, proj_full, preferred_element_type=jnp.float32)
            .astype(jnp.bfloat16)
            .reshape(head_shape)
        )
        scores_again = jnp.einsum(
            "ishd,ijhd->ihsj", query_rows, key_rows, preferred_element_type=jnp.float32
        )
        probs_again = jnp.exp(scores_again - log_totals)
        grad_weights = jnp.einsum(
            "ishd,ijhd->ihsj", grad_mixed, value_rows, preferred_element_type=jnp.float32
        )
        grad_values = jnp.einsum(
            "ihsj,ishd->ijhd",
            probs_again.astype(jnp.bfloat16),
            grad_mixed,
            preferred_element_type=jnp.float32,
        )
        inner_sum = jnp.sum(probs_again * grad_weights, axis=-1, keepdims=True)
        grad_scores = (probs_again * (grad_weights - inner_sum)).astype(jnp.bfloat16)
        grad_query = jnp.einsum(
            "ihsj,ijhd->ishd", grad_scores, key_rows, preferred_element_type=jnp.float32
        )
        grad_keys = jnp.einsum(
            "ihsj,ishd->ijhd", grad_scores, query_rows, preferred_element_type=jnp.float32
        )
        grad_qkv = jnp.stack(
            [
                grad_query.reshape(rows_mb, D),
                grad_keys.reshape(rows_mb, D),
                grad_values.reshape(rows_mb, D),
            ],
            axis=1,
        ).astype(jnp.bfloat16)
        acc_qkv = (
            acc_qkv
            + jnp.einsum("td,tje->dje", entry1, grad_qkv, preferred_element_type=jnp.float32)
            * column_scale
        )
        grad_sums = jnp.sum(grad_qkv.astype(jnp.float32), axis=0)
        acc_qv = acc_qv + jnp.stack([grad_sums[0] * scaling, grad_sums[2]])
        grad_entry1 = jnp.sum(
            jnp.einsum("tje,dje->tjd", grad_qkv, qkv_full, preferred_element_type=jnp.float32)
            * column_scale,
            axis=1,
        )
        grad_norm1, gain_one_grad, shift_one_grad = norm_backward(
            grad_entry1, normed1, inv_std1, gain_one
        )
        input_grads.append((grad_resid + grad_norm1).astype(jnp.bfloat16))
        acc_norms = acc_norms + jnp.stack(
            [gain_one_grad, shift_one_grad, gain_two_grad, shift_two_grad]
        )
    qkv_grad, proj_grad, router_grad, qv_grad, out_bias_grad = (
        lax.psum_scatter(acc_qkv, "col", scatter_dimension=2, tiled=True),
        lax.psum_scatter(acc_proj, "col", scatter_dimension=1, tiled=True),
        lax.psum_scatter(acc_router, "col", scatter_dimension=1, tiled=True),
        lax.psum_scatter(acc_qv, "col", scatter_dimension=1, tiled=True),
        lax.psum_scatter(acc_out_bias, "col", scatter_dimension=0, tiled=True),
    )
    qv_grad, out_bias_grad = lax.psum((qv_grad, out_bias_grad), "row")
    qkv_grad, proj_grad, router_grad, norm_grad = (
        lax.psum_scatter(
            qkv_grad.astype(jnp.bfloat16), "row", scatter_dimension=0, tiled=True
        ).astype(jnp.float32),
        lax.psum_scatter(
            proj_grad.astype(jnp.bfloat16), "row", scatter_dimension=0, tiled=True
        ).astype(jnp.float32),
        lax.psum_scatter(
            router_grad.astype(jnp.bfloat16), "row", scatter_dimension=0, tiled=True
        ).astype(jnp.float32),
        lax.psum_scatter(
            acc_norms.astype(jnp.bfloat16), "row", scatter_dimension=1, tiled=True
        ).astype(jnp.float32),
    )
    expert_stack, in_bias_grad, out_bias_expert = acc_experts
    norm_grad = lax.psum(norm_grad, "col")
    expert_blocks = lax.all_to_all(
        expert_stack.astype(jnp.bfloat16), "col", split_axis=2, concat_axis=1, tiled=True
    ).astype(expert_stack.dtype)
    return (
        jnp.concatenate(outputs, axis=0),
        jnp.concatenate(input_grads, axis=0),
        norm_grad[0],
        norm_grad[1],
        qkv_grad,
        qv_grad,
        proj_grad,
        out_bias_grad,
        norm_grad[2],
        norm_grad[3],
        router_grad,
        jnp.swapaxes(expert_blocks[0], 1, 2),
        in_bias_grad,
        expert_blocks[1],
        out_bias_expert,
    )

def ring_event(buf_of, sends, recvs, flow, step, r, c, pos, R, source_of=None, first=0):
    right, left = ring_at(pos + 1, R), ring_at(pos - 1, R)
    hops = R // 2
    from_left, from_right = ring_at(pos - step, R), ring_at(pos + step, R)
    a, b = buf_of(from_left), buf_of(from_right)
    if step > first:
        remote(a, a, sends.at[flow, 0, step - 1], recvs.at[flow, 0, step - 1], (right, c)).wait_recv()
        remote(b, b, sends.at[flow, 1, step - 1], recvs.at[flow, 1, step - 1], (left, c)).wait_recv()
    at_a, at_b = a, b
    if step == first and source_of is not None:
        at_a, at_b = source_of(from_left), source_of(from_right)
    if step == hops - 1:
        a, b, at_a, at_b = a.at[0], b.at[1], at_a.at[0], at_b.at[1]
    remote(at_a, a, sends.at[flow, 0, step], recvs.at[flow, 0, step], (right, c)).start()
    remote(at_b, b, sends.at[flow, 1, step], recvs.at[flow, 1, step], (left, c)).start()


def ring_finish(buf_of, sends, recvs, flow, r, c, pos, R, first, last):
    right, left = ring_at(pos + 1, R), ring_at(pos - 1, R)
    hops = R // 2
    if last > first:
        a, b = buf_of(ring_at(pos - last, R)), buf_of(ring_at(pos + last, R))
        if last == hops:
            a, b = a.at[0], b.at[1]
        remote(a, a, sends.at[flow, 0, last - 1], recvs.at[flow, 0, last - 1], (right, c)).wait_recv()
        remote(b, b, sends.at[flow, 1, last - 1], recvs.at[flow, 1, last - 1], (left, c)).wait_recv()
    own = buf_of(r)
    for step in range(first, last):
        a, b = (own, own) if step < hops - 1 else (own.at[0], own.at[1])
        remote(a, a, sends.at[flow, 0, step], recvs.at[flow, 0, step], (right, c)).wait_send()
        remote(b, b, sends.at[flow, 1, step], recvs.at[flow, 1, step], (left, c)).wait_send()


def front_kernel(
    R, C, E, SPLIT,
    tok, cot, pack, wexp, rt, upper,
    wbuf, e2_all, cot_all, info_all, wg_out, qkv_out, mixed_out, probs_out, resid_out, rprob, sm_out,
    wg, norm1, e2, wp, info, qkv, mixed, probs, resid,
    ring_s, ring_r, yring_s, yring_r, fan_s, fan_r, y_s, y_r,
    a2a_s, a2a_r, flow_s, flow_r, cot_s, cot_r, e2_s, e2_r, inf_s, inf_r, loc, keep_sem,
):
    r, c = lax.axis_index("row"), lax.axis_index("col")
    pos = ring_place(r, R)
    hops = R // 2
    right, left = ring_at(pos + 1, R), ring_at(pos - 1, R)
    core, ypeer, diag = col_core(c), col_y(c), col_diag(c)
    greet([(right, c), (left, c), (r, core), (r, ypeer), (r, diag)])
    HALF = 64
    TAIL = pack.shape[0] - HALF
    HB, WH = D // R, D // C
    W3 = 3 * WH
    heads = WH // HEAD_DIM

    at_l = [ring_at(pos - s, R) for s in range(hops + 1)]
    at_r = [ring_at(pos + s, R) for s in range(hops + 1)]
    rows_by = [r]
    for s in range(1, hops):
        rows_by += [at_l[s], at_r[s]]
    rows_by.append(at_l[hops])

    def fan(kind, j, col):
        blk = wg.at[col, rows_by[j]]
        return remote(blk, blk, fan_s.at[kind, j], fan_r.at[kind, j], (r, core))

    def over_y(n, j, col):
        blk = wg.at[col, rows_by[j]]
        return remote(blk, blk, y_s.at[n], y_r.at[n], (r, ypeer))

    def own_ring(d, s, blk):
        if s == hops - 1:
            blk = blk.at[pl.ds(0, HALF)] if d == 0 else blk.at[pl.ds(HALF, TAIL)]
        return remote(blk, blk, ring_s.at[d, s], ring_r.at[d, s], (right if d == 0 else left, c))

    def far_ring(d, s, blk):
        if s == hops - 1:
            blk = blk.at[pl.ds(0, HALF)] if d == 0 else blk.at[pl.ds(HALF, TAIL)]
        return remote(blk, blk, yring_s.at[d, s], yring_r.at[d, s], (right if d == 0 else left, c))

    own = wg.at[c, r]
    remote(pack, own, ring_s.at[0, 0], ring_r.at[0, 0], (right, c)).start()
    remote(pack, own, ring_s.at[1, 0], ring_r.at[1, 0], (left, c)).start()
    remote(pack, own, y_s.at[0], y_r.at[0], (r, ypeer)).start()
    remote(pack, own, fan_s.at[0, 0], fan_r.at[0, 0], (r, core)).start()
    own_pack = pltpu.make_async_copy(pack, own, loc.at[0])
    own_pack.start()
    own_exp = pltpu.make_async_copy(wexp.at[c], wbuf.at[c, r], loc.at[1])
    own_exp.start()
    own_cot = pltpu.make_async_copy(cot, cot_all.at[c], loc.at[2])
    own_cot.start()
    peers = [core, ypeer, diag]

    def a2a(n):
        return remote(wexp.at[peers[n]], wbuf.at[c, r], a2a_s.at[n], a2a_r.at[n], (r, peers[n]))

    def a2a_in(n):
        blk = wbuf.at[peers[n], r]
        return remote(blk, blk, a2a_s.at[n], a2a_r.at[n], (r, peers[n]))

    a2a(0).start()

    for i in range(IMAGES):
        rows = slice(i * IMG, (i + 1) * IMG)
        norm1[rows, :] = norm_rows(tok[rows, :].astype(F32))[0]

    over_y(0, 0, ypeer).wait_recv()
    far_ring(0, 0, wg.at[ypeer, r]).start()
    far_ring(1, 0, wg.at[ypeer, r]).start()
    fan(1, 0, ypeer).start()
    remote(cot, cot_all.at[c], cot_s.at[1], cot_r.at[1], (r, ypeer)).start()
    for s in range(1, hops + 1):
        for ring, col, kind in ((own_ring, c, 0), (far_ring, ypeer, 1)):
            for d, o in enumerate((at_l[s], at_r[s])):
                blk = wg.at[col, o]
                ring(d, s - 1, blk).wait_recv()
                if s < hops:
                    ring(d, s, blk).start()
            fan(kind, 2 * s - 1, col).start()
            if s < hops:
                fan(kind, 2 * s, col).start()
        if s == 2:
            a2a(1).start()
            a2a(2).start()
    own_pack.wait()
    own_exp.wait()

    def flow_buf(k):
        f = col_at(c, k)
        return lambda o: wbuf.at[f, o]

    def gather(k, s):
        if s < SPLIT[k]:
            ring_event(flow_buf(k), flow_s, flow_r, k, s, r, c, pos, R)

    gather(0, 0)
    a2a_in(0).wait_recv()
    gather(1, 0)
    remote(cot, cot_all.at[c], cot_s.at[0], cot_r.at[0], (r, core)).start()
    for j in range(R):
        fan(0, j, core).wait_recv()
        fan(1, j, diag).wait_recv()
    send_wg = pltpu.make_async_copy(wg, wg_out, loc.at[3])
    send_wg.start()

    own_small = jnp.zeros((SMALL, D), F32)
    for o in range(R):
        own_small = own_small + wg[c, o, HB : HB + SMALL, :].astype(F32)
    gain1, shift1 = own_small[0:1], own_small[1:2]
    gain2, shift2 = own_small[2:3], own_small[3:4]
    lane = lax.broadcasted_iota(jnp.int32, (1, W3), 1)
    col_scale = jnp.where(lane < WH, SCALE, 1.0).astype(F32)
    keep = lax.broadcasted_iota(jnp.int32, (1, IMG), 1) < SEQ
    rtr, pb, biases = [], [], []
    for g in range(C):
        wp[:, g * WH : (g + 1) * WH] = wg[g, :, 0:HB, W3:].reshape(D, WH)
        small = wg[g, 0, HB : HB + SMALL, :].astype(F32)
        bq, bv = small[4:5, :WH], small[5:6, :WH]
        biases.append(jnp.concatenate([bq, jnp.zeros_like(bq), bv], axis=1))
        pb.append(small[6:7, :WH])
        acc = jnp.zeros((1, D), F32)
        for o in range(R):
            acc = acc + wg[g, o, HB : HB + SMALL, :].astype(F32)[7:8]
        rtr.append(acc)
    pbias = jnp.concatenate(pb, axis=1)
    router_t = jnp.concatenate(rtr + [jnp.zeros((8 - C, D), F32)], axis=0)
    sm_out[0:SMALL, :] = own_small
    sm_out[SMALL : SMALL + 8, :] = router_t
    router_b = router_t.astype(BF16)
    exp_id = lax.broadcasted_iota(jnp.int32, (8, BLK), 0)

    def e2_copy(n, i, who, peer):
        part = pl.ds(i * IMG, IMG)
        src = e2.at[part] if n < 2 else e2_all.at[who, part]
        return remote(src, e2_all.at[who, part], e2_s.at[n, i], e2_r.at[n, i], (r, peer))

    locals_ = []
    for i in range(IMAGES):
        rows = slice(i * IMG, (i + 1) * IMG)
        entry1 = (norm1[rows, :] * gain1 + shift1).astype(BF16)
        acc = tok[rows, :].astype(F32) + pbias
        for g in range(C):
            w = wg[g, :, 0:HB, 0:W3].reshape(D, W3)
            z = ((dot_nn(entry1, w) + biases[g]) * col_scale).astype(BF16)
            qkv[g, rows, :] = z
            outs = []
            for h in range(heads):
                q = z[:, h * HEAD_DIM : (h + 1) * HEAD_DIM]
                kk = z[:, WH + h * HEAD_DIM : WH + (h + 1) * HEAD_DIM]
                v = z[:, 2 * WH + h * HEAD_DIM : 2 * WH + (h + 1) * HEAD_DIM]
                s = jnp.where(keep, dot_nt(q, kk), -1e30)
                ex = jnp.exp(s - jnp.max(s, axis=-1, keepdims=True))
                p = (ex / jnp.sum(ex, axis=-1, keepdims=True)).astype(BF16)
                probs[g, i, h] = p
                outs.append(dot_nn(p, v))
            mix = jnp.concatenate(outs, axis=1).astype(BF16)
            mixed[g, rows, :] = mix
            acc = acc + dot_nn(mix, wp[g * WH : (g + 1) * WH, :])
        resid[rows, :] = acc
        e2[rows, :] = (norm_rows(acc)[0] * gain2 + shift2).astype(BF16)
        e2_copy(1, i, c, ypeer).start()
        e2_copy(0, i, c, core).start()
        part = pl.ds(i * IMG, IMG)
        cp = pltpu.make_async_copy(e2.at[part], e2_all.at[c, part], loc.at[4 + i])
        cp.start()
        locals_.append(cp)
        for n, (src, dst) in enumerate((
            (qkv.at[:, part], qkv_out.at[:, part]),
            (mixed.at[:, part], mixed_out.at[:, part]),
            (probs.at[:, i], probs_out.at[:, i]),
            (resid.at[part], resid_out.at[part]),
        )):
            cp = pltpu.make_async_copy(src, dst, keep_sem.at[n, i])
            cp.start()
            locals_.append(cp)
        if i % IMG_MB == IMG_MB - 1:
            h = i // IMG_MB
            blk = e2[h * BLK : (h + 1) * BLK, :]
            logits = jnp.where(exp_id < E, dot_nt(router_b, blk), -1e30)
            ex = jnp.exp(logits - jnp.max(logits, axis=0, keepdims=True))
            prob = ex / jnp.sum(ex, axis=0, keepdims=True)
            rprob[h] = prob
            named = rt[h]
            member = (named[0:1] == exp_id.astype(F32)) | (named[1:2] == exp_id.astype(F32))
            flags = jnp.where(member, 1.0, 0.0)
            rank = dot_nn(flags.astype(BF16), upper[...])
            info[h, 0:8, :] = jnp.where(member, rank, -1.0)
            info[h, 8:16, :] = jnp.where(member, prob, 0.0)
        if i == IMAGES - 1:
            cp = pltpu.make_async_copy(info, info_all.at[c], loc.at[4 + IMAGES])
            cp.start()
            locals_.append(cp)
            for n, peer in enumerate(peers):
                remote(info, info_all.at[c], inf_s.at[n], inf_r.at[n], (r, peer)).start()
        if i > 0:
            e2_copy(1, i - 1, ypeer, ypeer).wait_recv()
            e2_copy(2, i - 1, ypeer, core).start()
        gather(0, 1 + i)
        gather(1, 1 + i)
        if i == 1:
            for n in (1, 2):
                a2a_in(n).wait_recv()
        if i >= 1:
            gather(2, i - 1)
            gather(3, i - 1)
    remote(cot, cot_all.at[ypeer], cot_s.at[1], cot_r.at[1], (r, ypeer)).wait_recv()
    remote(cot_all.at[ypeer], cot_all.at[ypeer], cot_s.at[2], cot_r.at[2], (r, core)).start()
    e2_copy(1, IMAGES - 1, ypeer, ypeer).wait_recv()
    e2_copy(2, IMAGES - 1, ypeer, core).start()

    for n, who in ((0, core), (2, diag)):
        blk = cot_all.at[who]
        remote(blk, blk, cot_s.at[n], cot_r.at[n], (r, core)).wait_recv()
    for n in range(3):
        remote(cot, cot_all.at[c], cot_s.at[n], cot_r.at[n], (r, core)).wait_send()
    for i in range(IMAGES):
        e2_copy(0, i, core, core).wait_recv()
        e2_copy(2, i, diag, core).wait_recv()
        for n in range(3):
            e2_copy(n, i, c, core).wait_send()
    for n, peer in enumerate(peers):
        cp = remote(info, info_all.at[peer], inf_s.at[n], inf_r.at[n], (r, peer))
        cp.wait_recv()
        cp.wait_send()
        a2a(n).wait_send()
    for j in range(R):
        fan(0, j, c).wait_send()
        fan(1, j, c).wait_send()
    over_y(0, 0, c).wait_send()
    for d in range(2):
        for s in range(hops):
            own_ring(d, s, own).wait_send()
            far_ring(d, s, own).wait_send()
    for k in range(C):
        ring_finish(flow_buf(k), flow_s, flow_r, k, r, c, pos, R, 0, SPLIT[k])
    own_cot.wait()
    send_wg.wait()
    for cp in locals_:
        cp.wait()


def front(R, C, E, SPLIT, tok, cot, pack, wexp, rt, upper):
    WH = D // C
    HB = D // R
    hops = R // 2
    vm = pl.BlockSpec(memory_space=pltpu.VMEM)
    hbm = pl.BlockSpec(memory_space=pl.ANY)
    sem = pltpu.SemaphoreType.DMA
    heads = WH // HEAD_DIM
    return pl.pallas_call(
        functools.partial(front_kernel, R, C, E, SPLIT),
        name="front",
        out_shape=(
            jax.ShapeDtypeStruct((C, R, 2, HB, D), BF16),
            jax.ShapeDtypeStruct((C, ROWS, D), BF16),
            jax.ShapeDtypeStruct((C, ROWS, D), BF16),
            jax.ShapeDtypeStruct((C, MICRO, 16, BLK), F32),
            jax.ShapeDtypeStruct((C, R, HB + SMALL, D), BF16),
            jax.ShapeDtypeStruct((C, ROWS, 3 * WH), BF16),
            jax.ShapeDtypeStruct((C, ROWS, WH), BF16),
            jax.ShapeDtypeStruct((C, IMAGES, heads, IMG, IMG), BF16),
            jax.ShapeDtypeStruct((ROWS, D), F32),
            jax.ShapeDtypeStruct((MICRO, 8, BLK), F32),
            jax.ShapeDtypeStruct((SMALL + 8, D), F32),
        ),
        in_specs=[vm, hbm, vm, hbm, vm, vm],
        out_specs=(hbm,) * 9 + (vm, vm),
        scratch_shapes=[
            pltpu.VMEM((C, R, HB + SMALL, D), BF16),
            pltpu.VMEM((ROWS, D), F32),
            pltpu.VMEM((ROWS, D), BF16),
            pltpu.VMEM((D, D), BF16),
            pltpu.VMEM((MICRO, 16, BLK), F32),
            pltpu.VMEM((C, ROWS, 3 * WH), BF16),
            pltpu.VMEM((C, ROWS, WH), BF16),
            pltpu.VMEM((C, IMAGES, heads, IMG, IMG), BF16),
            pltpu.VMEM((ROWS, D), F32),
            sem((2, hops)), sem((2, hops)),
            sem((2, hops)), sem((2, hops)),
            sem((2, R)), sem((2, R)),
            sem((1,)), sem((1,)),
            sem((3,)), sem((3,)),
            sem((C, 2, hops)), sem((C, 2, hops)),
            sem((3,)), sem((3,)),
            sem((3, IMAGES)), sem((3, IMAGES)),
            sem((3,)), sem((3,)),
            sem((5 + IMAGES,)), sem((4, IMAGES)),
        ],
        compiler_params=pltpu.CompilerParams(
            collective_id=1, has_side_effects=True, vmem_limit_bytes=56 << 20
        ),
    )(tok, cot, pack, wexp, rt, upper)

def reduce_event(parts, rbuf, sends, recvs, slot, step, r, c, pos, R):
    right, left = ring_at(pos + 1, R), ring_at(pos - 1, R)
    hops = R // 2
    to_right, to_left = ring_at(pos + hops - step, R), ring_at(pos - hops + step, R)
    for d, (dest, peer) in enumerate(((to_right, right), (to_left, left))):
        if step > 0:
            got = rbuf(d, step - 1)
            if step == 1:
                got, mine = got.at[d], parts.at[dest, d]
            else:
                mine = parts.at[dest]
            remote(got, got, sends.at[slot, d, step - 1], recvs.at[slot, d, step - 1], (peer, c)).wait_recv()
            mine[...] = (mine[...].astype(F32) + got[...].astype(F32)).astype(BF16)
        src, dst = parts.at[dest], rbuf(d, step)
        if step == 0:
            src, dst = src.at[d], dst.at[d]
        remote(src, dst, sends.at[slot, d, step], recvs.at[slot, d, step], (peer, c)).start()


def reduce_finish(parts, rbuf, sends, recvs, slot, r, c, pos, R):
    hops = R // 2
    total = parts[r].astype(F32)
    for d in range(2):
        got = rbuf(d, hops - 1)
        remote(got, got, sends.at[slot, d, hops - 1], recvs.at[slot, d, hops - 1], (r, c)).wait_recv()
        total = total + got[...].astype(F32)
    for d in range(2):
        for step in range(hops):
            src, dst = parts.at[r], rbuf(d, step)
            if step == 0:
                src, dst = src.at[d], dst.at[d]
            remote(src, dst, sends.at[slot, d, step], recvs.at[slot, d, step], (r, c)).wait_send()
    return total


def expert_kernel(
    R, C, CAP, SPLIT,
    e2_all, cot_all, info_all, wbuf, sm,
    ge_parts, mix_parts, mix_out, gg_all, dexp, raw, wfar, bias_out,
    wv, eb, gb, info, X, GR, RES, GE, act, gh, stage, rbuf, corebuf, mixd, fin, ggs,
    w_sem, eb_sem, loc, flow_s, flow_r, red_s, red_r, fin_s, fin_r, core_s, core_r, ge_s, ge_r, mx_s, mx_r, gg_s, gg_r,
):
    r, c = lax.axis_index("row"), lax.axis_index("col")
    pos = ring_place(r, R)
    hops = R // 2
    HB = D // R
    right, left = ring_at(pos + 1, R), ring_at(pos - 1, R)
    core, ypeer, diag = col_core(c), col_y(c), col_diag(c)
    greet([(right, c), (left, c), (r, core), (r, ypeer), (r, diag)])
    NB = C * MICRO
    TR = NB * CAP

    def from_front(k):
        f = col_at(c, k)
        return lambda o: wbuf.at[f, o]

    def far_buf(k):
        return lambda o: wfar.at[k - 2, o]

    def gather(k, s):
        if s >= SPLIT[k]:
            ring_event(
                far_buf(k), flow_s, flow_r, k - 2, s, r, c, pos, R, from_front(k), SPLIT[k]
            )

    def weights(k):
        if k < 2:
            return [pltpu.make_async_copy(wbuf.at[col_at(c, k)], wv.at[k], w_sem.at[k, 0])]
        cps = []
        origins = [(r, 0)]
        for s in range(1, hops):
            origins += [(ring_at(pos - s, R), s), (ring_at(pos + s, R), s)]
        origins.append((ring_at(pos + hops, R), hops))
        for n, (o, s) in enumerate(origins):
            src = from_front(k)(o) if s <= SPLIT[k] else far_buf(k)(o)
            cps.append(pltpu.make_async_copy(src, wv.at[k - 2, o], w_sem.at[k, n]))
        return cps

    pending = {k: weights(k) for k in range(2)}
    for cp in pending[0] + pending[1]:
        cp.start()
    get_info = pltpu.make_async_copy(info_all, info, loc.at[0])
    get_info.start()
    gather(2, 2)
    gather(3, 0)

    def place(p):
        return col_at(c, C - 1 - lax.div(p, MICRO)), lax.rem(p, MICRO)

    def fetch(p, slot, which):
        s, h = place(p)
        src, dst = (e2_all, eb) if which == 0 else (cot_all, gb)
        return pltpu.make_async_copy(
            src.at[s, pl.ds(pl.multiple_of(h * BLK, 16), BLK)], dst.at[slot], eb_sem.at[which, slot]
        )

    slot_id = lax.broadcasted_iota(jnp.int32, (CAP, BLK), 0).astype(F32)

    def pick(p):
        s, h = place(p)
        code = info[s, h, pl.ds(c, 1), :]
        gate = info[s, h, pl.ds(8 + c, 1), :]
        hot = jnp.where(slot_id == code, 1.0, 0.0)
        gate_slot = jnp.sum(hot * gate, axis=1, keepdims=True)
        return hot, gate_slot

    fetch(0, 0, 0).start()
    fetch(0, 0, 1).start()
    get_info.wait()

    def dispatch(p, bias):
        slot = lax.rem(p, 2)

        @pl.when(p + 1 < NB)
        def _():
            fetch(p + 1, 1 - slot, 0).start()
            fetch(p + 1, 1 - slot, 1).start()

        fetch(p, slot, 0).wait()
        fetch(p, slot, 1).wait()
        hot, gate_slot = pick(p)
        hot = hot.astype(BF16)
        rows = pl.ds(pl.multiple_of(p * CAP, 16), CAP)
        X[rows, :] = dot_nn(hot, eb[slot]).astype(BF16)
        g16 = (gate_slot * dot_nn(hot, gb[slot])).astype(BF16)
        GR[rows, :] = g16
        return bias + jnp.sum(g16.astype(F32), axis=0, keepdims=True)

    bias_out[...] = jnp.zeros_like(bias_out)
    out_bias = lax.fori_loop(0, NB // 2, dispatch, jnp.zeros((1, D), F32))
    gather(2, 3)
    gather(3, 1)
    bias_out[0:1, :] = lax.fori_loop(NB // 2, NB, dispatch, out_bias)
    gather(3, 2)

    def red(k, step):
        reduce_event(stage.at[k], lambda d, s: rbuf.at[k, d, s], red_s, red_r, k, step, r, c, pos, R)

    def red_end(k):
        total = reduce_finish(stage.at[k], lambda d, s: rbuf.at[k, d, s], red_s, red_r, k, r, c, pos, R)
        fin[k] = total.astype(BF16)
        if k == 0:
            cp = pltpu.make_async_copy(fin.at[0], dexp.at[c], loc.at[1])
        else:
            cp = remote(fin.at[1], dexp.at[c], fin_s.at[0], fin_r.at[0], (r, core))
        cp.start()
        return cp

    MT = 512
    DT = D // 2
    HALFR = TR // 2

    def ffn(k, at, n):
        f = col_at(c, k)
        b1 = sm[pl.ds(9 + f, 1), :]
        slot = k % 2

        def tile(m, bias):
            rows = pl.ds(pl.multiple_of(at + m * MT, 16), MT)
            win = wv[slot, :, 0].reshape(D, D)
            wout = wv[slot, :, 1].reshape(D, D)
            hid = dot_nn(X[rows, :], win) + b1
            cdf = 0.5 * (1.0 + lax.erf(hid * (2.0 ** -0.5)))
            a16 = (hid * cdf).astype(BF16)
            act[slot, rows, :] = a16
            slope = cdf + hid * (jnp.exp(-0.5 * hid * hid) * ((2.0 * math.pi) ** -0.5))
            ga = dot_nn(GR[rows, :], wout)
            g16 = (ga * slope).astype(BF16)
            gh[slot, rows, :] = g16
            res = dot_nt(a16, wout)
            gen = dot_nt(g16, win)
            if k == 0:
                RES[rows, :] = res
                GE[rows, :] = gen
            else:
                RES[rows, :] = RES[rows, :] + res
                GE[rows, :] = GE[rows, :] + gen
            return bias + jnp.sum(g16.astype(F32), axis=0, keepdims=True)

        bsum = lax.fori_loop(0, n // MT, tile, jnp.zeros((1, D), F32))
        bias_out[pl.ds(1 + f, 1), :] = bias_out[pl.ds(1 + f, 1), :] + bsum

    def weight_grads(k):
        slot = k % 2

        def tile(j, _):
            cols = pl.ds(pl.multiple_of(j * DT, 128), DT)
            blocks = pl.ds(j * (R // 2), R // 2)
            stage[k, blocks, 0] = dot_tn(X[:, cols], gh[slot]).astype(BF16).reshape(R // 2, HB, D)
            stage[k, blocks, 1] = dot_tn(GR[:, cols], act[slot]).astype(BF16).reshape(R // 2, HB, D)
            return 0

        lax.fori_loop(0, 2, tile, 0)

    order = [diag, ypeer, core, c]
    b2 = sm[8:9, :]
    sends = []

    def give_back(o):
        for h in range(MICRO):
            n = o * MICRO + h
            slot = n % 2
            if n + 1 < NB:
                fetch(n + 1, 1 - slot, 1).start()
            fetch(n, slot, 1).wait()
            if o == 0:
                ge_blk, mx_blk = eb.at[h], mixd.at[h]
            elif o == 1:
                ge_blk, mx_blk = corebuf.at[0, h], corebuf.at[1, h]
            else:
                at = pl.ds((o - 2) * MICRO * BLK + h * BLK, BLK)
                ge_blk, mx_blk = X.at[at], GR.at[at]
            hot, gate_slot = pick(n)
            hot_t = hot.T.astype(BF16)
            rows = slice(n * CAP, (n + 1) * CAP)
            res = (RES[rows, :] + b2).astype(BF16).astype(F32)
            g = dot_nn(hot.astype(BF16), gb[slot])
            gg = jnp.sum(g * res, axis=1, keepdims=True)
            gg_row = jnp.sum(hot * gg, axis=0, keepdims=True)
            mine = lax.broadcasted_iota(jnp.int32, (8, BLK), 0) == c
            ggs[o, h] = jnp.where(mine, gg_row, 0.0)
            ge = dot_nn(hot_t, GE[rows, :].astype(BF16))
            mx = dot_nn(hot_t, (gate_slot * res).astype(BF16))
            part = pl.ds(h * BLK, BLK)
            if o == 1:
                for t in range(2):
                    cb = corebuf.at[t, h]
                    remote(cb, cb, core_s.at[t, h], core_r.at[t, h], (r, core)).wait_recv()
                ge = ge + corebuf[0, h].astype(F32)
                mx = mx + corebuf[1, h].astype(F32)
            ge_blk[...] = ge.astype(BF16)
            mx_blk[...] = mx.astype(BF16)
            if o == 0:
                cps = [
                    remote(ge_blk, corebuf.at[0, h], core_s.at[0, h], core_r.at[0, h], (r, core)),
                    remote(mx_blk, corebuf.at[1, h], core_s.at[1, h], core_r.at[1, h], (r, core)),
                ]
            elif o == 1:
                cps = [
                    remote(ge_blk, ge_parts.at[2, part], ge_s.at[1, h], ge_r.at[1, h], (r, ypeer)),
                    pltpu.make_async_copy(mx_blk, mix_out.at[part], loc.at[4 + h]),
                ]
            elif o == 2:
                cps = [
                    remote(ge_blk, ge_parts.at[1, part], ge_s.at[0, h], ge_r.at[0, h], (r, core)),
                    remote(mx_blk, mix_parts.at[1, part], mx_s.at[h], mx_r.at[h], (r, core)),
                ]
            else:
                cps = [
                    pltpu.make_async_copy(ge_blk, ge_parts.at[0, part], loc.at[6 + h]),
                    pltpu.make_async_copy(mx_blk, mix_parts.at[0, part], loc.at[8 + h]),
                ]
            for cp in cps:
                cp.start()
            sends.append((o, cps))
        if o < 3:
            cp = remote(ggs.at[o], gg_all.at[c], gg_s.at[o], gg_r.at[o], (r, order[o]))
        else:
            cp = pltpu.make_async_copy(ggs.at[3], gg_all.at[c], loc.at[10])
        cp.start()
        sends.append((4 if o < 3 else 5, [cp]))

    def load(k):
        for cp in weights(k):
            cp.start()

    def loaded(k):
        for cp in weights(k):
            cp.wait()

    loaded(0)
    ffn(0, 0, HALFR)
    gather(3, 3)
    ffn(0, HALFR, HALFR)
    weight_grads(0)
    red(0, 0)
    loaded(1)
    ffn(1, 0, HALFR)
    ring_finish(far_buf(2), flow_s, flow_r, 0, r, c, pos, R, SPLIT[2], hops)
    load(2)
    ffn(1, HALFR, HALFR)
    red(0, 1)
    ring_finish(far_buf(3), flow_s, flow_r, 1, r, c, pos, R, SPLIT[3], hops)
    load(3)
    weight_grads(1)
    red(1, 0)
    loaded(2)
    fetch(0, 0, 1).start()
    ffn(2, 0, HALFR)
    red(0, 2)
    loaded(3)
    ffn(3, 0, HALFR)
    red(1, 1)
    give_back(0)
    give_back(1)
    red(0, 3)
    ffn(2, HALFR, HALFR)
    red(1, 2)
    ffn(3, HALFR, HALFR)
    end0 = red_end(0)
    weight_grads(2)
    red(1, 3)
    raws = [pltpu.make_async_copy(stage.at[2], raw.at[0], loc.at[2])]
    raws[0].start()
    weight_grads(3)
    raws.append(pltpu.make_async_copy(stage.at[3], raw.at[1], loc.at[3]))
    raws[1].start()
    give_back(2)
    give_back(3)
    end1 = red_end(1)

    for o, cps in sends:
        for t, cp in enumerate(cps):
            if o == 3 or o == 5 or (o == 1 and t == 1):
                cp.wait()
            else:
                cp.wait_send()
    for h in range(MICRO):
        part = pl.ds(h * BLK, BLK)
        for n2, slot2 in enumerate((1, 2)):
            g_ref = ge_parts.at[slot2, part]
            remote(g_ref, g_ref, ge_s.at[n2, h], ge_r.at[n2, h], (r, core)).wait_recv()
        m_ref = mix_parts.at[1, part]
        remote(m_ref, m_ref, mx_s.at[h], mx_r.at[h], (r, core)).wait_recv()
    for o, peer in enumerate((diag, ypeer, core)):
        g_ref = gg_all.at[peer]
        remote(g_ref, g_ref, gg_s.at[o], gg_r.at[o], (r, peer)).wait_recv()
    end0.wait()
    end1.wait_send()
    d_ref = dexp.at[core]
    remote(d_ref, d_ref, fin_s.at[0], fin_r.at[0], (r, core)).wait_recv()
    for cp in raws:
        cp.wait()


def expert(R, C, CAP, SPLIT, e2_all, cot_all, info_all, wbuf, sm):
    HB = D // R
    hops = R // 2
    TR = C * MICRO * CAP
    vm = pl.BlockSpec(memory_space=pltpu.VMEM)
    hbm = pl.BlockSpec(memory_space=pl.ANY)
    sem = pltpu.SemaphoreType.DMA
    return pl.pallas_call(
        functools.partial(expert_kernel, R, C, CAP, SPLIT),
        name="expert",
        out_shape=(
            jax.ShapeDtypeStruct((3, ROWS, D), BF16),
            jax.ShapeDtypeStruct((2, ROWS, D), BF16),
            jax.ShapeDtypeStruct((ROWS, D), BF16),
            jax.ShapeDtypeStruct((C, MICRO, 8, BLK), F32),
            jax.ShapeDtypeStruct((C, 2, HB, D), BF16),
            jax.ShapeDtypeStruct((2, R, 2, HB, D), BF16),
            jax.ShapeDtypeStruct((2, R, 2, HB, D), BF16),
            jax.ShapeDtypeStruct((8, D), F32),
        ),
        in_specs=[hbm, hbm, hbm, hbm, vm],
        out_specs=(hbm, hbm, hbm, hbm, hbm, hbm, hbm, vm),
        scratch_shapes=[
            pltpu.VMEM((2, R, 2, HB, D), BF16),
            pltpu.VMEM((2, BLK, D), BF16),
            pltpu.VMEM((2, BLK, D), BF16),
            pltpu.VMEM((C, MICRO, 16, BLK), F32),
            pltpu.VMEM((TR, D), BF16),
            pltpu.VMEM((TR, D), BF16),
            pltpu.VMEM((TR, D), F32),
            pltpu.VMEM((TR, D), F32),
            pltpu.VMEM((2, TR, D), BF16),
            pltpu.VMEM((2, TR, D), BF16),
            pltpu.VMEM((C, R, 2, HB, D), BF16),
            pltpu.VMEM((2, 2, hops, 2, HB, D), BF16),
            pltpu.VMEM((2, MICRO, BLK, D), BF16),
            pltpu.VMEM((MICRO, BLK, D), BF16),
            pltpu.VMEM((2, 2, HB, D), BF16),
            pltpu.VMEM((C, MICRO, 8, BLK), F32),
            sem((C, R)), sem((2, 2)), sem((11,)),
            sem((2, 2, hops)), sem((2, 2, hops)),
            sem((2, 2, hops)), sem((2, 2, hops)),
            sem((1,)), sem((1,)),
            sem((2, MICRO)), sem((2, MICRO)),
            sem((2, MICRO)), sem((2, MICRO)),
            sem((MICRO,)), sem((MICRO,)),
            sem((3,)), sem((3,)),
        ],
        compiler_params=pltpu.CompilerParams(
            collective_id=2, has_side_effects=True, vmem_limit_bytes=62 << 20
        ),
    )(e2_all, cot_all, info_all, wbuf, sm)

def back_kernel(
    R, C, E,
    tok, cot, ge_parts, mix_parts, mix_out, gg, rprob, resid_in, qkv_in, mixed_in, probs_in, wg_in, sm, raw, bias_in,
    out, input_grad, attn_grad, dexp, sums, mixy,
    wg, gp, resid, qkv, mixed, probs, stage, rbuf, wp, gbr, dres, gm, e1t, dz, ge1, gblk, corein, yin, apart, abuf, small, sbuf,
    loc, red_s, red_r, fin_s, fin_r, mix_s, mix_r, ag_s, ag_r, ar_s, ar_r, sm_s, sm_r,
):
    r, c = lax.axis_index("row"), lax.axis_index("col")
    pos = ring_place(r, R)
    hops = R // 2
    HB = D // R
    WH = D // C
    W3 = 3 * WH
    heads = WH // HEAD_DIM
    right, left = ring_at(pos + 1, R), ring_at(pos - 1, R)
    core, ypeer, diag = col_core(c), col_y(c), col_diag(c)

    copies = [
        pltpu.make_async_copy(raw, stage, loc.at[0]),
        pltpu.make_async_copy(ge_parts, gp, loc.at[1]),
        pltpu.make_async_copy(wg_in.at[:, :, pl.ds(0, HB)], wg, loc.at[2]),
        pltpu.make_async_copy(resid_in, resid, loc.at[4]),
        pltpu.make_async_copy(mixed_in, mixed, loc.at[5]),
        pltpu.make_async_copy(qkv_in, qkv, loc.at[6]),
        pltpu.make_async_copy(probs_in, probs, loc.at[7]),
    ]
    for cp in copies:
        cp.start()
    pairs = [(r, core), (r, ypeer)]
    step_bit = 1
    while step_bit < R:
        bit = lax.rem(lax.div(r, step_bit), 2)
        pairs.append((r + step_bit - 2 * step_bit * bit, c))
        step_bit *= 2
    greet([(right, c), (left, c), (r, core), (r, ypeer), (r, diag)] + pairs[2:])

    send_mix = remote(mix_out, mixy, mix_s.at[0], mix_r.at[0], (r, ypeer))
    send_mix.start()
    copies[0].wait()

    def red(k, step):
        reduce_event(stage.at[k], lambda d, s: rbuf.at[k, d, s], red_s, red_r, k, step, r, c, pos, R)

    red(0, 0)
    red(1, 0)
    copies[1].wait()
    copies[2].wait()
    copies[3].wait()
    gain1, shift1 = sm[0:1], sm[1:2]
    gain2, shift2 = sm[2:3], sm[3:4]
    router_b = sm[SMALL : SMALL + 8].astype(BF16)
    router3 = jnp.concatenate([router_b, router_b, router_b], axis=0)
    for g in range(C):
        wp[:, g * WH : (g + 1) * WH] = wg[g, :, :, W3:].reshape(D, WH)
    small[...] = jnp.zeros_like(small)
    small[24:32, :] = bias_in[...]

    for h in range(MICRO):
        rp = rprob[h]
        p = gg[0, h]
        for e in range(1, E):
            p = p + gg[e, h]
        gl = rp * (p - jnp.sum(rp * p, axis=0, keepdims=True))
        hi = gl.astype(BF16)
        rest = gl - hi.astype(F32)
        mid = rest.astype(BF16)
        low = (rest - mid.astype(F32)).astype(BF16)
        gl3 = jnp.concatenate([hi.astype(F32), mid.astype(F32), low.astype(F32)], axis=0)
        gl3_t = gl3.T.astype(BF16)
        gl3 = gl3.astype(BF16)
        drt = jnp.zeros((24, D), F32)
        vecs = [jnp.zeros((1, D), F32) for _ in range(3)]
        for i in range(IMG_MB):
            at = h * BLK + i * IMG
            rows = slice(at, at + IMG)
            n2, inv2 = norm_rows(resid[rows, :])
            e2 = (n2 * gain2 + shift2).astype(BF16)
            drt = drt + dot_nn(gl3[:, i * IMG : (i + 1) * IMG], e2)
            ge2 = gp[0, rows, :].astype(F32) + gp[1, rows, :].astype(F32) + gp[2, rows, :].astype(F32)
            ge2 = ge2 + dot_nn(gl3_t[i * IMG : (i + 1) * IMG], router3)
            b = ge2 * gain2
            inner = b - jnp.mean(b, axis=-1, keepdims=True) - n2 * jnp.mean(b * n2, axis=-1, keepdims=True)
            gr = cot[rows, :].astype(F32) + inv2 * inner
            dres[rows, :] = gr
            g16 = gr.astype(BF16)
            gbr[rows, :] = g16
            vecs[0] = vecs[0] + jnp.sum(ge2 * n2, axis=0, keepdims=True)
            vecs[1] = vecs[1] + jnp.sum(ge2, axis=0, keepdims=True)
            vecs[2] = vecs[2] + jnp.sum(g16.astype(F32), axis=0, keepdims=True)
            for g in range(C):
                gm[g, rows, :] = dot_nt(g16, wp[g * WH : (g + 1) * WH, :]).astype(BF16)
            n1, _u = norm_rows(tok[rows, :].astype(F32))
            e1 = n1 * gain1 + shift1
            e1t[h * IMG_MB + i] = e1.T.astype(BF16)
        small[2:3, :] = small[2:3, :] + vecs[0]
        small[3:4, :] = small[3:4, :] + vecs[1]
        small[12:13, :] = small[12:13, :] + vecs[2]
        small[4:12, :] = small[4:12, :] + drt[0:8] + drt[8:16] + drt[16:24]
        red(h, 1)
    get_mix = pltpu.make_async_copy(mix_parts, gp.at[pl.ds(0, 2)], loc.at[3])
    get_mix.start()
    red(0, 2)
    copies[4].wait()
    copies[5].wait()
    copies[6].wait()
    for g in range(C):
        dp = dot_tn(mixed[g], gbr[...]).astype(BF16)
        for g2 in range(C):
            gblk[g2, g * WH : (g + 1) * WH, W3:] = dp[:, g2 * WH : (g2 + 1) * WH]

    order = [diag, ypeer, core, c]
    sends = []

    def close(k, peer):
        stage[k, r] = reduce_finish(
            stage.at[k], lambda d, s: rbuf.at[k, d, s], red_s, red_r, k, r, c, pos, R
        ).astype(BF16)
        cp = remote(stage.at[k, r], dexp.at[c], fin_s.at[k], fin_r.at[k], (r, peer))
        cp.start()
        sends.append(cp)

    for o in range(C):
        g = order[o]

        def image(i, vec, g=g):
            rows = pl.ds(pl.multiple_of(i * IMG, 16), IMG)
            z = qkv[g, rows, :]
            gmv = gm[g, rows, :]
            dq, dk, dv = [], [], []
            for h in range(heads):
                q = z[:, h * HEAD_DIM : (h + 1) * HEAD_DIM]
                kk = z[:, WH + h * HEAD_DIM : WH + (h + 1) * HEAD_DIM]
                v = z[:, 2 * WH + h * HEAD_DIM : 2 * WH + (h + 1) * HEAD_DIM]
                gmh = gmv[:, h * HEAD_DIM : (h + 1) * HEAD_DIM]
                p16 = probs[g, i, h]
                p = p16.astype(F32)
                w = dot_nt(gmh, v)
                ds = (p * (w - jnp.sum(p * w, axis=-1, keepdims=True))).astype(BF16)
                dq.append(dot_nn(ds, kk))
                dk.append(dot_tn(ds, q))
                dv.append(dot_tn(p16, gmh))
            d = jnp.concatenate(
                [v.astype(BF16).astype(F32) * SCALE for v in dq] + [v.astype(BF16).astype(F32) for v in dk + dv],
                axis=1,
            )
            dz[rows, :] = d.astype(BF16)
            w = wg[g, :, :, 0:W3].reshape(D, W3)
            part = dot_nt(d.astype(BF16), w)
            ge1[rows, :] = part if o == 0 else ge1[rows, :] + part
            return vec + jnp.sum(d, axis=0, keepdims=True)

        vec = lax.fori_loop(0, IMAGES, image, jnp.zeros((1, W3), F32))
        small[pl.ds(13 + g, 1), 0:W3] = vec
        for j in range(2):
            half = slice(j * (D // 2), (j + 1) * (D // 2))
            acc = jnp.zeros((D // 2, W3), F32)
            for i in range(IMAGES):
                acc = acc + dot_nn(e1t[i, half, :], dz[i * IMG : (i + 1) * IMG, :])
            gblk[g, half, 0:W3] = acc.astype(BF16)
        blk = gblk.at[g]
        if o == 0:
            cp = remote(blk, corein.at[0], ag_s.at[0], ag_r.at[0], (r, core))
            cp.start()
            sends.append(cp)
        elif o == 1:
            remote(blk, corein.at[0], ag_s.at[0], ag_r.at[0], (r, core)).wait_recv()
            blk[...] = (blk[...].astype(F32) + corein[0].astype(F32)).astype(BF16)
            cp = remote(blk, yin, ag_s.at[1], ag_r.at[1], (r, ypeer))
            cp.start()
            sends.append(cp)
        elif o == 2:
            cp = remote(blk, corein.at[1], ag_s.at[2], ag_r.at[2], (r, core))
            cp.start()
            sends.append(cp)
        if o == 0:
            red(1, 2)
        elif o == 1:
            red(0, 3)
        elif o == 2:
            red(1, 3)
            close(0, ypeer)
    close(1, diag)

    remote(gblk.at[c], corein.at[1], ag_s.at[2], ag_r.at[2], (r, core)).wait_recv()
    remote(gblk.at[c], yin, ag_s.at[1], ag_r.at[1], (r, ypeer)).wait_recv()
    for o in range(R):
        rows = slice(o * HB, (o + 1) * HB)
        tot = gblk[c, rows, :].astype(F32) + corein[1, rows, :].astype(F32) + yin[rows, :].astype(F32)
        apart[o, 0] = tot[0 : HB // 2].astype(BF16)
        apart[o, 1] = tot[HB // 2 :].astype(BF16)

    def ring(step):
        reduce_event(apart, lambda d, s: abuf.at[d, s], ar_s, ar_r, 0, step, r, c, pos, R)

    ring(0)

    dg = jnp.zeros((1, D), F32)
    dsh = jnp.zeros((1, D), F32)
    for i in range(IMAGES):
        rows = slice(i * IMG, (i + 1) * IMG)
        n1, inv1 = norm_rows(tok[rows, :].astype(F32))
        a = ge1[rows, :]
        b = a * gain1
        inner = b - jnp.mean(b, axis=-1, keepdims=True) - n1 * jnp.mean(b * n1, axis=-1, keepdims=True)
        input_grad[rows, :] = (dres[rows, :] + inv1 * inner).astype(BF16)
        dg = dg + jnp.sum(a * n1, axis=0, keepdims=True)
        dsh = dsh + jnp.sum(a, axis=0, keepdims=True)
        if i == 1:
            ring(1)
    small[0:1, :] = dg
    small[1:2, :] = dsh

    for n, peer in enumerate(pairs):
        size = 24 if n < 2 else 32
        cp = remote(small.at[pl.ds(0, size)], sbuf.at[n, pl.ds(0, size)], sm_s.at[n], sm_r.at[n], peer)
        cp.start()
        cp.wait()
        small[0:size, :] = small[0:size, :] + sbuf[n, 0:size, :]
        if n == 1:
            ring(2)
        if n == 3:
            ring(3)
    sums[...] = small[...]

    send_mix.wait()
    get_far = pltpu.make_async_copy(mixy, gp.at[2], loc.at[1])
    get_far.start()
    get_mix.wait()
    get_far.wait()
    for i in range(IMAGES):
        rows = slice(i * IMG, (i + 1) * IMG)
        o = resid[rows, :] + gp[0, rows, :].astype(F32) + gp[1, rows, :].astype(F32) + gp[2, rows, :].astype(F32)
        out[rows, :] = o.astype(BF16)

    total = reduce_finish(apart, lambda d, s: abuf.at[d, s], ar_s, ar_r, 0, r, c, pos, R)
    attn_grad[...] = total.reshape(HB, D)
    for cp in sends:
        cp.wait_send()
    for k, peer in enumerate((ypeer, diag)):
        d_ref = dexp.at[peer]
        remote(d_ref, d_ref, fin_s.at[k], fin_r.at[k], (r, peer)).wait_recv()


def back(R, C, E, tok, cot, ge_parts, mix_parts, mix_out, gg, rprob, resid, qkv, mixed, probs, wg, sm, raw, bias):
    HB = D // R
    WH = D // C
    hops = R // 2
    vm = pl.BlockSpec(memory_space=pltpu.VMEM)
    hbm = pl.BlockSpec(memory_space=pl.ANY)
    sem = pltpu.SemaphoreType.DMA
    steps = 2 + int(math.log2(R))
    heads = WH // HEAD_DIM
    return pl.pallas_call(
        functools.partial(back_kernel, R, C, E),
        name="back",
        out_shape=(
            jax.ShapeDtypeStruct((ROWS, D), BF16),
            jax.ShapeDtypeStruct((ROWS, D), BF16),
            jax.ShapeDtypeStruct((HB, D), F32),
            jax.ShapeDtypeStruct((C, 2, HB, D), BF16),
            jax.ShapeDtypeStruct((32, D), F32),
            jax.ShapeDtypeStruct((ROWS, D), BF16),
        ),
        in_specs=[vm, vm, hbm, hbm, hbm, vm, vm, hbm, hbm, hbm, hbm, hbm, vm, hbm, vm],
        out_specs=(vm, vm, vm, hbm, vm, hbm),
        scratch_shapes=[
            pltpu.VMEM((C, R, HB, D), BF16),
            pltpu.VMEM((3, ROWS, D), BF16),
            pltpu.VMEM((ROWS, D), F32),
            pltpu.VMEM((C, ROWS, 3 * WH), BF16),
            pltpu.VMEM((C, ROWS, WH), BF16),
            pltpu.VMEM((C, IMAGES, heads, IMG, IMG), BF16),
            pltpu.VMEM((2, R, 2, HB, D), BF16),
            pltpu.VMEM((2, 2, hops, 2, HB, D), BF16),
            pltpu.VMEM((D, D), BF16),
            pltpu.VMEM((ROWS, D), BF16),
            pltpu.VMEM((ROWS, D), F32),
            pltpu.VMEM((C, ROWS, WH), BF16),
            pltpu.VMEM((IMAGES, D, IMG), BF16),
            pltpu.VMEM((ROWS, 3 * WH), BF16),
            pltpu.VMEM((ROWS, D), F32),
            pltpu.VMEM((C, D, D), BF16),
            pltpu.VMEM((2, D, D), BF16),
            pltpu.VMEM((D, D), BF16),
            pltpu.VMEM((R, 2, HB // 2, D), BF16),
            pltpu.VMEM((2, hops, 2, HB // 2, D), BF16),
            pltpu.VMEM((32, D), F32),
            pltpu.VMEM((steps, 32, D), F32),
            sem((8,)),
            sem((2, 2, hops)), sem((2, 2, hops)),
            sem((2,)), sem((2,)),
            sem((1,)), sem((1,)),
            sem((3,)), sem((3,)),
            sem((1, 2, hops)), sem((1, 2, hops)),
            sem((steps,)), sem((steps,)),
        ],
        compiler_params=pltpu.CompilerParams(
            collective_id=3, has_side_effects=True, vmem_limit_bytes=62 << 20
        ),
    )(tok, cot, ge_parts, mix_parts, mix_out, gg, rprob, resid, qkv, mixed, probs, wg, sm, raw, bias)

def pad_rows(v):
    return jnp.pad(v.reshape(IMAGES, SEQ, D), ((0, 0), (0, IMG - SEQ), (0, 0))).reshape(ROWS, D)


def unpad_rows(v):
    return v.reshape(IMAGES, IMG, D)[:, :SEQ].reshape(IMAGES * SEQ, D)


def spread(v, at, n):
    wide = jnp.tile(v, (1, n))
    piece = lax.broadcasted_iota(jnp.int32, wide.shape, 1) // v.shape[1]
    return jnp.where(piece == at, wide, jnp.zeros_like(wide))


def prepare(R, C, tokens, cotangent, routes, norm1_gain, norm1_shift, attn_in, attn_bias, attn_proj,
            proj_bias, norm2_gain, norm2_shift, router, expert_in, expert_in_bias, expert_out, expert_out_bias):
    r = lax.axis_index("row")
    HB, WH = D // R, D // C
    norms = spread(jnp.stack([norm1_gain, norm1_shift, norm2_gain, norm2_shift]), r, R)
    thin = jnp.pad(jnp.concatenate([attn_bias, proj_bias[None]], axis=0), ((0, 0), (0, D - WH)))
    owned = spread(jnp.concatenate([router.T, expert_out_bias], axis=0), r, R)
    ff_rows = expert_in_bias.shape[1] * R // D
    inner = spread(expert_in_bias, r, R).reshape(ff_rows, D)
    smalls = jnp.concatenate([norms, thin, owned, inner], axis=0)
    smalls = jnp.pad(smalls, ((0, SMALL - smalls.shape[0]), (0, 0)))
    pack = jnp.concatenate([jnp.concatenate([attn_in.reshape(HB, 3 * WH), attn_proj], axis=1), smalls], axis=0)
    wexp = jnp.stack([expert_in, jnp.swapaxes(expert_out, 1, 2)], axis=1)
    named = routes.astype(F32).T.reshape(2, IMAGES, SEQ)
    named = jnp.pad(named, ((0, 6), (0, 0), (0, IMG - SEQ)), constant_values=-1.0)
    rt = jnp.swapaxes(named.reshape(8, MICRO, BLK), 0, 1)
    upper = (lax.broadcasted_iota(jnp.int32, (BLK, BLK), 0) < lax.broadcasted_iota(jnp.int32, (BLK, BLK), 1)).astype(BF16)
    return pad_rows(tokens), pad_rows(cotangent), pack, wexp, rt, upper

SPLIT = (4, 4, 2, 0)


def rings(
    tokens, cotangent, routes, norm1_gain, norm1_shift, attn_in, attn_bias, attn_proj, proj_bias,
    norm2_gain, norm2_shift, router, expert_in, expert_in_bias, expert_out, expert_out_bias,
):
    R, C = lax.axis_size("row"), lax.axis_size("col")
    E = expert_in.shape[0]
    HB, WH = D // R, D // C
    W3 = 3 * WH
    rows_mb = IMG_MB * SEQ
    cap = (2 * rows_mb * 13 // (10 * E) + 7) // 8 * 8
    cap = (cap + 15) // 16 * 16
    tok, cot, pack, wexp, rt, upper = prepare(
        R, C, tokens, cotangent, routes, norm1_gain, norm1_shift, attn_in, attn_bias, attn_proj, proj_bias,
        norm2_gain, norm2_shift, router, expert_in, expert_in_bias, expert_out, expert_out_bias,
    )
    wbuf, e2_all, cot_all, info_all, wg, qkv, mixed, probs, resid, rprob, sm = front(
        R, C, E, SPLIT, tok, cot, pack, wexp, rt, upper
    )
    ge_parts, mix_parts, mix_out, gg, dexp_a, raw, _, bias = expert(
        R, C, cap, SPLIT, e2_all, cot_all, info_all, wbuf, sm
    )
    out, input_grad, attn_grad, dexp_b, sums, _ = back(
        R, C, E, tok, cot, ge_parts, mix_parts, mix_out, gg, rprob, resid, qkv, mixed, probs, wg, sm, raw, bias
    )
    r, c = lax.axis_index("row"), lax.axis_index("col")
    e = lax.broadcasted_iota(jnp.int32, (E, 1, 1, 1), 0)
    near = lax.div(e, 2) == lax.div(c, 2)
    dexp = jnp.where(near, dexp_a, dexp_b).astype(F32)
    norms = lax.dynamic_slice(sums, (0, r * HB), (4, HB))
    grad_router = lax.dynamic_slice(sums, (4 + c, r * HB), (1, HB)).reshape(HB, 1)
    grad_pb = lax.dynamic_slice(sums, (12, c * WH), (1, WH)).reshape(WH)
    group = lax.dynamic_slice(sums, (13 + c, 0), (1, W3)).reshape(3, WH)
    grad_ab = jnp.stack([group[0], group[2]])
    grad_eob = lax.dynamic_slice(sums, (24, r * HB), (1, HB))
    ff = expert_in_bias.shape[1]
    grad_eib = lax.dynamic_slice(sums[25 : 25 + ff * R // D].reshape(1, ff * R), (0, r * ff), (1, ff))
    return (
        unpad_rows(out),
        unpad_rows(input_grad),
        norms[0],
        norms[1],
        attn_grad[:, :W3].reshape(HB, 3, WH),
        grad_ab,
        attn_grad[:, W3:],
        grad_pb,
        norms[2],
        norms[3],
        grad_router,
        dexp[:, 0],
        grad_eib,
        jnp.swapaxes(dexp[:, 1], 1, 2),
        grad_eob,
    )


def solution(mesh):
    in_specs = (
        P(("row", "col"), None),
        P(("row", "col"), None),
        P(("row", "col"), None),
        P("row"),
        P("row"),
        P("row", None, "col"),
        P(None, "col"),
        P("row", "col"),
        P("col"),
        P("row"),
        P("row"),
        P("row", "col"),
        P(None, "row", "col"),
        P("col", "row"),
        P(None, "col", "row"),
        P("col", "row"),
    )
    out_specs = (
        P(("row", "col"), None),
        P(("row", "col"), None),
        P("row"),
        P("row"),
        P("row", None, "col"),
        P(None, "col"),
        P("row", "col"),
        P("col"),
        P("row"),
        P("row"),
        P("row", "col"),
        P(None, "row", "col"),
        P("col", "row"),
        P(None, "col", "row"),
        P("col", "row"),
    )
    body = rings if (mesh.shape["row"], mesh.shape["col"]) == (8, 4) else shards
    return jax.shard_map(body, mesh=mesh, in_specs=in_specs, out_specs=out_specs, check_vma=False)
```

```python
import functools
import math

import jax
import jax.numpy as jnp
from jax import lax
from jax.experimental import pallas as pl
from jax.experimental.pallas import tpu as pltpu
from jax.sharding import PartitionSpec as P

D = 768
HEADS = 12
HEAD_DIM = 64
SEQ = 197
IMG_MB = 2
MICRO = 2
IMAGES = IMG_MB * MICRO
IMG = (SEQ + 15) // 16 * 16
BLK = IMG_MB * IMG
ROWS = IMAGES * IMG
SCALE = HEAD_DIM ** (-0.5)
SMALL = 16
epsilon = 1e-06

MESH = pl.DeviceIdType.MESH
F32 = jnp.float32
BF16 = jnp.bfloat16
NT = (((1,), (1,)), ((), ()))
TN = (((0,), (0,)), ((), ()))


def dot_nn(a, b):
    return jnp.dot(a, b, preferred_element_type=F32)


def dot_nt(a, b):
    return lax.dot_general(a, b, NT, preferred_element_type=F32)


def dot_tn(a, b):
    return lax.dot_general(a, b, TN, preferred_element_type=F32)


def norm_rows(vals):
    centred = vals - jnp.mean(vals, axis=-1, keepdims=True)
    inv_std = lax.rsqrt(jnp.mean(centred * centred, axis=-1, keepdims=True) + epsilon)
    return centred * inv_std, inv_std


def ring_place(r, R):
    half = lax.rem(r, 2)
    return lax.div(r, 2) * (1 - half) + half * (R - 1 - lax.div(r, 2))


def ring_at(p, R):
    p = lax.rem(p + 2 * R, R)
    back = lax.div(p, R // 2)
    return (1 - back) * (2 * p) + back * (2 * (R - 1 - p) + 1)


def col_core(c):
    return c + 1 - 2 * lax.rem(c, 2)


def col_y(c):
    return c + 2 - 4 * lax.div(c, 2)


def col_diag(c):
    return 3 - c


def col_at(c, k):
    low = lax.rem(lax.rem(c, 2) + lax.rem(k, 2), 2)
    high = lax.rem(lax.div(c, 2) + lax.div(k, 2), 2)
    return low + 2 * high


def remote(src, dst, send, recv, dev):
    return pltpu.make_async_remote_copy(
        src_ref=src, dst_ref=dst, send_sem=send, recv_sem=recv, device_id=dev, device_id_type=MESH
    )


def greet(devs):
    bar = pltpu.get_barrier_semaphore()
    for dev in devs:
        pl.semaphore_signal(bar, inc=1, device_id=dev, device_id_type=MESH)
    pl.semaphore_wait(bar, len(devs))

def norm_forward(row_vals, norm_gain, norm_shift):
    centred = row_vals - jnp.mean(row_vals, axis=-1, keepdims=True)
    inv_std = lax.rsqrt(jnp.mean(centred * centred, axis=-1, keepdims=True) + epsilon)
    normed = centred * inv_std
    return (normed * norm_gain + norm_shift, normed, inv_std)


def norm_backward(grad_rows, normed, inv_std, norm_gain):
    scaled = grad_rows * norm_gain
    inner = (
        scaled
        - jnp.mean(scaled, axis=-1, keepdims=True)
        - normed * jnp.mean(scaled * normed, axis=-1, keepdims=True)
    )
    return (inv_std * inner, jnp.sum(grad_rows * normed, axis=0), jnp.sum(grad_rows, axis=0))


def gelu_exact(values):
    return jax.nn.gelu(values, approximate=False)


def shards(
    tokens,
    cotangent,
    routes,
    norm1_gain,
    norm1_shift,
    attn_in,
    attn_bias,
    attn_proj,
    proj_bias,
    norm2_gain,
    norm2_shift,
    router,
    expert_in,
    expert_in_bias,
    expert_out,
    expert_out_bias,
):
    experts_all = expert_in.shape[0]
    rows_mb = IMG_MB * SEQ
    capacity = (2 * rows_mb * 13 // (10 * experts_all) + 7) // 8 * 8
    scaling = HEAD_DIM ** (-0.5)
    head_shape = (IMG_MB, SEQ, HEADS, HEAD_DIM)
    stacked = jnp.stack([jnp.swapaxes(expert_in, 1, 2), expert_out])
    owned_cols = lax.all_to_all(stacked, "col", split_axis=1, concat_axis=2, tiled=True)
    norm_pack = jnp.stack([norm1_gain, norm1_shift, norm2_gain, norm2_shift])
    qkv_rows, proj_rows, router_rows, norm_full, owned, first_bias, second_bias = (
        lax.all_gather(attn_in, "row", axis=0, tiled=True),
        lax.all_gather(attn_proj, "row", axis=0, tiled=True),
        lax.all_gather(router, "row", axis=0, tiled=True),
        lax.all_gather(norm_pack, "row", axis=1, tiled=True),
        lax.all_gather(owned_cols, "row", axis=3, tiled=True),
        lax.all_gather(expert_in_bias, "row", axis=1, tiled=True),
        lax.all_gather(expert_out_bias, "row", axis=1, tiled=True),
    )
    qkv_full, proj_full, router_full, qv_bias, out_bias_vec = (
        lax.all_gather(qkv_rows, "col", axis=2, tiled=True),
        lax.all_gather(proj_rows, "col", axis=1, tiled=True),
        lax.all_gather(router_rows, "col", axis=1, tiled=True),
        lax.all_gather(attn_bias, "col", axis=1, tiled=True),
        lax.all_gather(proj_bias, "col", axis=0, tiled=True),
    )
    norms_wide = norm_full.astype(jnp.float32)
    gain_one, shift_one, gain_two, shift_two = (
        norms_wide[0],
        norms_wide[1],
        norms_wide[2],
        norms_wide[3],
    )
    qv_bias_wide = qv_bias.astype(jnp.float32)
    out_bias_wide = out_bias_vec.astype(jnp.float32)
    first_w = owned[0]
    second_w = owned[1]
    first_bias_wide = first_bias.astype(jnp.float32)[:, None, :]
    second_bias_wide = second_bias.astype(jnp.float32)[:, None, :]
    router_wide = router_full.astype(jnp.float32)
    expert_ids = jnp.arange(experts_all, dtype=jnp.int32)
    column_scale = jnp.array([scaling, 1.0, 1.0], jnp.float32)[None, :, None]
    exp_dev = owned.shape[1]
    acc_qkv = jnp.zeros(qkv_full.shape, jnp.float32)
    acc_proj = jnp.zeros(proj_full.shape, jnp.float32)
    acc_router = jnp.zeros(router_full.shape, jnp.float32)
    acc_qv = jnp.zeros(qv_bias.shape, jnp.float32)
    acc_out_bias = jnp.zeros(out_bias_vec.shape, jnp.float32)
    acc_norms = jnp.zeros(norm_full.shape, jnp.float32)
    acc_experts = (
        jnp.zeros((2, exp_dev, owned.shape[2], expert_in.shape[1]), jnp.float32),
        jnp.zeros(expert_in_bias.shape, jnp.float32),
        jnp.zeros(expert_out_bias.shape, jnp.float32),
    )
    outputs = []
    input_grads = []
    for batch_index in range(MICRO):
        offset = batch_index * rows_mb
        row_vals = tokens[offset : offset + rows_mb].astype(jnp.float32)
        grad_out = cotangent[offset : offset + rows_mb].astype(jnp.float32)
        route_mb = routes[offset : offset + rows_mb]
        normed_out1, normed1, inv_std1 = norm_forward(row_vals, gain_one, shift_one)
        entry1 = normed_out1.astype(jnp.bfloat16)
        projected = jnp.einsum("td,dje->tje", entry1, qkv_full, preferred_element_type=jnp.float32)
        query_rows = (
            ((projected[:, 0] + qv_bias_wide[0]) * scaling).astype(jnp.bfloat16).reshape(head_shape)
        )
        key_rows = projected[:, 1].astype(jnp.bfloat16).reshape(head_shape)
        value_rows = (projected[:, 2] + qv_bias_wide[1]).astype(jnp.bfloat16).reshape(head_shape)
        scores = jnp.einsum(
            "ishd,ijhd->ihsj", query_rows, key_rows, preferred_element_type=jnp.float32
        )
        row_peak = jnp.max(scores, axis=-1, keepdims=True)
        exp_scores = jnp.exp(scores - row_peak)
        totals = jnp.sum(exp_scores, axis=-1, keepdims=True)
        attn_probs = exp_scores / totals
        log_totals = row_peak + jnp.log(totals)
        attn_mixed = (
            jnp.einsum(
                "ihsj,ijhd->ishd",
                attn_probs.astype(jnp.bfloat16),
                value_rows,
                preferred_element_type=jnp.float32,
            )
            .reshape(rows_mb, D)
            .astype(jnp.bfloat16)
        )
        branch = jnp.dot(attn_mixed, proj_full, preferred_element_type=jnp.float32) + out_bias_wide
        resid = row_vals + branch
        normed_out2, normed2, inv_std2 = norm_forward(resid, gain_two, shift_two)
        entry2 = normed_out2.astype(jnp.bfloat16)
        logits = jnp.dot(entry2, router_full, preferred_element_type=jnp.float32)
        router_probs = jax.nn.softmax(logits, axis=-1)
        chosen = route_mb[:, :, None] == expert_ids[None, None, :]
        gate_values = jnp.sum(jnp.where(chosen, router_probs[:, None, :], 0.0), axis=-1)
        route_flags = chosen.reshape(2 * rows_mb, experts_all).astype(jnp.int32)
        before = jnp.cumsum(route_flags, axis=0) - route_flags
        target = route_mb.reshape(-1) * capacity + jnp.sum(before * route_flags, axis=-1)
        outgoing = (
            jnp.zeros((experts_all * capacity, D), jnp.bfloat16)
            .at[target]
            .set(jnp.repeat(entry2, 2, axis=0))
        )
        arrived = lax.all_to_all(
            outgoing.reshape(experts_all, capacity, D),
            "col",
            split_axis=0,
            concat_axis=1,
            tiled=True,
        )
        pre_act = (
            jnp.einsum("erd,efd->erf", arrived, first_w, preferred_element_type=jnp.float32)
            + first_bias_wide
        )
        active = gelu_exact(pre_act).astype(jnp.bfloat16)
        result = (
            jnp.einsum("erf,efd->erd", active, second_w, preferred_element_type=jnp.float32)
            + second_bias_wide
        ).astype(jnp.bfloat16)
        returned = lax.all_to_all(result, "col", split_axis=1, concat_axis=0, tiled=True).reshape(
            experts_all * capacity, D
        )
        picked = returned[target].reshape(rows_mb, 2, D).astype(jnp.float32)
        outputs.append(
            (resid + jnp.sum(gate_values[:, :, None] * picked, axis=1)).astype(jnp.bfloat16)
        )
        grad_gates = jnp.sum(grad_out[:, None, :] * picked, axis=-1)
        grad_sent = (
            (gate_values[:, :, None] * grad_out[:, None, :])
            .astype(jnp.bfloat16)
            .reshape(2 * rows_mb, D)
        )
        grad_outgoing = (
            jnp.zeros((experts_all * capacity, D), jnp.bfloat16).at[target].set(grad_sent)
        )
        grad_result = lax.all_to_all(
            grad_outgoing.reshape(experts_all, capacity, D),
            "col",
            split_axis=0,
            concat_axis=1,
            tiled=True,
        )
        grad_active = jnp.einsum(
            "erd,efd->erf", grad_result, second_w, preferred_element_type=jnp.float32
        )
        grad_pre = jax.vjp(gelu_exact, pre_act)[1](grad_active)[0].astype(jnp.bfloat16)
        weight_terms = jnp.stack(
            [
                jnp.einsum("erf,erd->efd", grad_pre, arrived, preferred_element_type=jnp.float32),
                jnp.einsum("erf,erd->efd", active, grad_result, preferred_element_type=jnp.float32),
            ]
        )
        in_bias_terms = jnp.sum(grad_pre.astype(jnp.float32), axis=1)
        out_bias_terms = jnp.sum(grad_result.astype(jnp.float32), axis=1)
        weight_piece, in_bias_piece, out_bias_piece = (
            lax.psum_scatter(
                weight_terms.astype(jnp.bfloat16), "row", scatter_dimension=3, tiled=True
            ).astype(jnp.float32),
            lax.psum_scatter(
                in_bias_terms.astype(jnp.bfloat16), "row", scatter_dimension=1, tiled=True
            ).astype(jnp.float32),
            lax.psum_scatter(
                out_bias_terms.astype(jnp.bfloat16), "row", scatter_dimension=1, tiled=True
            ).astype(jnp.float32),
        )
        acc_experts = (
            acc_experts[0] + weight_piece,
            acc_experts[1] + in_bias_piece,
            acc_experts[2] + out_bias_piece,
        )
        grad_entry = jnp.einsum(
            "erf,efd->erd", grad_pre, first_w, preferred_element_type=jnp.float32
        ).astype(jnp.bfloat16)
        grad_back = lax.all_to_all(
            grad_entry, "col", split_axis=1, concat_axis=0, tiled=True
        ).reshape(experts_all * capacity, D)
        grad_entry2 = jnp.sum(grad_back[target].reshape(rows_mb, 2, D).astype(jnp.float32), axis=1)
        grad_probs = jnp.sum(jnp.where(chosen, grad_gates[:, :, None], 0.0), axis=1)
        grad_logits = router_probs * (
            grad_probs - jnp.sum(router_probs * grad_probs, axis=-1, keepdims=True)
        )
        grad_entry2 = grad_entry2 + jnp.dot(
            grad_logits, router_wide.T, precision=lax.Precision.HIGHEST
        )
        acc_router = acc_router + jnp.dot(
            entry2.astype(jnp.float32).T, grad_logits, precision=lax.Precision.HIGHEST
        )
        grad_norm2, gain_two_grad, shift_two_grad = norm_backward(
            grad_entry2, normed2, inv_std2, gain_two
        )
        grad_resid = grad_out + grad_norm2
        grad_branch = grad_resid.astype(jnp.bfloat16)
        acc_proj = acc_proj + jnp.einsum(
            "td,te->de", attn_mixed, grad_branch, preferred_element_type=jnp.float32
        )
        acc_out_bias = acc_out_bias + jnp.sum(grad_branch.astype(jnp.float32), axis=0)
        grad_mixed = (
            jnp.einsum("te,de->td", grad_branch, proj_full, preferred_element_type=jnp.float32)
            .astype(jnp.bfloat16)
            .reshape(head_shape)
        )
        scores_again = jnp.einsum(
            "ishd,ijhd->ihsj", query_rows, key_rows, preferred_element_type=jnp.float32
        )
        probs_again = jnp.exp(scores_again - log_totals)
        grad_weights = jnp.einsum(
            "ishd,ijhd->ihsj", grad_mixed, value_rows, preferred_element_type=jnp.float32
        )
        grad_values = jnp.einsum(
            "ihsj,ishd->ijhd",
            probs_again.astype(jnp.bfloat16),
            grad_mixed,
            preferred_element_type=jnp.float32,
        )
        inner_sum = jnp.sum(probs_again * grad_weights, axis=-1, keepdims=True)
        grad_scores = (probs_again * (grad_weights - inner_sum)).astype(jnp.bfloat16)
        grad_query = jnp.einsum(
            "ihsj,ijhd->ishd", grad_scores, key_rows, preferred_element_type=jnp.float32
        )
        grad_keys = jnp.einsum(
            "ihsj,ishd->ijhd", grad_scores, query_rows, preferred_element_type=jnp.float32
        )
        grad_qkv = jnp.stack(
            [
                grad_query.reshape(rows_mb, D),
                grad_keys.reshape(rows_mb, D),
                grad_values.reshape(rows_mb, D),
            ],
            axis=1,
        ).astype(jnp.bfloat16)
        acc_qkv = (
            acc_qkv
            + jnp.einsum("td,tje->dje", entry1, grad_qkv, preferred_element_type=jnp.float32)
            * column_scale
        )
        grad_sums = jnp.sum(grad_qkv.astype(jnp.float32), axis=0)
        acc_qv = acc_qv + jnp.stack([grad_sums[0] * scaling, grad_sums[2]])
        grad_entry1 = jnp.sum(
            jnp.einsum("tje,dje->tjd", grad_qkv, qkv_full, preferred_element_type=jnp.float32)
            * column_scale,
            axis=1,
        )
        grad_norm1, gain_one_grad, shift_one_grad = norm_backward(
            grad_entry1, normed1, inv_std1, gain_one
        )
        input_grads.append((grad_resid + grad_norm1).astype(jnp.bfloat16))
        acc_norms = acc_norms + jnp.stack(
            [gain_one_grad, shift_one_grad, gain_two_grad, shift_two_grad]
        )
    qkv_grad, proj_grad, router_grad, qv_grad, out_bias_grad = (
        lax.psum_scatter(acc_qkv, "col", scatter_dimension=2, tiled=True),
        lax.psum_scatter(acc_proj, "col", scatter_dimension=1, tiled=True),
        lax.psum_scatter(acc_router, "col", scatter_dimension=1, tiled=True),
        lax.psum_scatter(acc_qv, "col", scatter_dimension=1, tiled=True),
        lax.psum_scatter(acc_out_bias, "col", scatter_dimension=0, tiled=True),
    )
    qv_grad, out_bias_grad = lax.psum((qv_grad, out_bias_grad), "row")
    qkv_grad, proj_grad, router_grad, norm_grad = (
        lax.psum_scatter(
            qkv_grad.astype(jnp.bfloat16), "row", scatter_dimension=0, tiled=True
        ).astype(jnp.float32),
        lax.psum_scatter(
            proj_grad.astype(jnp.bfloat16), "row", scatter_dimension=0, tiled=True
        ).astype(jnp.float32),
        lax.psum_scatter(
            router_grad.astype(jnp.bfloat16), "row", scatter_dimension=0, tiled=True
        ).astype(jnp.float32),
        lax.psum_scatter(
            acc_norms.astype(jnp.bfloat16), "row", scatter_dimension=1, tiled=True
        ).astype(jnp.float32),
    )
    expert_stack, in_bias_grad, out_bias_expert = acc_experts
    norm_grad = lax.psum(norm_grad, "col")
    expert_blocks = lax.all_to_all(
        expert_stack.astype(jnp.bfloat16), "col", split_axis=2, concat_axis=1, tiled=True
    ).astype(expert_stack.dtype)
    return (
        jnp.concatenate(outputs, axis=0),
        jnp.concatenate(input_grads, axis=0),
        norm_grad[0],
        norm_grad[1],
        qkv_grad,
        qv_grad,
        proj_grad,
        out_bias_grad,
        norm_grad[2],
        norm_grad[3],
        router_grad,
        jnp.swapaxes(expert_blocks[0], 1, 2),
        in_bias_grad,
        expert_blocks[1],
        out_bias_expert,
    )

def ring_event(buf_of, sends, recvs, flow, step, r, c, pos, R, source_of=None, first=0):
    right, left = ring_at(pos + 1, R), ring_at(pos - 1, R)
    hops = R // 2
    from_left, from_right = ring_at(pos - step, R), ring_at(pos + step, R)
    a, b = buf_of(from_left), buf_of(from_right)
    if step > first:
        remote(a, a, sends.at[flow, 0, step - 1], recvs.at[flow, 0, step - 1], (right, c)).wait_recv()
        remote(b, b, sends.at[flow, 1, step - 1], recvs.at[flow, 1, step - 1], (left, c)).wait_recv()
    at_a, at_b = a, b
    if step == first and source_of is not None:
        at_a, at_b = source_of(from_left), source_of(from_right)
    if step == hops - 1:
        a, b, at_a, at_b = a.at[0], b.at[1], at_a.at[0], at_b.at[1]
    remote(at_a, a, sends.at[flow, 0, step], recvs.at[flow, 0, step], (right, c)).start()
    remote(at_b, b, sends.at[flow, 1, step], recvs.at[flow, 1, step], (left, c)).start()


def ring_finish(buf_of, sends, recvs, flow, r, c, pos, R, first, last):
    right, left = ring_at(pos + 1, R), ring_at(pos - 1, R)
    hops = R // 2
    if last > first:
        a, b = buf_of(ring_at(pos - last, R)), buf_of(ring_at(pos + last, R))
        if last == hops:
            a, b = a.at[0], b.at[1]
        remote(a, a, sends.at[flow, 0, last - 1], recvs.at[flow, 0, last - 1], (right, c)).wait_recv()
        remote(b, b, sends.at[flow, 1, last - 1], recvs.at[flow, 1, last - 1], (left, c)).wait_recv()
    own = buf_of(r)
    for step in range(first, last):
        a, b = (own, own) if step < hops - 1 else (own.at[0], own.at[1])
        remote(a, a, sends.at[flow, 0, step], recvs.at[flow, 0, step], (right, c)).wait_send()
        remote(b, b, sends.at[flow, 1, step], recvs.at[flow, 1, step], (left, c)).wait_send()


def front_kernel(
    R, C, E, SPLIT,
    tok, cot_in, pack, wexp, rt,
    wbuf, e2_all, cot_all, info_all, tok_out, wg_out, qkv_out, mixed_out, probs_out, resid_out, rprob, sm_out,
    flat, tokp, cot, wg, norm1, e2, wp, info, qkv, mixed, probs, resid,
    ring_s, ring_r, yring_s, yring_r, fan_s, fan_r, y_s, y_r,
    a2a_s, a2a_r, flow_s, flow_r, cot_s, cot_r, e2_s, e2_r, inf_s, inf_r, loc, keep_sem,
):
    r, c = lax.axis_index("row"), lax.axis_index("col")
    pos = ring_place(r, R)
    hops = R // 2
    right, left = ring_at(pos + 1, R), ring_at(pos - 1, R)
    core, ypeer, diag = col_core(c), col_y(c), col_diag(c)
    greet([(right, c), (left, c), (r, core), (r, ypeer), (r, diag)])
    HALF = 64
    TAIL = pack.shape[0] - HALF
    HB, WH = D // R, D // C
    W3 = 3 * WH
    heads = WH // HEAD_DIM

    at_l = [ring_at(pos - s, R) for s in range(hops + 1)]
    at_r = [ring_at(pos + s, R) for s in range(hops + 1)]
    rows_by = [r]
    for s in range(1, hops):
        rows_by += [at_l[s], at_r[s]]
    rows_by.append(at_l[hops])

    def fan(kind, j, col):
        blk = wg.at[col, rows_by[j]]
        return remote(blk, blk, fan_s.at[kind, j], fan_r.at[kind, j], (r, core))

    def over_y(n, j, col):
        blk = wg.at[col, rows_by[j]]
        return remote(blk, blk, y_s.at[n], y_r.at[n], (r, ypeer))

    def own_ring(d, s, blk):
        if s == hops - 1:
            blk = blk.at[pl.ds(0, HALF)] if d == 0 else blk.at[pl.ds(HALF, TAIL)]
        return remote(blk, blk, ring_s.at[d, s], ring_r.at[d, s], (right if d == 0 else left, c))

    def far_ring(d, s, blk):
        if s == hops - 1:
            blk = blk.at[pl.ds(0, HALF)] if d == 0 else blk.at[pl.ds(HALF, TAIL)]
        return remote(blk, blk, yring_s.at[d, s], yring_r.at[d, s], (right if d == 0 else left, c))

    own = wg.at[c, r]
    remote(pack, own, ring_s.at[0, 0], ring_r.at[0, 0], (right, c)).start()
    remote(pack, own, ring_s.at[1, 0], ring_r.at[1, 0], (left, c)).start()
    remote(pack, own, y_s.at[0], y_r.at[0], (r, ypeer)).start()
    remote(pack, own, fan_s.at[0, 0], fan_r.at[0, 0], (r, core)).start()
    own_pack = pltpu.make_async_copy(pack, own, loc.at[0])
    own_pack.start()
    own_exp = pltpu.make_async_copy(wexp.at[c], wbuf.at[c, r], loc.at[1])
    own_exp.start()
    peers = [core, ypeer, diag]

    def a2a(n):
        return remote(wexp.at[peers[n]], wbuf.at[c, r], a2a_s.at[n], a2a_r.at[n], (r, peers[n]))

    def a2a_in(n):
        blk = wbuf.at[peers[n], r]
        return remote(blk, blk, a2a_s.at[n], a2a_r.at[n], (r, peers[n]))

    a2a(0).start()

    real = lax.broadcasted_iota(jnp.int32, (IMG, 1), 0) < SEQ
    even = tok.shape[0] // 16 * 16

    def images(src):
        flat[0:even, :] = src[0:even, :].astype(F32)
        flat[even : src.shape[0], :] = src[even : src.shape[0], :].astype(F32)
        for i in range(IMAGES):
            yield i, jnp.where(real, flat[i * SEQ : i * SEQ + IMG, :], 0.0)

    for i, rows in images(cot_in):
        cot[i * IMG : (i + 1) * IMG, :] = rows.astype(BF16)
    own_cot = pltpu.make_async_copy(cot, cot_all.at[c], loc.at[2])
    own_cot.start()
    for i, rows in images(tok):
        tokp[i * IMG : (i + 1) * IMG, :] = rows.astype(BF16)
        norm1[i * IMG : (i + 1) * IMG, :] = norm_rows(rows)[0]
    own_tok = pltpu.make_async_copy(tokp, tok_out, loc.at[5 + IMAGES])
    own_tok.start()

    over_y(0, 0, ypeer).wait_recv()
    far_ring(0, 0, wg.at[ypeer, r]).start()
    far_ring(1, 0, wg.at[ypeer, r]).start()
    fan(1, 0, ypeer).start()
    remote(cot, cot_all.at[c], cot_s.at[1], cot_r.at[1], (r, ypeer)).start()
    for s in range(1, hops + 1):
        for ring, col, kind in ((own_ring, c, 0), (far_ring, ypeer, 1)):
            for d, o in enumerate((at_l[s], at_r[s])):
                blk = wg.at[col, o]
                ring(d, s - 1, blk).wait_recv()
                if s < hops:
                    ring(d, s, blk).start()
            fan(kind, 2 * s - 1, col).start()
            if s < hops:
                fan(kind, 2 * s, col).start()
        if s == 2:
            a2a(1).start()
            a2a(2).start()
    own_pack.wait()
    own_exp.wait()

    def flow_buf(k):
        f = col_at(c, k)
        return lambda o: wbuf.at[f, o]

    def gather(k, s):
        if s < SPLIT[k]:
            ring_event(flow_buf(k), flow_s, flow_r, k, s, r, c, pos, R)

    gather(0, 0)
    a2a_in(0).wait_recv()
    gather(1, 0)
    remote(cot, cot_all.at[c], cot_s.at[0], cot_r.at[0], (r, core)).start()
    for j in range(R):
        fan(0, j, core).wait_recv()
        fan(1, j, diag).wait_recv()
    send_wg = pltpu.make_async_copy(wg, wg_out, loc.at[3])
    send_wg.start()

    own_small = jnp.zeros((SMALL, D), F32)
    for o in range(R):
        own_small = own_small + wg[c, o, HB : HB + SMALL, :].astype(F32)
    gain1, shift1 = own_small[0:1], own_small[1:2]
    gain2, shift2 = own_small[2:3], own_small[3:4]
    lane = lax.broadcasted_iota(jnp.int32, (1, W3), 1)
    col_scale = jnp.where(lane < WH, SCALE, 1.0).astype(F32)
    keep = lax.broadcasted_iota(jnp.int32, (1, IMG), 1) < SEQ
    rtr, pb, biases = [], [], []
    for g in range(C):
        wp[:, g * WH : (g + 1) * WH] = wg[g, :, 0:HB, W3:].reshape(D, WH)
        small = wg[g, 0, HB : HB + SMALL, :].astype(F32)
        bq, bv = small[4:5, :WH], small[5:6, :WH]
        biases.append(jnp.concatenate([bq, jnp.zeros_like(bq), bv], axis=1))
        pb.append(small[6:7, :WH])
        acc = jnp.zeros((1, D), F32)
        for o in range(R):
            acc = acc + wg[g, o, HB : HB + SMALL, :].astype(F32)[7:8]
        rtr.append(acc)
    pbias = jnp.concatenate(pb, axis=1)
    router_t = jnp.concatenate(rtr + [jnp.zeros((8 - C, D), F32)], axis=0)
    sm_out[0:SMALL, :] = own_small
    sm_out[SMALL : SMALL + 8, :] = router_t
    router_b = router_t.astype(BF16)
    upper = (
        lax.broadcasted_iota(jnp.int32, (BLK, BLK), 0) < lax.broadcasted_iota(jnp.int32, (BLK, BLK), 1)
    ).astype(BF16)
    exp_id = lax.broadcasted_iota(jnp.int32, (8, BLK), 0)

    def e2_copy(n, i, who, peer):
        part = pl.ds(i * IMG, IMG)
        src = e2.at[part] if n < 2 else e2_all.at[who, part]
        return remote(src, e2_all.at[who, part], e2_s.at[n, i], e2_r.at[n, i], (r, peer))

    locals_ = []
    for i in range(IMAGES):
        rows = slice(i * IMG, (i + 1) * IMG)
        entry1 = (norm1[rows, :] * gain1 + shift1).astype(BF16)
        acc = tokp[rows, :].astype(F32) + pbias
        for g in range(C):
            w = wg[g, :, 0:HB, 0:W3].reshape(D, W3)
            z = ((dot_nn(entry1, w) + biases[g]) * col_scale).astype(BF16)
            qkv[g, rows, :] = z
            outs = []
            for h in range(heads):
                q = z[:, h * HEAD_DIM : (h + 1) * HEAD_DIM]
                kk = z[:, WH + h * HEAD_DIM : WH + (h + 1) * HEAD_DIM]
                v = z[:, 2 * WH + h * HEAD_DIM : 2 * WH + (h + 1) * HEAD_DIM]
                s = jnp.where(keep, dot_nt(q, kk), -1e30)
                ex = jnp.exp(s - jnp.max(s, axis=-1, keepdims=True))
                p = (ex / jnp.sum(ex, axis=-1, keepdims=True)).astype(BF16)
                probs[g, i, h] = p
                outs.append(dot_nn(p, v))
            mix = jnp.concatenate(outs, axis=1).astype(BF16)
            mixed[g, rows, :] = mix
            acc = acc + dot_nn(mix, wp[g * WH : (g + 1) * WH, :])
        resid[rows, :] = acc
        e2[rows, :] = (norm_rows(acc)[0] * gain2 + shift2).astype(BF16)
        e2_copy(1, i, c, ypeer).start()
        e2_copy(0, i, c, core).start()
        part = pl.ds(i * IMG, IMG)
        cp = pltpu.make_async_copy(e2.at[part], e2_all.at[c, part], loc.at[4 + i])
        cp.start()
        locals_.append(cp)
        for n, (src, dst) in enumerate((
            (qkv.at[:, part], qkv_out.at[:, part]),
            (mixed.at[:, part], mixed_out.at[:, part]),
            (probs.at[:, i], probs_out.at[:, i]),
            (resid.at[part], resid_out.at[part]),
        )):
            cp = pltpu.make_async_copy(src, dst, keep_sem.at[n, i])
            cp.start()
            locals_.append(cp)
        if i % IMG_MB == IMG_MB - 1:
            h = i // IMG_MB
            blk = e2[h * BLK : (h + 1) * BLK, :]
            logits = jnp.where(exp_id < E, dot_nt(router_b, blk), -1e30)
            ex = jnp.exp(logits - jnp.max(logits, axis=0, keepdims=True))
            prob = ex / jnp.sum(ex, axis=0, keepdims=True)
            rprob[h] = prob
            named = rt[h]
            member = (named[0:1] == exp_id.astype(F32)) | (named[1:2] == exp_id.astype(F32))
            flags = jnp.where(member, 1.0, 0.0)
            rank = dot_nn(flags.astype(BF16), upper)
            info[h, 0:8, :] = jnp.where(member, rank, -1.0)
            info[h, 8:16, :] = jnp.where(member, prob, 0.0)
        if i == IMAGES - 1:
            cp = pltpu.make_async_copy(info, info_all.at[c], loc.at[4 + IMAGES])
            cp.start()
            locals_.append(cp)
            for n, peer in enumerate(peers):
                remote(info, info_all.at[c], inf_s.at[n], inf_r.at[n], (r, peer)).start()
        if i == 1:
            gather(0, 1)
        if i == 2:
            gather(1, 1)

    def relay(i):
        e2_copy(1, i, ypeer, ypeer).wait_recv()
        e2_copy(2, i, ypeer, core).start()

    relay(0)
    remote(cot, cot_all.at[ypeer], cot_s.at[1], cot_r.at[1], (r, ypeer)).wait_recv()
    remote(cot_all.at[ypeer], cot_all.at[ypeer], cot_s.at[2], cot_r.at[2], (r, core)).start()
    gather(0, 2)
    relay(1)
    gather(1, 2)
    for n in (1, 2):
        a2a_in(n).wait_recv()
    gather(2, 0)
    relay(2)
    gather(0, 3)
    gather(1, 3)
    relay(3)
    gather(2, 1)

    for n, who in ((0, core), (2, diag)):
        blk = cot_all.at[who]
        remote(blk, blk, cot_s.at[n], cot_r.at[n], (r, core)).wait_recv()
    for n in range(3):
        remote(cot, cot_all.at[c], cot_s.at[n], cot_r.at[n], (r, core)).wait_send()
    for i in range(IMAGES):
        e2_copy(0, i, core, core).wait_recv()
        e2_copy(2, i, diag, core).wait_recv()
        for n in range(3):
            e2_copy(n, i, c, core).wait_send()
    for n, peer in enumerate(peers):
        cp = remote(info, info_all.at[peer], inf_s.at[n], inf_r.at[n], (r, peer))
        cp.wait_recv()
        cp.wait_send()
        a2a(n).wait_send()
    for j in range(R):
        fan(0, j, c).wait_send()
        fan(1, j, c).wait_send()
    over_y(0, 0, c).wait_send()
    for d in range(2):
        for s in range(hops):
            own_ring(d, s, own).wait_send()
            far_ring(d, s, own).wait_send()
    for k in range(C):
        ring_finish(flow_buf(k), flow_s, flow_r, k, r, c, pos, R, 0, SPLIT[k])
    own_cot.wait()
    own_tok.wait()
    send_wg.wait()
    for cp in locals_:
        cp.wait()


def front(R, C, E, SPLIT, tok, cot, pack, wexp, rt):
    WH = D // C
    HB = D // R
    hops = R // 2
    vm = pl.BlockSpec(memory_space=pltpu.VMEM)
    hbm = pl.BlockSpec(memory_space=pl.ANY)
    sem = pltpu.SemaphoreType.DMA
    heads = WH // HEAD_DIM
    return pl.pallas_call(
        functools.partial(front_kernel, R, C, E, SPLIT),
        name="front",
        out_shape=(
            jax.ShapeDtypeStruct((C, R, 2, HB, D), BF16),
            jax.ShapeDtypeStruct((C, ROWS, D), BF16),
            jax.ShapeDtypeStruct((C, ROWS, D), BF16),
            jax.ShapeDtypeStruct((C, MICRO, 16, BLK), F32),
            jax.ShapeDtypeStruct((ROWS, D), BF16),
            jax.ShapeDtypeStruct((C, R, HB + SMALL, D), BF16),
            jax.ShapeDtypeStruct((C, ROWS, 3 * WH), BF16),
            jax.ShapeDtypeStruct((C, ROWS, WH), BF16),
            jax.ShapeDtypeStruct((C, IMAGES, heads, IMG, IMG), BF16),
            jax.ShapeDtypeStruct((ROWS, D), F32),
            jax.ShapeDtypeStruct((MICRO, 8, BLK), F32),
            jax.ShapeDtypeStruct((SMALL + 8, D), F32),
        ),
        in_specs=[vm] * 5,
        out_specs=(hbm,) * 10 + (vm, vm),
        scratch_shapes=[
            pltpu.VMEM(((IMAGES - 1) * SEQ + IMG + 1, D), F32),
            pltpu.VMEM((ROWS, D), BF16),
            pltpu.VMEM((ROWS, D), BF16),
            pltpu.VMEM((C, R, HB + SMALL, D), BF16),
            pltpu.VMEM((ROWS, D), F32),
            pltpu.VMEM((ROWS, D), BF16),
            pltpu.VMEM((D, D), BF16),
            pltpu.VMEM((MICRO, 16, BLK), F32),
            pltpu.VMEM((C, ROWS, 3 * WH), BF16),
            pltpu.VMEM((C, ROWS, WH), BF16),
            pltpu.VMEM((C, IMAGES, heads, IMG, IMG), BF16),
            pltpu.VMEM((ROWS, D), F32),
            sem((2, hops)), sem((2, hops)),
            sem((2, hops)), sem((2, hops)),
            sem((2, R)), sem((2, R)),
            sem((1,)), sem((1,)),
            sem((3,)), sem((3,)),
            sem((C, 2, hops)), sem((C, 2, hops)),
            sem((3,)), sem((3,)),
            sem((3, IMAGES)), sem((3, IMAGES)),
            sem((3,)), sem((3,)),
            sem((6 + IMAGES,)), sem((4, IMAGES)),
        ],
        compiler_params=pltpu.CompilerParams(
            collective_id=1, has_side_effects=True, vmem_limit_bytes=56 << 20
        ),
    )(tok, cot, pack, wexp, rt)

def reduce_event(parts, rbuf, sends, recvs, slot, step, r, c, pos, R):
    right, left = ring_at(pos + 1, R), ring_at(pos - 1, R)
    hops = R // 2
    to_right, to_left = ring_at(pos + hops - step, R), ring_at(pos - hops + step, R)
    for d, (dest, peer) in enumerate(((to_right, right), (to_left, left))):
        if step > 0:
            got = rbuf(d, step - 1)
            if step == 1:
                got, mine = got.at[d], parts.at[dest, d]
            else:
                mine = parts.at[dest]
            remote(got, got, sends.at[slot, d, step - 1], recvs.at[slot, d, step - 1], (peer, c)).wait_recv()
            mine[...] = (mine[...].astype(F32) + got[...].astype(F32)).astype(BF16)
        src, dst = parts.at[dest], rbuf(d, step)
        if step == 0:
            src, dst = src.at[d], dst.at[d]
        remote(src, dst, sends.at[slot, d, step], recvs.at[slot, d, step], (peer, c)).start()


def reduce_finish(parts, rbuf, sends, recvs, slot, r, c, pos, R):
    hops = R // 2
    total = parts[r].astype(F32)
    for d in range(2):
        got = rbuf(d, hops - 1)
        remote(got, got, sends.at[slot, d, hops - 1], recvs.at[slot, d, hops - 1], (r, c)).wait_recv()
        total = total + got[...].astype(F32)
    for d in range(2):
        for step in range(hops):
            src, dst = parts.at[r], rbuf(d, step)
            if step == 0:
                src, dst = src.at[d], dst.at[d]
            remote(src, dst, sends.at[slot, d, step], recvs.at[slot, d, step], (r, c)).wait_send()
    return total


def expert_kernel(
    R, C, CAP, SPLIT,
    e2_all, cot_all, info_all, wbuf, sm,
    ge_parts, mix_parts, mix_out, gg_all, dexp, raw, wfar, bias_out,
    wv, eb, gb, info, X, GR, RES, GE, act, gh, stage, rbuf, corebuf, mixd, fin, ggs,
    w_sem, eb_sem, loc, flow_s, flow_r, red_s, red_r, fin_s, fin_r, core_s, core_r, ge_s, ge_r, mx_s, mx_r, gg_s, gg_r,
):
    r, c = lax.axis_index("row"), lax.axis_index("col")
    pos = ring_place(r, R)
    hops = R // 2
    HB = D // R
    right, left = ring_at(pos + 1, R), ring_at(pos - 1, R)
    core, ypeer, diag = col_core(c), col_y(c), col_diag(c)
    greet([(right, c), (left, c), (r, core), (r, ypeer), (r, diag)])
    NB = C * MICRO
    TR = NB * CAP

    def from_front(k):
        f = col_at(c, k)
        return lambda o: wbuf.at[f, o]

    def far_buf(k):
        return lambda o: wfar.at[k - 2, o]

    def gather(k, s):
        if s >= SPLIT[k]:
            ring_event(
                far_buf(k), flow_s, flow_r, k - 2, s, r, c, pos, R, from_front(k), SPLIT[k]
            )

    def more(k, s):
        if s > SPLIT[k]:
            gather(k, s)

    def weights(k):
        if k < 2:
            return [pltpu.make_async_copy(wbuf.at[col_at(c, k)], wv.at[k], w_sem.at[k, 0])]
        cps = []
        origins = [(r, 0)]
        for s in range(1, hops):
            origins += [(ring_at(pos - s, R), s), (ring_at(pos + s, R), s)]
        origins.append((ring_at(pos + hops, R), hops))
        for n, (o, s) in enumerate(origins):
            src = from_front(k)(o) if s <= SPLIT[k] else far_buf(k)(o)
            cps.append(pltpu.make_async_copy(src, wv.at[k - 2, o], w_sem.at[k, n]))
        return cps

    pending = {k: weights(k) for k in range(2)}
    for cp in pending[0] + pending[1]:
        cp.start()
    get_info = pltpu.make_async_copy(info_all, info, loc.at[0])
    get_info.start()
    gather(2, SPLIT[2])

    def place(p):
        return col_at(c, C - 1 - lax.div(p, MICRO)), lax.rem(p, MICRO)

    def fetch(p, slot, which):
        s, h = place(p)
        src, dst = (e2_all, eb) if which == 0 else (cot_all, gb)
        return pltpu.make_async_copy(
            src.at[s, pl.ds(pl.multiple_of(h * BLK, 16), BLK)], dst.at[slot], eb_sem.at[which, slot]
        )

    slot_id = lax.broadcasted_iota(jnp.int32, (CAP, BLK), 0).astype(F32)

    def pick(p):
        s, h = place(p)
        code = info[s, h, pl.ds(c, 1), :]
        gate = info[s, h, pl.ds(8 + c, 1), :]
        hot = jnp.where(slot_id == code, 1.0, 0.0)
        gate_slot = jnp.sum(hot * gate, axis=1, keepdims=True)
        return hot, gate_slot

    fetch(0, 0, 0).start()
    fetch(0, 0, 1).start()
    get_info.wait()

    def dispatch(p, bias):
        slot = lax.rem(p, 2)

        @pl.when(p + 1 < NB)
        def _():
            fetch(p + 1, 1 - slot, 0).start()
            fetch(p + 1, 1 - slot, 1).start()

        fetch(p, slot, 0).wait()
        fetch(p, slot, 1).wait()
        hot, gate_slot = pick(p)
        hot = hot.astype(BF16)
        rows = pl.ds(pl.multiple_of(p * CAP, 16), CAP)
        X[rows, :] = dot_nn(hot, eb[slot]).astype(BF16)
        g16 = (gate_slot * dot_nn(hot, gb[slot])).astype(BF16)
        GR[rows, :] = g16
        return bias + jnp.sum(g16.astype(F32), axis=0, keepdims=True)

    bias_out[...] = jnp.zeros_like(bias_out)
    out_bias = lax.fori_loop(0, NB // 2, dispatch, jnp.zeros((1, D), F32))
    gather(3, 0)
    bias_out[0:1, :] = lax.fori_loop(NB // 2, NB, dispatch, out_bias)
    more(2, 2)

    def red(k, step):
        reduce_event(stage.at[k], lambda d, s: rbuf.at[k, d, s], red_s, red_r, k, step, r, c, pos, R)

    def red_end(k):
        total = reduce_finish(stage.at[k], lambda d, s: rbuf.at[k, d, s], red_s, red_r, k, r, c, pos, R)
        fin[k] = total.astype(BF16)
        if k == 0:
            cp = pltpu.make_async_copy(fin.at[0], dexp.at[c], loc.at[1])
        else:
            cp = remote(fin.at[1], dexp.at[c], fin_s.at[0], fin_r.at[0], (r, core))
        cp.start()
        return cp

    MT = 512
    DT = D // 2
    HALFR = TR // 2

    def ffn(k, at, n):
        f = col_at(c, k)
        b1 = sm[pl.ds(9 + f, 1), :]
        slot = k % 2

        def tile(m, bias):
            rows = pl.ds(pl.multiple_of(at + m * MT, 16), MT)
            win = wv[slot, :, 0].reshape(D, D)
            wout = wv[slot, :, 1].reshape(D, D)
            hid = dot_nn(X[rows, :], win) + b1
            cdf = 0.5 * (1.0 + lax.erf(hid * (2.0 ** -0.5)))
            a16 = (hid * cdf).astype(BF16)
            act[slot, rows, :] = a16
            slope = cdf + hid * (jnp.exp(-0.5 * hid * hid) * ((2.0 * math.pi) ** -0.5))
            ga = dot_nn(GR[rows, :], wout)
            g16 = (ga * slope).astype(BF16)
            gh[slot, rows, :] = g16
            res = dot_nt(a16, wout)
            gen = dot_nt(g16, win)
            if k == 0:
                RES[rows, :] = res
                GE[rows, :] = gen
            else:
                RES[rows, :] = RES[rows, :] + res
                GE[rows, :] = GE[rows, :] + gen
            return bias + jnp.sum(g16.astype(F32), axis=0, keepdims=True)

        bsum = lax.fori_loop(0, n // MT, tile, jnp.zeros((1, D), F32))
        bias_out[pl.ds(1 + f, 1), :] = bias_out[pl.ds(1 + f, 1), :] + bsum

    def weight_grads(k, first, last):
        slot = k % 2

        def tile(j, _):
            cols = pl.ds(pl.multiple_of(j * DT, 128), DT)
            blocks = pl.ds(j * (R // 2), R // 2)
            stage[k, blocks, 0] = dot_tn(X[:, cols], gh[slot]).astype(BF16).reshape(R // 2, HB, D)
            stage[k, blocks, 1] = dot_tn(GR[:, cols], act[slot]).astype(BF16).reshape(R // 2, HB, D)
            return 0

        lax.fori_loop(first, last, tile, 0)

    order = [diag, ypeer, core, c]
    b2 = sm[8:9, :]
    sends = []

    def give_back(o):
        for h in range(MICRO):
            n = o * MICRO + h
            slot = n % 2
            if n + 1 < NB:
                fetch(n + 1, 1 - slot, 1).start()
            fetch(n, slot, 1).wait()
            if o == 0:
                ge_blk, mx_blk = eb.at[h], mixd.at[h]
            elif o == 1:
                ge_blk, mx_blk = corebuf.at[0, h], corebuf.at[1, h]
            else:
                at = pl.ds((o - 2) * MICRO * BLK + h * BLK, BLK)
                ge_blk, mx_blk = X.at[at], GR.at[at]
            hot, gate_slot = pick(n)
            hot_t = hot.T.astype(BF16)
            rows = slice(n * CAP, (n + 1) * CAP)
            res = (RES[rows, :] + b2).astype(BF16).astype(F32)
            g = dot_nn(hot.astype(BF16), gb[slot])
            gg = jnp.sum(g * res, axis=1, keepdims=True)
            gg_row = jnp.sum(hot * gg, axis=0, keepdims=True)
            mine = lax.broadcasted_iota(jnp.int32, (8, BLK), 0) == c
            ggs[o, h] = jnp.where(mine, gg_row, 0.0)
            ge = dot_nn(hot_t, GE[rows, :].astype(BF16))
            mx = dot_nn(hot_t, (gate_slot * res).astype(BF16))
            part = pl.ds(h * BLK, BLK)
            if o == 1:
                for t in range(2):
                    cb = corebuf.at[t, h]
                    remote(cb, cb, core_s.at[t, h], core_r.at[t, h], (r, core)).wait_recv()
                ge = ge + corebuf[0, h].astype(F32)
                mx = mx + corebuf[1, h].astype(F32)
            ge_blk[...] = ge.astype(BF16)
            mx_blk[...] = mx.astype(BF16)
            if o == 0:
                cps = [
                    remote(ge_blk, corebuf.at[0, h], core_s.at[0, h], core_r.at[0, h], (r, core)),
                    remote(mx_blk, corebuf.at[1, h], core_s.at[1, h], core_r.at[1, h], (r, core)),
                ]
            elif o == 1:
                cps = [
                    remote(ge_blk, ge_parts.at[2, part], ge_s.at[1, h], ge_r.at[1, h], (r, ypeer)),
                    pltpu.make_async_copy(mx_blk, mix_out.at[part], loc.at[4 + h]),
                ]
            elif o == 2:
                cps = [
                    remote(ge_blk, ge_parts.at[1, part], ge_s.at[0, h], ge_r.at[0, h], (r, core)),
                    remote(mx_blk, mix_parts.at[1, part], mx_s.at[h], mx_r.at[h], (r, core)),
                ]
            else:
                cps = [
                    pltpu.make_async_copy(ge_blk, ge_parts.at[0, part], loc.at[6 + h]),
                    pltpu.make_async_copy(mx_blk, mix_parts.at[0, part], loc.at[8 + h]),
                ]
            for cp in cps:
                cp.start()
            sends.append((o, cps))
        if o < 3:
            cp = remote(ggs.at[o], gg_all.at[c], gg_s.at[o], gg_r.at[o], (r, order[o]))
        else:
            cp = pltpu.make_async_copy(ggs.at[3], gg_all.at[c], loc.at[10])
        cp.start()
        sends.append((4 if o < 3 else 5, [cp]))

    def load(k):
        for cp in weights(k):
            cp.start()

    def loaded(k):
        for cp in weights(k):
            cp.wait()

    loaded(0)
    ffn(0, 0, HALFR)
    gather(3, 1)
    ffn(0, HALFR, HALFR)
    weight_grads(0, 0, 2)
    more(2, 3)
    loaded(1)
    ffn(1, 0, HALFR)
    gather(3, 2)
    ring_finish(far_buf(2), flow_s, flow_r, 0, r, c, pos, R, SPLIT[2], hops)
    load(2)
    ffn(1, HALFR, HALFR)
    weight_grads(1, 0, 1)
    gather(3, 3)
    weight_grads(1, 1, 2)
    red(0, 0)
    loaded(2)
    fetch(0, 0, 1).start()
    ffn(2, 0, HALFR)
    ring_finish(far_buf(3), flow_s, flow_r, 1, r, c, pos, R, SPLIT[3], hops)
    load(3)
    red(0, 1)
    red(1, 0)
    loaded(3)
    ffn(3, 0, HALFR)
    red(0, 2)
    give_back(0)
    give_back(1)
    red(1, 1)
    ffn(2, HALFR, HALFR)
    red(0, 3)
    ffn(3, HALFR, HALFR)
    red(1, 2)
    weight_grads(2, 0, 2)
    end0 = red_end(0)
    red(1, 3)
    raws = [pltpu.make_async_copy(stage.at[2], raw.at[0], loc.at[2])]
    raws[0].start()
    weight_grads(3, 0, 2)
    raws.append(pltpu.make_async_copy(stage.at[3], raw.at[1], loc.at[3]))
    raws[1].start()
    give_back(2)
    give_back(3)
    end1 = red_end(1)

    for o, cps in sends:
        for t, cp in enumerate(cps):
            if o == 3 or o == 5 or (o == 1 and t == 1):
                cp.wait()
            else:
                cp.wait_send()
    for h in range(MICRO):
        part = pl.ds(h * BLK, BLK)
        for n2, slot2 in enumerate((1, 2)):
            g_ref = ge_parts.at[slot2, part]
            remote(g_ref, g_ref, ge_s.at[n2, h], ge_r.at[n2, h], (r, core)).wait_recv()
        m_ref = mix_parts.at[1, part]
        remote(m_ref, m_ref, mx_s.at[h], mx_r.at[h], (r, core)).wait_recv()
    for o, peer in enumerate((diag, ypeer, core)):
        g_ref = gg_all.at[peer]
        remote(g_ref, g_ref, gg_s.at[o], gg_r.at[o], (r, peer)).wait_recv()
    end0.wait()
    end1.wait_send()
    d_ref = dexp.at[core]
    remote(d_ref, d_ref, fin_s.at[0], fin_r.at[0], (r, core)).wait_recv()
    for cp in raws:
        cp.wait()


def expert(R, C, CAP, SPLIT, e2_all, cot_all, info_all, wbuf, sm):
    HB = D // R
    hops = R // 2
    TR = C * MICRO * CAP
    vm = pl.BlockSpec(memory_space=pltpu.VMEM)
    hbm = pl.BlockSpec(memory_space=pl.ANY)
    sem = pltpu.SemaphoreType.DMA
    return pl.pallas_call(
        functools.partial(expert_kernel, R, C, CAP, SPLIT),
        name="expert",
        out_shape=(
            jax.ShapeDtypeStruct((3, ROWS, D), BF16),
            jax.ShapeDtypeStruct((2, ROWS, D), BF16),
            jax.ShapeDtypeStruct((ROWS, D), BF16),
            jax.ShapeDtypeStruct((C, MICRO, 8, BLK), F32),
            jax.ShapeDtypeStruct((C, 2, HB, D), BF16),
            jax.ShapeDtypeStruct((2, R, 2, HB, D), BF16),
            jax.ShapeDtypeStruct((2, R, 2, HB, D), BF16),
            jax.ShapeDtypeStruct((8, D), F32),
        ),
        in_specs=[hbm, hbm, hbm, hbm, vm],
        out_specs=(hbm, hbm, hbm, hbm, hbm, hbm, hbm, vm),
        scratch_shapes=[
            pltpu.VMEM((2, R, 2, HB, D), BF16),
            pltpu.VMEM((2, BLK, D), BF16),
            pltpu.VMEM((2, BLK, D), BF16),
            pltpu.VMEM((C, MICRO, 16, BLK), F32),
            pltpu.VMEM((TR, D), BF16),
            pltpu.VMEM((TR, D), BF16),
            pltpu.VMEM((TR, D), F32),
            pltpu.VMEM((TR, D), F32),
            pltpu.VMEM((2, TR, D), BF16),
            pltpu.VMEM((2, TR, D), BF16),
            pltpu.VMEM((C, R, 2, HB, D), BF16),
            pltpu.VMEM((2, 2, hops, 2, HB, D), BF16),
            pltpu.VMEM((2, MICRO, BLK, D), BF16),
            pltpu.VMEM((MICRO, BLK, D), BF16),
            pltpu.VMEM((2, 2, HB, D), BF16),
            pltpu.VMEM((C, MICRO, 8, BLK), F32),
            sem((C, R)), sem((2, 2)), sem((11,)),
            sem((2, 2, hops)), sem((2, 2, hops)),
            sem((2, 2, hops)), sem((2, 2, hops)),
            sem((1,)), sem((1,)),
            sem((2, MICRO)), sem((2, MICRO)),
            sem((2, MICRO)), sem((2, MICRO)),
            sem((MICRO,)), sem((MICRO,)),
            sem((3,)), sem((3,)),
        ],
        compiler_params=pltpu.CompilerParams(
            collective_id=2, has_side_effects=True, vmem_limit_bytes=62 << 20
        ),
    )(e2_all, cot_all, info_all, wbuf, sm)

def back_kernel(
    R, C, E,
    tok, cot_all, ge_parts, mix_parts, mix_out, gg, rprob, resid_in, qkv_in, mixed_in, probs_in, wg_in, sm, raw, bias_in,
    out, input_grad, attn_grad, dexp, sums, mixy,
    cot, wg, gp, resid, qkv, mixed, probs, stage, rbuf, wp, gbr, dres, gm, e1t, dz, ge1, gblk, corein, yin, apart, abuf, early, late, sbuf, cbuf, rbuf2,
    loc, red_s, red_r, fin_s, fin_r, mix_s, mix_r, ag_s, ag_r, ar_s, ar_r, sm_s, sm_r, lc_s, lc_r, lr_s, lr_r,
):
    r, c = lax.axis_index("row"), lax.axis_index("col")
    pos = ring_place(r, R)
    hops = R // 2
    HB = D // R
    WH = D // C
    W3 = 3 * WH
    heads = WH // HEAD_DIM
    right, left = ring_at(pos + 1, R), ring_at(pos - 1, R)
    core, ypeer, diag = col_core(c), col_y(c), col_diag(c)

    copies = [
        pltpu.make_async_copy(raw, stage, loc.at[0]),
        pltpu.make_async_copy(ge_parts, gp, loc.at[1]),
        pltpu.make_async_copy(resid_in, resid, loc.at[4]),
        pltpu.make_async_copy(cot_all.at[c], cot, loc.at[8]),
        pltpu.make_async_copy(wg_in.at[:, :, pl.ds(0, HB)], wg, loc.at[2]),
    ]
    later = [
        pltpu.make_async_copy(mixed_in, mixed, loc.at[5]),
        pltpu.make_async_copy(qkv_in, qkv, loc.at[6]),
        pltpu.make_async_copy(probs_in, probs, loc.at[7]),
    ]
    for cp in copies:
        cp.start()
    pairs = [(r, core), (r, ypeer)]
    step_bit = 1
    while step_bit < R:
        bit = lax.rem(lax.div(r, step_bit), 2)
        pairs.append((r + step_bit - 2 * step_bit * bit, c))
        step_bit *= 2
    others = [(lax.rem(r + n, R), c) for n in range(1, R)]
    greet([(r, core), (r, ypeer), (r, diag)] + others)

    send_mix = remote(mix_out, mixy, mix_s.at[0], mix_r.at[0], (r, ypeer))
    send_mix.start()
    copies[0].wait()

    def red(k, step):
        reduce_event(stage.at[k], lambda d, s: rbuf.at[k, d, s], red_s, red_r, k, step, r, c, pos, R)

    red(0, 0)
    red(1, 0)
    for cp in copies[1:]:
        cp.wait()
    for cp in later:
        cp.start()
    gain1, shift1 = sm[0:1], sm[1:2]
    gain2, shift2 = sm[2:3], sm[3:4]
    router_b = sm[SMALL : SMALL + 8].astype(BF16)
    router3 = jnp.concatenate([router_b, router_b, router_b], axis=0)
    for g in range(C):
        wp[:, g * WH : (g + 1) * WH] = wg[g, :, :, W3:].reshape(D, WH)
    early[...] = jnp.zeros_like(early)
    late[...] = jnp.zeros_like(late)
    early[16:24, :] = bias_in[...]

    def pair(n):
        size = 16 if n < 2 else 24
        return remote(early.at[pl.ds(0, size)], sbuf.at[n, pl.ds(0, size)], sm_s.at[n], sm_r.at[n], pairs[n])

    def paired(n):
        size = 16 if n < 2 else 24
        pair(n).wait()
        early[0:size, :] = early[0:size, :] + sbuf[n, 0:size, :]
        if n + 1 < len(pairs):
            pair(n + 1).start()


    for h in range(MICRO):
        rp = rprob[h]
        p = gg[0, h]
        for e in range(1, E):
            p = p + gg[e, h]
        gl = rp * (p - jnp.sum(rp * p, axis=0, keepdims=True))
        hi = gl.astype(BF16)
        rest = gl - hi.astype(F32)
        mid = rest.astype(BF16)
        low = (rest - mid.astype(F32)).astype(BF16)
        gl3 = jnp.concatenate([hi.astype(F32), mid.astype(F32), low.astype(F32)], axis=0)
        gl3_t = gl3.T.astype(BF16)
        gl3 = gl3.astype(BF16)
        drt = jnp.zeros((24, D), F32)
        vecs = [jnp.zeros((1, D), F32) for _ in range(3)]
        for i in range(IMG_MB):
            at = h * BLK + i * IMG
            rows = slice(at, at + IMG)
            n2, inv2 = norm_rows(resid[rows, :])
            e2 = (n2 * gain2 + shift2).astype(BF16)
            drt = drt + dot_nn(gl3[:, i * IMG : (i + 1) * IMG], e2)
            ge2 = gp[0, rows, :].astype(F32) + gp[1, rows, :].astype(F32) + gp[2, rows, :].astype(F32)
            ge2 = ge2 + dot_nn(gl3_t[i * IMG : (i + 1) * IMG], router3)
            b = ge2 * gain2
            inner = b - jnp.mean(b, axis=-1, keepdims=True) - n2 * jnp.mean(b * n2, axis=-1, keepdims=True)
            gr = cot[rows, :].astype(F32) + inv2 * inner
            dres[rows, :] = gr
            g16 = gr.astype(BF16)
            gbr[rows, :] = g16
            vecs[0] = vecs[0] + jnp.sum(ge2 * n2, axis=0, keepdims=True)
            vecs[1] = vecs[1] + jnp.sum(ge2, axis=0, keepdims=True)
            vecs[2] = vecs[2] + jnp.sum(g16.astype(F32), axis=0, keepdims=True)
            for g in range(C):
                gm[g, rows, :] = dot_nt(g16, wp[g * WH : (g + 1) * WH, :]).astype(BF16)
            n1, _u = norm_rows(tok[rows, :].astype(F32))
            e1 = n1 * gain1 + shift1
            e1t[h * IMG_MB + i] = e1.T.astype(BF16)
        for n in range(3):
            early[n : n + 1, :] = early[n : n + 1, :] + vecs[n]
        early[8:16, :] = early[8:16, :] + drt[0:8] + drt[8:16] + drt[16:24]
        if h == 1:
            red(0, 1)
    get_mix = pltpu.make_async_copy(mix_parts, gp.at[pl.ds(0, 2)], loc.at[3])
    get_mix.start()
    pair(0).start()
    red(1, 1)
    for cp in later:
        cp.wait()
    for g in range(C):
        dp = dot_tn(mixed[g], gbr[...]).astype(BF16)
        for g2 in range(C):
            gblk[g2, g * WH : (g + 1) * WH, W3:] = dp[:, g2 * WH : (g2 + 1) * WH]

    order = [diag, ypeer, core, c]
    sends = []

    def close(k, peer):
        stage[k, r] = reduce_finish(
            stage.at[k], lambda d, s: rbuf.at[k, d, s], red_s, red_r, k, r, c, pos, R
        ).astype(BF16)
        cp = remote(stage.at[k, r], dexp.at[c], fin_s.at[k], fin_r.at[k], (r, peer))
        cp.start()
        sends.append(cp)

    for o in range(C):
        g = order[o]

        def image(i, vec, g=g):
            rows = pl.ds(pl.multiple_of(i * IMG, 16), IMG)
            z = qkv[g, rows, :]
            gmv = gm[g, rows, :]
            dq, dk, dv = [], [], []
            for h in range(heads):
                q = z[:, h * HEAD_DIM : (h + 1) * HEAD_DIM]
                kk = z[:, WH + h * HEAD_DIM : WH + (h + 1) * HEAD_DIM]
                v = z[:, 2 * WH + h * HEAD_DIM : 2 * WH + (h + 1) * HEAD_DIM]
                gmh = gmv[:, h * HEAD_DIM : (h + 1) * HEAD_DIM]
                p16 = probs[g, i, h]
                p = p16.astype(F32)
                w = dot_nt(gmh, v)
                ds = (p * (w - jnp.sum(p * w, axis=-1, keepdims=True))).astype(BF16)
                dq.append(dot_nn(ds, kk))
                dk.append(dot_tn(ds, q))
                dv.append(dot_tn(p16, gmh))
            d = jnp.concatenate(
                [v.astype(BF16).astype(F32) * SCALE for v in dq] + [v.astype(BF16).astype(F32) for v in dk + dv],
                axis=1,
            )
            dz[rows, :] = d.astype(BF16)
            w = wg[g, :, :, 0:W3].reshape(D, W3)
            part = dot_nt(d.astype(BF16), w)
            ge1[rows, :] = part if o == 0 else ge1[rows, :] + part
            return vec + jnp.sum(d, axis=0, keepdims=True)

        vec = lax.fori_loop(0, IMAGES, image, jnp.zeros((1, W3), F32))
        late[pl.ds(2 + g, 1), 0:W3] = vec
        for j in range(2):
            half = slice(j * (D // 2), (j + 1) * (D // 2))
            acc = jnp.zeros((D // 2, W3), F32)
            for i in range(IMAGES):
                acc = acc + dot_nn(e1t[i, half, :], dz[i * IMG : (i + 1) * IMG, :])
            gblk[g, half, 0:W3] = acc.astype(BF16)
        blk = gblk.at[g]
        if o == 0:
            cp = remote(blk, corein.at[0], ag_s.at[0], ag_r.at[0], (r, core))
            cp.start()
            sends.append(cp)
        elif o == 1:
            remote(blk, corein.at[0], ag_s.at[0], ag_r.at[0], (r, core)).wait_recv()
            blk[...] = (blk[...].astype(F32) + corein[0].astype(F32)).astype(BF16)
            cp = remote(blk, yin, ag_s.at[1], ag_r.at[1], (r, ypeer))
            cp.start()
            sends.append(cp)
        elif o == 2:
            cp = remote(blk, corein.at[1], ag_s.at[2], ag_r.at[2], (r, core))
            cp.start()
            sends.append(cp)
        paired(o)
        if o == 1:
            red(0, 2)
        elif o == 2:
            red(1, 2)
        elif o == 3:
            red(0, 3)
            red(1, 3)
            close(0, ypeer)
            close(1, diag)

    remote(gblk.at[c], corein.at[1], ag_s.at[2], ag_r.at[2], (r, core)).wait_recv()
    remote(gblk.at[c], yin, ag_s.at[1], ag_r.at[1], (r, ypeer)).wait_recv()
    for o in range(R):
        rows = slice(o * HB, (o + 1) * HB)
        tot = gblk[c, rows, :].astype(F32) + corein[1, rows, :].astype(F32) + yin[rows, :].astype(F32)
        apart[o, 0] = tot[0 : HB // 2].astype(BF16)
        apart[o, 1] = tot[HB // 2 :].astype(BF16)

    def ring(step):
        reduce_event(apart, lambda d, s: abuf.at[d, s], ar_s, ar_r, 0, step, r, c, pos, R)

    ring(0)

    def tight(dst, src):
        even = dst.shape[0] // 16 * 16
        dst[0:even, :] = src[0:even, :].astype(BF16)
        dst[even : dst.shape[0], :] = src[even : dst.shape[0], :].astype(BF16)

    dg = jnp.zeros((1, D), F32)
    dsh = jnp.zeros((1, D), F32)
    for i in range(IMAGES):
        rows = slice(i * IMG, (i + 1) * IMG)
        n1, inv1 = norm_rows(tok[rows, :].astype(F32))
        a = ge1[rows, :]
        b = a * gain1
        inner = b - jnp.mean(b, axis=-1, keepdims=True) - n1 * jnp.mean(b * n1, axis=-1, keepdims=True)
        full = dres[rows, :] + inv1 * inner
        dres[i * SEQ : (i + 1) * SEQ, :] = full[:SEQ]
        dg = dg + jnp.sum(a * n1, axis=0, keepdims=True)
        dsh = dsh + jnp.sum(a, axis=0, keepdims=True)
    tight(input_grad, dres)
    late[0:1, :] = dg
    late[1:2, :] = dsh
    cbuf[c] = late[...]
    firsts = [
        remote(late, cbuf.at[c], lc_s.at[n], lc_r.at[n], (r, peer)) for n, peer in enumerate((core, ypeer, diag))
    ]
    for cp in firsts:
        cp.start()
    for n in range(len(order), len(pairs)):
        paired(n)
    sums[0:24, :] = early[...]
    ring(1)
    for cp in firsts:
        cp.wait()
    tot = cbuf[0]
    for n in range(1, C):
        tot = tot + cbuf[n]
    late[...] = tot
    rbuf2[r] = tot
    seconds = [
        remote(late, rbuf2.at[r], lr_s.at[n], lr_r.at[n], peer) for n, peer in enumerate(others)
    ]
    for cp in seconds:
        cp.start()

    send_mix.wait()
    get_far = pltpu.make_async_copy(mixy, gp.at[2], loc.at[1])
    get_far.start()
    get_mix.wait()
    get_far.wait()
    for i in range(IMAGES):
        rows = slice(i * IMG, (i + 1) * IMG)
        o = resid[rows, :] + gp[0, rows, :].astype(F32) + gp[1, rows, :].astype(F32) + gp[2, rows, :].astype(F32)
        resid[i * SEQ : (i + 1) * SEQ, :] = o[:SEQ]
    tight(out, resid)
    ring(2)
    for cp in seconds:
        cp.wait()
    tot = rbuf2[0]
    for n in range(1, R):
        tot = tot + rbuf2[n]
    sums[24:32, :] = tot
    ring(3)

    total = reduce_finish(apart, lambda d, s: abuf.at[d, s], ar_s, ar_r, 0, r, c, pos, R)
    attn_grad[...] = total.reshape(HB, D)
    for cp in sends:
        cp.wait_send()
    for k, peer in enumerate((ypeer, diag)):
        d_ref = dexp.at[peer]
        remote(d_ref, d_ref, fin_s.at[k], fin_r.at[k], (r, peer)).wait_recv()


def back(R, C, E, tok, cot, ge_parts, mix_parts, mix_out, gg, rprob, resid, qkv, mixed, probs, wg, sm, raw, bias):
    HB = D // R
    WH = D // C
    hops = R // 2
    vm = pl.BlockSpec(memory_space=pltpu.VMEM)
    hbm = pl.BlockSpec(memory_space=pl.ANY)
    sem = pltpu.SemaphoreType.DMA
    steps = 2 + int(math.log2(R))
    heads = WH // HEAD_DIM
    return pl.pallas_call(
        functools.partial(back_kernel, R, C, E),
        name="back",
        out_shape=(
            jax.ShapeDtypeStruct((IMAGES * SEQ, D), BF16),
            jax.ShapeDtypeStruct((IMAGES * SEQ, D), BF16),
            jax.ShapeDtypeStruct((HB, D), F32),
            jax.ShapeDtypeStruct((C, 2, HB, D), BF16),
            jax.ShapeDtypeStruct((32, D), F32),
            jax.ShapeDtypeStruct((ROWS, D), BF16),
        ),
        in_specs=[vm, hbm, hbm, hbm, hbm, vm, vm, hbm, hbm, hbm, hbm, hbm, vm, hbm, vm],
        out_specs=(vm, vm, vm, hbm, vm, hbm),
        scratch_shapes=[
            pltpu.VMEM((ROWS, D), BF16),
            pltpu.VMEM((C, R, HB, D), BF16),
            pltpu.VMEM((3, ROWS, D), BF16),
            pltpu.VMEM((ROWS, D), F32),
            pltpu.VMEM((C, ROWS, 3 * WH), BF16),
            pltpu.VMEM((C, ROWS, WH), BF16),
            pltpu.VMEM((C, IMAGES, heads, IMG, IMG), BF16),
            pltpu.VMEM((2, R, 2, HB, D), BF16),
            pltpu.VMEM((2, 2, hops, 2, HB, D), BF16),
            pltpu.VMEM((D, D), BF16),
            pltpu.VMEM((ROWS, D), BF16),
            pltpu.VMEM((ROWS, D), F32),
            pltpu.VMEM((C, ROWS, WH), BF16),
            pltpu.VMEM((IMAGES, D, IMG), BF16),
            pltpu.VMEM((ROWS, 3 * WH), BF16),
            pltpu.VMEM((ROWS, D), F32),
            pltpu.VMEM((C, D, D), BF16),
            pltpu.VMEM((2, D, D), BF16),
            pltpu.VMEM((D, D), BF16),
            pltpu.VMEM((R, 2, HB // 2, D), BF16),
            pltpu.VMEM((2, hops, 2, HB // 2, D), BF16),
            pltpu.VMEM((24, D), F32),
            pltpu.VMEM((8, D), F32),
            pltpu.VMEM((steps, 24, D), F32),
            pltpu.VMEM((C, 8, D), F32),
            pltpu.VMEM((R, 8, D), F32),
            sem((9,)),
            sem((2, 2, hops)), sem((2, 2, hops)),
            sem((2,)), sem((2,)),
            sem((1,)), sem((1,)),
            sem((3,)), sem((3,)),
            sem((1, 2, hops)), sem((1, 2, hops)),
            sem((steps,)), sem((steps,)),
            sem((C - 1,)), sem((C - 1,)),
            sem((R - 1,)), sem((R - 1,)),
        ],
        compiler_params=pltpu.CompilerParams(
            collective_id=3, has_side_effects=True, vmem_limit_bytes=62 << 20
        ),
    )(tok, cot, ge_parts, mix_parts, mix_out, gg, rprob, resid, qkv, mixed, probs, wg, sm, raw, bias)

def spread(v, at, n):
    wide = jnp.tile(v, (1, n))
    piece = lax.broadcasted_iota(jnp.int32, wide.shape, 1) // v.shape[1]
    return jnp.where(piece == at, wide, jnp.zeros_like(wide))


def prepare(R, C, tokens, cotangent, routes, norm1_gain, norm1_shift, attn_in, attn_bias, attn_proj,
            proj_bias, norm2_gain, norm2_shift, router, expert_in, expert_in_bias, expert_out, expert_out_bias):
    r = lax.axis_index("row")
    HB, WH = D // R, D // C
    norms = spread(jnp.stack([norm1_gain, norm1_shift, norm2_gain, norm2_shift]), r, R)
    thin = jnp.pad(jnp.concatenate([attn_bias, proj_bias[None]], axis=0), ((0, 0), (0, D - WH)))
    owned = spread(jnp.concatenate([router.T, expert_out_bias], axis=0), r, R)
    ff_rows = expert_in_bias.shape[1] * R // D
    inner = spread(expert_in_bias, r, R).reshape(ff_rows, D)
    smalls = jnp.concatenate([norms, thin, owned, inner], axis=0)
    smalls = jnp.pad(smalls, ((0, SMALL - smalls.shape[0]), (0, 0)))
    pack = jnp.concatenate([jnp.concatenate([attn_in.reshape(HB, 3 * WH), attn_proj], axis=1), smalls], axis=0)
    wexp = jnp.stack([expert_in, jnp.swapaxes(expert_out, 1, 2)], axis=1)
    named = routes.astype(F32).T.reshape(2, IMAGES, SEQ)
    named = jnp.pad(named, ((0, 6), (0, 0), (0, IMG - SEQ)), constant_values=-1.0)
    rt = jnp.swapaxes(named.reshape(8, MICRO, BLK), 0, 1)
    return pack, wexp, rt

SPLIT = (4, 4, 1, 0)


def rings(
    tokens, cotangent, routes, norm1_gain, norm1_shift, attn_in, attn_bias, attn_proj, proj_bias,
    norm2_gain, norm2_shift, router, expert_in, expert_in_bias, expert_out, expert_out_bias,
):
    R, C = lax.axis_size("row"), lax.axis_size("col")
    E = expert_in.shape[0]
    HB, WH = D // R, D // C
    W3 = 3 * WH
    rows_mb = IMG_MB * SEQ
    cap = (2 * rows_mb * 13 // (10 * E) + 7) // 8 * 8
    cap = (cap + 15) // 16 * 16
    pack, wexp, rt = prepare(
        R, C, tokens, cotangent, routes, norm1_gain, norm1_shift, attn_in, attn_bias, attn_proj, proj_bias,
        norm2_gain, norm2_shift, router, expert_in, expert_in_bias, expert_out, expert_out_bias,
    )
    wbuf, e2_all, cot_all, info_all, tok, wg, qkv, mixed, probs, resid, rprob, sm = front(
        R, C, E, SPLIT, tokens, cotangent, pack, wexp, rt
    )
    ge_parts, mix_parts, mix_out, gg, dexp_a, raw, _, bias = expert(
        R, C, cap, SPLIT, e2_all, cot_all, info_all, wbuf, sm
    )
    out, input_grad, attn_grad, dexp_b, sums, _ = back(
        R, C, E, tok, cot_all, ge_parts, mix_parts, mix_out, gg, rprob, resid, qkv, mixed, probs, wg, sm, raw, bias
    )
    r, c = lax.axis_index("row"), lax.axis_index("col")
    e = lax.broadcasted_iota(jnp.int32, (E, 1, 1, 1), 0)
    near = lax.div(e, 2) == lax.div(c, 2)
    dexp = jnp.where(near, dexp_a, dexp_b).astype(F32)
    norm1 = lax.dynamic_slice(sums, (24, r * HB), (2, HB))
    norm2 = lax.dynamic_slice(sums, (0, r * HB), (2, HB))
    grad_router = lax.dynamic_slice(sums, (8 + c, r * HB), (1, HB)).reshape(HB, 1)
    grad_pb = lax.dynamic_slice(sums, (2, c * WH), (1, WH)).reshape(WH)
    group = lax.dynamic_slice(sums, (26 + c, 0), (1, W3)).reshape(3, WH)
    grad_ab = jnp.stack([group[0], group[2]])
    grad_eob = lax.dynamic_slice(sums, (16, r * HB), (1, HB))
    ff = expert_in_bias.shape[1]
    grad_eib = lax.dynamic_slice(sums[17 : 17 + ff * R // D].reshape(1, ff * R), (0, r * ff), (1, ff))
    return (
        out,
        input_grad,
        norm1[0],
        norm1[1],
        attn_grad[:, :W3].reshape(HB, 3, WH),
        grad_ab,
        attn_grad[:, W3:],
        grad_pb,
        norm2[0],
        norm2[1],
        grad_router,
        dexp[:, 0],
        grad_eib,
        jnp.swapaxes(dexp[:, 1], 1, 2),
        grad_eob,
    )


def solution(mesh):
    in_specs = (
        P(("row", "col"), None),
        P(("row", "col"), None),
        P(("row", "col"), None),
        P("row"),
        P("row"),
        P("row", None, "col"),
        P(None, "col"),
        P("row", "col"),
        P("col"),
        P("row"),
        P("row"),
        P("row", "col"),
        P(None, "row", "col"),
        P("col", "row"),
        P(None, "col", "row"),
        P("col", "row"),
    )
    out_specs = (
        P(("row", "col"), None),
        P(("row", "col"), None),
        P("row"),
        P("row"),
        P("row", None, "col"),
        P(None, "col"),
        P("row", "col"),
        P("col"),
        P("row"),
        P("row"),
        P("row", "col"),
        P(None, "row", "col"),
        P("col", "row"),
        P(None, "col", "row"),
        P("col", "row"),
    )
    body = rings if (mesh.shape["row"], mesh.shape["col"]) == (8, 4) else shards
    return jax.shard_map(body, mesh=mesh, in_specs=in_specs, out_specs=out_specs, check_vma=False)
```

```python
import functools
import math

import jax
import jax.numpy as jnp
from jax import lax
from jax.experimental import pallas as pl
from jax.experimental.pallas import tpu as pltpu
from jax.sharding import PartitionSpec as P

D = 768
HEADS = 12
HEAD_DIM = 64
SEQ = 197
IMG_MB = 2
MICRO = 2
IMAGES = IMG_MB * MICRO
IMG = (SEQ + 15) // 16 * 16
BLK = IMG_MB * IMG
ROWS = IMAGES * IMG
SCALE = HEAD_DIM ** (-0.5)
SMALL = 16
epsilon = 1e-06

MESH = pl.DeviceIdType.MESH
F32 = jnp.float32
BF16 = jnp.bfloat16
NT = (((1,), (1,)), ((), ()))
TN = (((0,), (0,)), ((), ()))


def dot_nn(a, b):
    return jnp.dot(a, b, preferred_element_type=F32)


def dot_nt(a, b):
    return lax.dot_general(a, b, NT, preferred_element_type=F32)


def dot_tn(a, b):
    return lax.dot_general(a, b, TN, preferred_element_type=F32)


def norm_rows(vals):
    centred = vals - jnp.mean(vals, axis=-1, keepdims=True)
    inv_std = lax.rsqrt(jnp.mean(centred * centred, axis=-1, keepdims=True) + epsilon)
    return centred * inv_std, inv_std


def ring_place(r, R):
    half = lax.rem(r, 2)
    return lax.div(r, 2) * (1 - half) + half * (R - 1 - lax.div(r, 2))


def ring_at(p, R):
    p = lax.rem(p + 2 * R, R)
    back = lax.div(p, R // 2)
    return (1 - back) * (2 * p) + back * (2 * (R - 1 - p) + 1)


def col_core(c):
    return c + 1 - 2 * lax.rem(c, 2)


def col_y(c):
    return c + 2 - 4 * lax.div(c, 2)


def col_diag(c):
    return 3 - c


def col_at(c, k):
    low = lax.rem(lax.rem(c, 2) + lax.rem(k, 2), 2)
    high = lax.rem(lax.div(c, 2) + lax.div(k, 2), 2)
    return low + 2 * high


def remote(src, dst, send, recv, dev):
    return pltpu.make_async_remote_copy(
        src_ref=src, dst_ref=dst, send_sem=send, recv_sem=recv, device_id=dev, device_id_type=MESH
    )


def greet(devs):
    bar = pltpu.get_barrier_semaphore()
    for dev in devs:
        pl.semaphore_signal(bar, inc=1, device_id=dev, device_id_type=MESH)
    pl.semaphore_wait(bar, len(devs))

def norm_forward(row_vals, norm_gain, norm_shift):
    centred = row_vals - jnp.mean(row_vals, axis=-1, keepdims=True)
    inv_std = lax.rsqrt(jnp.mean(centred * centred, axis=-1, keepdims=True) + epsilon)
    normed = centred * inv_std
    return (normed * norm_gain + norm_shift, normed, inv_std)


def norm_backward(grad_rows, normed, inv_std, norm_gain):
    scaled = grad_rows * norm_gain
    inner = (
        scaled
        - jnp.mean(scaled, axis=-1, keepdims=True)
        - normed * jnp.mean(scaled * normed, axis=-1, keepdims=True)
    )
    return (inv_std * inner, jnp.sum(grad_rows * normed, axis=0), jnp.sum(grad_rows, axis=0))


def gelu_exact(values):
    return jax.nn.gelu(values, approximate=False)


def shards(
    tokens,
    cotangent,
    routes,
    norm1_gain,
    norm1_shift,
    attn_in,
    attn_bias,
    attn_proj,
    proj_bias,
    norm2_gain,
    norm2_shift,
    router,
    expert_in,
    expert_in_bias,
    expert_out,
    expert_out_bias,
):
    experts_all = expert_in.shape[0]
    rows_mb = IMG_MB * SEQ
    capacity = (2 * rows_mb * 13 // (10 * experts_all) + 7) // 8 * 8
    scaling = HEAD_DIM ** (-0.5)
    head_shape = (IMG_MB, SEQ, HEADS, HEAD_DIM)
    stacked = jnp.stack([jnp.swapaxes(expert_in, 1, 2), expert_out])
    owned_cols = lax.all_to_all(stacked, "col", split_axis=1, concat_axis=2, tiled=True)
    norm_pack = jnp.stack([norm1_gain, norm1_shift, norm2_gain, norm2_shift])
    qkv_rows, proj_rows, router_rows, norm_full, owned, first_bias, second_bias = (
        lax.all_gather(attn_in, "row", axis=0, tiled=True),
        lax.all_gather(attn_proj, "row", axis=0, tiled=True),
        lax.all_gather(router, "row", axis=0, tiled=True),
        lax.all_gather(norm_pack, "row", axis=1, tiled=True),
        lax.all_gather(owned_cols, "row", axis=3, tiled=True),
        lax.all_gather(expert_in_bias, "row", axis=1, tiled=True),
        lax.all_gather(expert_out_bias, "row", axis=1, tiled=True),
    )
    qkv_full, proj_full, router_full, qv_bias, out_bias_vec = (
        lax.all_gather(qkv_rows, "col", axis=2, tiled=True),
        lax.all_gather(proj_rows, "col", axis=1, tiled=True),
        lax.all_gather(router_rows, "col", axis=1, tiled=True),
        lax.all_gather(attn_bias, "col", axis=1, tiled=True),
        lax.all_gather(proj_bias, "col", axis=0, tiled=True),
    )
    norms_wide = norm_full.astype(jnp.float32)
    gain_one, shift_one, gain_two, shift_two = (
        norms_wide[0],
        norms_wide[1],
        norms_wide[2],
        norms_wide[3],
    )
    qv_bias_wide = qv_bias.astype(jnp.float32)
    out_bias_wide = out_bias_vec.astype(jnp.float32)
    first_w = owned[0]
    second_w = owned[1]
    first_bias_wide = first_bias.astype(jnp.float32)[:, None, :]
    second_bias_wide = second_bias.astype(jnp.float32)[:, None, :]
    router_wide = router_full.astype(jnp.float32)
    expert_ids = jnp.arange(experts_all, dtype=jnp.int32)
    column_scale = jnp.array([scaling, 1.0, 1.0], jnp.float32)[None, :, None]
    exp_dev = owned.shape[1]
    acc_qkv = jnp.zeros(qkv_full.shape, jnp.float32)
    acc_proj = jnp.zeros(proj_full.shape, jnp.float32)
    acc_router = jnp.zeros(router_full.shape, jnp.float32)
    acc_qv = jnp.zeros(qv_bias.shape, jnp.float32)
    acc_out_bias = jnp.zeros(out_bias_vec.shape, jnp.float32)
    acc_norms = jnp.zeros(norm_full.shape, jnp.float32)
    acc_experts = (
        jnp.zeros((2, exp_dev, owned.shape[2], expert_in.shape[1]), jnp.float32),
        jnp.zeros(expert_in_bias.shape, jnp.float32),
        jnp.zeros(expert_out_bias.shape, jnp.float32),
    )
    outputs = []
    input_grads = []
    for batch_index in range(MICRO):
        offset = batch_index * rows_mb
        row_vals = tokens[offset : offset + rows_mb].astype(jnp.float32)
        grad_out = cotangent[offset : offset + rows_mb].astype(jnp.float32)
        route_mb = routes[offset : offset + rows_mb]
        normed_out1, normed1, inv_std1 = norm_forward(row_vals, gain_one, shift_one)
        entry1 = normed_out1.astype(jnp.bfloat16)
        projected = jnp.einsum("td,dje->tje", entry1, qkv_full, preferred_element_type=jnp.float32)
        query_rows = (
            ((projected[:, 0] + qv_bias_wide[0]) * scaling).astype(jnp.bfloat16).reshape(head_shape)
        )
        key_rows = projected[:, 1].astype(jnp.bfloat16).reshape(head_shape)
        value_rows = (projected[:, 2] + qv_bias_wide[1]).astype(jnp.bfloat16).reshape(head_shape)
        scores = jnp.einsum(
            "ishd,ijhd->ihsj", query_rows, key_rows, preferred_element_type=jnp.float32
        )
        row_peak = jnp.max(scores, axis=-1, keepdims=True)
        exp_scores = jnp.exp(scores - row_peak)
        totals = jnp.sum(exp_scores, axis=-1, keepdims=True)
        attn_probs = exp_scores / totals
        log_totals = row_peak + jnp.log(totals)
        attn_mixed = (
            jnp.einsum(
                "ihsj,ijhd->ishd",
                attn_probs.astype(jnp.bfloat16),
                value_rows,
                preferred_element_type=jnp.float32,
            )
            .reshape(rows_mb, D)
            .astype(jnp.bfloat16)
        )
        branch = jnp.dot(attn_mixed, proj_full, preferred_element_type=jnp.float32) + out_bias_wide
        resid = row_vals + branch
        normed_out2, normed2, inv_std2 = norm_forward(resid, gain_two, shift_two)
        entry2 = normed_out2.astype(jnp.bfloat16)
        logits = jnp.dot(entry2, router_full, preferred_element_type=jnp.float32)
        router_probs = jax.nn.softmax(logits, axis=-1)
        chosen = route_mb[:, :, None] == expert_ids[None, None, :]
        gate_values = jnp.sum(jnp.where(chosen, router_probs[:, None, :], 0.0), axis=-1)
        route_flags = chosen.reshape(2 * rows_mb, experts_all).astype(jnp.int32)
        before = jnp.cumsum(route_flags, axis=0) - route_flags
        target = route_mb.reshape(-1) * capacity + jnp.sum(before * route_flags, axis=-1)
        outgoing = (
            jnp.zeros((experts_all * capacity, D), jnp.bfloat16)
            .at[target]
            .set(jnp.repeat(entry2, 2, axis=0))
        )
        arrived = lax.all_to_all(
            outgoing.reshape(experts_all, capacity, D),
            "col",
            split_axis=0,
            concat_axis=1,
            tiled=True,
        )
        pre_act = (
            jnp.einsum("erd,efd->erf", arrived, first_w, preferred_element_type=jnp.float32)
            + first_bias_wide
        )
        active = gelu_exact(pre_act).astype(jnp.bfloat16)
        result = (
            jnp.einsum("erf,efd->erd", active, second_w, preferred_element_type=jnp.float32)
            + second_bias_wide
        ).astype(jnp.bfloat16)
        returned = lax.all_to_all(result, "col", split_axis=1, concat_axis=0, tiled=True).reshape(
            experts_all * capacity, D
        )
        picked = returned[target].reshape(rows_mb, 2, D).astype(jnp.float32)
        outputs.append(
            (resid + jnp.sum(gate_values[:, :, None] * picked, axis=1)).astype(jnp.bfloat16)
        )
        grad_gates = jnp.sum(grad_out[:, None, :] * picked, axis=-1)
        grad_sent = (
            (gate_values[:, :, None] * grad_out[:, None, :])
            .astype(jnp.bfloat16)
            .reshape(2 * rows_mb, D)
        )
        grad_outgoing = (
            jnp.zeros((experts_all * capacity, D), jnp.bfloat16).at[target].set(grad_sent)
        )
        grad_result = lax.all_to_all(
            grad_outgoing.reshape(experts_all, capacity, D),
            "col",
            split_axis=0,
            concat_axis=1,
            tiled=True,
        )
        grad_active = jnp.einsum(
            "erd,efd->erf", grad_result, second_w, preferred_element_type=jnp.float32
        )
        grad_pre = jax.vjp(gelu_exact, pre_act)[1](grad_active)[0].astype(jnp.bfloat16)
        weight_terms = jnp.stack(
            [
                jnp.einsum("erf,erd->efd", grad_pre, arrived, preferred_element_type=jnp.float32),
                jnp.einsum("erf,erd->efd", active, grad_result, preferred_element_type=jnp.float32),
            ]
        )
        in_bias_terms = jnp.sum(grad_pre.astype(jnp.float32), axis=1)
        out_bias_terms = jnp.sum(grad_result.astype(jnp.float32), axis=1)
        weight_piece, in_bias_piece, out_bias_piece = (
            lax.psum_scatter(
                weight_terms.astype(jnp.bfloat16), "row", scatter_dimension=3, tiled=True
            ).astype(jnp.float32),
            lax.psum_scatter(
                in_bias_terms.astype(jnp.bfloat16), "row", scatter_dimension=1, tiled=True
            ).astype(jnp.float32),
            lax.psum_scatter(
                out_bias_terms.astype(jnp.bfloat16), "row", scatter_dimension=1, tiled=True
            ).astype(jnp.float32),
        )
        acc_experts = (
            acc_experts[0] + weight_piece,
            acc_experts[1] + in_bias_piece,
            acc_experts[2] + out_bias_piece,
        )
        grad_entry = jnp.einsum(
            "erf,efd->erd", grad_pre, first_w, preferred_element_type=jnp.float32
        ).astype(jnp.bfloat16)
        grad_back = lax.all_to_all(
            grad_entry, "col", split_axis=1, concat_axis=0, tiled=True
        ).reshape(experts_all * capacity, D)
        grad_entry2 = jnp.sum(grad_back[target].reshape(rows_mb, 2, D).astype(jnp.float32), axis=1)
        grad_probs = jnp.sum(jnp.where(chosen, grad_gates[:, :, None], 0.0), axis=1)
        grad_logits = router_probs * (
            grad_probs - jnp.sum(router_probs * grad_probs, axis=-1, keepdims=True)
        )
        grad_entry2 = grad_entry2 + jnp.dot(
            grad_logits, router_wide.T, precision=lax.Precision.HIGHEST
        )
        acc_router = acc_router + jnp.dot(
            entry2.astype(jnp.float32).T, grad_logits, precision=lax.Precision.HIGHEST
        )
        grad_norm2, gain_two_grad, shift_two_grad = norm_backward(
            grad_entry2, normed2, inv_std2, gain_two
        )
        grad_resid = grad_out + grad_norm2
        grad_branch = grad_resid.astype(jnp.bfloat16)
        acc_proj = acc_proj + jnp.einsum(
            "td,te->de", attn_mixed, grad_branch, preferred_element_type=jnp.float32
        )
        acc_out_bias = acc_out_bias + jnp.sum(grad_branch.astype(jnp.float32), axis=0)
        grad_mixed = (
            jnp.einsum("te,de->td", grad_branch, proj_full, preferred_element_type=jnp.float32)
            .astype(jnp.bfloat16)
            .reshape(head_shape)
        )
        scores_again = jnp.einsum(
            "ishd,ijhd->ihsj", query_rows, key_rows, preferred_element_type=jnp.float32
        )
        probs_again = jnp.exp(scores_again - log_totals)
        grad_weights = jnp.einsum(
            "ishd,ijhd->ihsj", grad_mixed, value_rows, preferred_element_type=jnp.float32
        )
        grad_values = jnp.einsum(
            "ihsj,ishd->ijhd",
            probs_again.astype(jnp.bfloat16),
            grad_mixed,
            preferred_element_type=jnp.float32,
        )
        inner_sum = jnp.sum(probs_again * grad_weights, axis=-1, keepdims=True)
        grad_scores = (probs_again * (grad_weights - inner_sum)).astype(jnp.bfloat16)
        grad_query = jnp.einsum(
            "ihsj,ijhd->ishd", grad_scores, key_rows, preferred_element_type=jnp.float32
        )
        grad_keys = jnp.einsum(
            "ihsj,ishd->ijhd", grad_scores, query_rows, preferred_element_type=jnp.float32
        )
        grad_qkv = jnp.stack(
            [
                grad_query.reshape(rows_mb, D),
                grad_keys.reshape(rows_mb, D),
                grad_values.reshape(rows_mb, D),
            ],
            axis=1,
        ).astype(jnp.bfloat16)
        acc_qkv = (
            acc_qkv
            + jnp.einsum("td,tje->dje", entry1, grad_qkv, preferred_element_type=jnp.float32)
            * column_scale
        )
        grad_sums = jnp.sum(grad_qkv.astype(jnp.float32), axis=0)
        acc_qv = acc_qv + jnp.stack([grad_sums[0] * scaling, grad_sums[2]])
        grad_entry1 = jnp.sum(
            jnp.einsum("tje,dje->tjd", grad_qkv, qkv_full, preferred_element_type=jnp.float32)
            * column_scale,
            axis=1,
        )
        grad_norm1, gain_one_grad, shift_one_grad = norm_backward(
            grad_entry1, normed1, inv_std1, gain_one
        )
        input_grads.append((grad_resid + grad_norm1).astype(jnp.bfloat16))
        acc_norms = acc_norms + jnp.stack(
            [gain_one_grad, shift_one_grad, gain_two_grad, shift_two_grad]
        )
    qkv_grad, proj_grad, router_grad, qv_grad, out_bias_grad = (
        lax.psum_scatter(acc_qkv, "col", scatter_dimension=2, tiled=True),
        lax.psum_scatter(acc_proj, "col", scatter_dimension=1, tiled=True),
        lax.psum_scatter(acc_router, "col", scatter_dimension=1, tiled=True),
        lax.psum_scatter(acc_qv, "col", scatter_dimension=1, tiled=True),
        lax.psum_scatter(acc_out_bias, "col", scatter_dimension=0, tiled=True),
    )
    qv_grad, out_bias_grad = lax.psum((qv_grad, out_bias_grad), "row")
    qkv_grad, proj_grad, router_grad, norm_grad = (
        lax.psum_scatter(
            qkv_grad.astype(jnp.bfloat16), "row", scatter_dimension=0, tiled=True
        ).astype(jnp.float32),
        lax.psum_scatter(
            proj_grad.astype(jnp.bfloat16), "row", scatter_dimension=0, tiled=True
        ).astype(jnp.float32),
        lax.psum_scatter(
            router_grad.astype(jnp.bfloat16), "row", scatter_dimension=0, tiled=True
        ).astype(jnp.float32),
        lax.psum_scatter(
            acc_norms.astype(jnp.bfloat16), "row", scatter_dimension=1, tiled=True
        ).astype(jnp.float32),
    )
    expert_stack, in_bias_grad, out_bias_expert = acc_experts
    norm_grad = lax.psum(norm_grad, "col")
    expert_blocks = lax.all_to_all(
        expert_stack.astype(jnp.bfloat16), "col", split_axis=2, concat_axis=1, tiled=True
    ).astype(expert_stack.dtype)
    return (
        jnp.concatenate(outputs, axis=0),
        jnp.concatenate(input_grads, axis=0),
        norm_grad[0],
        norm_grad[1],
        qkv_grad,
        qv_grad,
        proj_grad,
        out_bias_grad,
        norm_grad[2],
        norm_grad[3],
        router_grad,
        jnp.swapaxes(expert_blocks[0], 1, 2),
        in_bias_grad,
        expert_blocks[1],
        out_bias_expert,
    )

def ring_event(buf_of, sends, recvs, flow, step, r, c, pos, R, source_of=None, first=0):
    right, left = ring_at(pos + 1, R), ring_at(pos - 1, R)
    hops = R // 2
    from_left, from_right = ring_at(pos - step, R), ring_at(pos + step, R)
    a, b = buf_of(from_left), buf_of(from_right)
    if step > first:
        remote(a, a, sends.at[flow, 0, step - 1], recvs.at[flow, 0, step - 1], (right, c)).wait_recv()
        remote(b, b, sends.at[flow, 1, step - 1], recvs.at[flow, 1, step - 1], (left, c)).wait_recv()
    at_a, at_b = a, b
    if step == first and source_of is not None:
        at_a, at_b = source_of(from_left), source_of(from_right)
    if step == hops - 1:
        a, b, at_a, at_b = a.at[0], b.at[1], at_a.at[0], at_b.at[1]
    remote(at_a, a, sends.at[flow, 0, step], recvs.at[flow, 0, step], (right, c)).start()
    remote(at_b, b, sends.at[flow, 1, step], recvs.at[flow, 1, step], (left, c)).start()


def ring_finish(buf_of, sends, recvs, flow, r, c, pos, R, first, last):
    right, left = ring_at(pos + 1, R), ring_at(pos - 1, R)
    hops = R // 2
    if last > first:
        a, b = buf_of(ring_at(pos - last, R)), buf_of(ring_at(pos + last, R))
        if last == hops:
            a, b = a.at[0], b.at[1]
        remote(a, a, sends.at[flow, 0, last - 1], recvs.at[flow, 0, last - 1], (right, c)).wait_recv()
        remote(b, b, sends.at[flow, 1, last - 1], recvs.at[flow, 1, last - 1], (left, c)).wait_recv()
    own = buf_of(r)
    for step in range(first, last):
        a, b = (own, own) if step < hops - 1 else (own.at[0], own.at[1])
        remote(a, a, sends.at[flow, 0, step], recvs.at[flow, 0, step], (right, c)).wait_send()
        remote(b, b, sends.at[flow, 1, step], recvs.at[flow, 1, step], (left, c)).wait_send()


def front_kernel(
    R, C, E, SPLIT, FFP,
    tok, cot_in, packed, g1, s1, g2, s2, qv_bias, p_bias, router_col, out_bias, in_bias, wexp, rt,
    wbuf, e2_all, cot_all, info_all, tok_out, wg_out, qkv_out, mixed_out, probs_out, resid_out, rprob, sm_out,
    pack, flat, tokp, cot, wg, norm1, e2, wp, info, qkv, mixed, probs, resid,
    ring_s, ring_r, yring_s, yring_r, fan_s, fan_r, y_s, y_r,
    a2a_s, a2a_r, flow_s, flow_r, cot_s, cot_r, e2_s, e2_r, inf_s, inf_r, loc, keep_sem,
):
    r, c = lax.axis_index("row"), lax.axis_index("col")
    pos = ring_place(r, R)
    hops = R // 2
    right, left = ring_at(pos + 1, R), ring_at(pos - 1, R)
    core, ypeer, diag = col_core(c), col_y(c), col_diag(c)
    HB = D // R
    pack[0:HB, :] = packed[...]
    wide = []
    for ref in (g1, s1, g2, s2, qv_bias, p_bias, router_col, out_bias, in_bias):
        v = ref[...].astype(F32)
        wide.append(jnp.concatenate([v, jnp.zeros((v.shape[0], D - v.shape[1]), F32)], axis=1))
    wide.append(jnp.zeros((SMALL - 10, D), F32))
    vecs = jnp.concatenate(wide, axis=0)
    row_id = lax.broadcasted_iota(jnp.int32, (SMALL, D), 0)
    turned = pltpu.roll(vecs, r * HB, 1)
    inner = jnp.sum(jnp.where(row_id == 9, vecs, 0.0), axis=0, keepdims=True)
    inner = pltpu.roll(jnp.broadcast_to(inner, (SMALL, D)), lax.rem(r * FFP, D), 1)
    placed = jnp.where((row_id >= 4) & (row_id < 7), vecs, turned)
    placed = jnp.where(row_id < 9, placed, jnp.where(row_id == 9 + lax.div(r * FFP, D), inner, 0.0))
    pack[HB : HB + SMALL, :] = placed.astype(BF16)
    greet([(right, c), (left, c), (r, core), (r, ypeer), (r, diag)])
    HALF = 64
    TAIL = pack.shape[0] - HALF
    HB, WH = D // R, D // C
    W3 = 3 * WH
    heads = WH // HEAD_DIM

    at_l = [ring_at(pos - s, R) for s in range(hops + 1)]
    at_r = [ring_at(pos + s, R) for s in range(hops + 1)]
    rows_by = [r]
    for s in range(1, hops):
        rows_by += [at_l[s], at_r[s]]
    rows_by.append(at_l[hops])

    def fan(kind, j, col):
        blk = wg.at[col, rows_by[j]]
        return remote(blk, blk, fan_s.at[kind, j], fan_r.at[kind, j], (r, core))

    def over_y(n, j, col):
        blk = wg.at[col, rows_by[j]]
        return remote(blk, blk, y_s.at[n], y_r.at[n], (r, ypeer))

    def own_ring(d, s, blk):
        if s == hops - 1:
            blk = blk.at[pl.ds(0, HALF)] if d == 0 else blk.at[pl.ds(HALF, TAIL)]
        return remote(blk, blk, ring_s.at[d, s], ring_r.at[d, s], (right if d == 0 else left, c))

    def far_ring(d, s, blk):
        if s == hops - 1:
            blk = blk.at[pl.ds(0, HALF)] if d == 0 else blk.at[pl.ds(HALF, TAIL)]
        return remote(blk, blk, yring_s.at[d, s], yring_r.at[d, s], (right if d == 0 else left, c))

    own = wg.at[c, r]
    remote(pack, own, ring_s.at[0, 0], ring_r.at[0, 0], (right, c)).start()
    remote(pack, own, ring_s.at[1, 0], ring_r.at[1, 0], (left, c)).start()
    remote(pack, own, y_s.at[0], y_r.at[0], (r, ypeer)).start()
    remote(pack, own, fan_s.at[0, 0], fan_r.at[0, 0], (r, core)).start()
    own_pack = pltpu.make_async_copy(pack, own, loc.at[0])
    own_pack.start()
    own_exp = pltpu.make_async_copy(wexp.at[c], wbuf.at[c, r], loc.at[1])
    own_exp.start()
    peers = [core, ypeer, diag]

    def a2a(n):
        return remote(wexp.at[peers[n]], wbuf.at[c, r], a2a_s.at[n], a2a_r.at[n], (r, peers[n]))

    def a2a_in(n):
        blk = wbuf.at[peers[n], r]
        return remote(blk, blk, a2a_s.at[n], a2a_r.at[n], (r, peers[n]))

    a2a(0).start()

    real = lax.broadcasted_iota(jnp.int32, (IMG, 1), 0) < SEQ
    even = tok.shape[0] // 16 * 16

    def images(src):
        flat[0:even, :] = src[0:even, :].astype(F32)
        flat[even : src.shape[0], :] = src[even : src.shape[0], :].astype(F32)
        for i in range(IMAGES):
            yield i, jnp.where(real, flat[i * SEQ : i * SEQ + IMG, :], 0.0)

    for i, rows in images(cot_in):
        cot[i * IMG : (i + 1) * IMG, :] = rows.astype(BF16)
    own_cot = pltpu.make_async_copy(cot, cot_all.at[c], loc.at[2])
    own_cot.start()
    for i, rows in images(tok):
        tokp[i * IMG : (i + 1) * IMG, :] = rows.astype(BF16)
        norm1[i * IMG : (i + 1) * IMG, :] = norm_rows(rows)[0]
    own_tok = pltpu.make_async_copy(tokp, tok_out, loc.at[5 + IMAGES])
    own_tok.start()

    over_y(0, 0, ypeer).wait_recv()
    far_ring(0, 0, wg.at[ypeer, r]).start()
    far_ring(1, 0, wg.at[ypeer, r]).start()
    fan(1, 0, ypeer).start()
    remote(cot, cot_all.at[c], cot_s.at[1], cot_r.at[1], (r, ypeer)).start()
    for s in range(1, hops + 1):
        for ring, col, kind in ((own_ring, c, 0), (far_ring, ypeer, 1)):
            for d, o in enumerate((at_l[s], at_r[s])):
                blk = wg.at[col, o]
                ring(d, s - 1, blk).wait_recv()
                if s < hops:
                    ring(d, s, blk).start()
            fan(kind, 2 * s - 1, col).start()
            if s < hops:
                fan(kind, 2 * s, col).start()
        if s == 2:
            a2a(1).start()
            a2a(2).start()
    own_pack.wait()
    own_exp.wait()

    def flow_buf(k):
        f = col_at(c, k)
        return lambda o: wbuf.at[f, o]

    def gather(k, s):
        if s < SPLIT[k]:
            ring_event(flow_buf(k), flow_s, flow_r, k, s, r, c, pos, R)

    gather(0, 0)
    a2a_in(0).wait_recv()
    gather(1, 0)
    remote(cot, cot_all.at[c], cot_s.at[0], cot_r.at[0], (r, core)).start()
    for j in range(R):
        fan(0, j, core).wait_recv()
        fan(1, j, diag).wait_recv()
    send_wg = pltpu.make_async_copy(wg, wg_out, loc.at[3])
    send_wg.start()

    own_small = jnp.zeros((SMALL, D), F32)
    for o in range(R):
        own_small = own_small + wg[c, o, HB : HB + SMALL, :].astype(F32)
    gain1, shift1 = own_small[0:1], own_small[1:2]
    gain2, shift2 = own_small[2:3], own_small[3:4]
    lane = lax.broadcasted_iota(jnp.int32, (1, W3), 1)
    col_scale = jnp.where(lane < WH, SCALE, 1.0).astype(F32)
    keep = lax.broadcasted_iota(jnp.int32, (1, IMG), 1) < SEQ
    rtr, pb, biases = [], [], []
    for g in range(C):
        wp[:, g * WH : (g + 1) * WH] = wg[g, :, 0:HB, W3:].reshape(D, WH)
        small = wg[g, 0, HB : HB + SMALL, :].astype(F32)
        bq, bv = small[4:5, :WH], small[5:6, :WH]
        biases.append(jnp.concatenate([bq, jnp.zeros_like(bq), bv], axis=1))
        pb.append(small[6:7, :WH])
        acc = jnp.zeros((1, D), F32)
        for o in range(R):
            acc = acc + wg[g, o, HB : HB + SMALL, :].astype(F32)[7:8]
        rtr.append(acc)
    pbias = jnp.concatenate(pb, axis=1)
    router_t = jnp.concatenate(rtr + [jnp.zeros((8 - C, D), F32)], axis=0)
    sm_out[0:SMALL, :] = own_small
    sm_out[SMALL : SMALL + 8, :] = router_t
    router_b = router_t.astype(BF16)
    upper = (
        lax.broadcasted_iota(jnp.int32, (BLK, BLK), 0) < lax.broadcasted_iota(jnp.int32, (BLK, BLK), 1)
    ).astype(BF16)
    exp_id = lax.broadcasted_iota(jnp.int32, (8, BLK), 0)

    def e2_copy(n, i, who, peer):
        part = pl.ds(i * IMG, IMG)
        src = e2.at[part] if n < 2 else e2_all.at[who, part]
        return remote(src, e2_all.at[who, part], e2_s.at[n, i], e2_r.at[n, i], (r, peer))

    locals_ = []
    for i in range(IMAGES):
        rows = slice(i * IMG, (i + 1) * IMG)
        entry1 = (norm1[rows, :] * gain1 + shift1).astype(BF16)
        acc = tokp[rows, :].astype(F32) + pbias
        for g in range(C):
            w = wg[g, :, 0:HB, 0:W3].reshape(D, W3)
            z = ((dot_nn(entry1, w) + biases[g]) * col_scale).astype(BF16)
            qkv[g, rows, :] = z
            outs = []
            for h in range(heads):
                q = z[:, h * HEAD_DIM : (h + 1) * HEAD_DIM]
                kk = z[:, WH + h * HEAD_DIM : WH + (h + 1) * HEAD_DIM]
                v = z[:, 2 * WH + h * HEAD_DIM : 2 * WH + (h + 1) * HEAD_DIM]
                s = jnp.where(keep, dot_nt(q, kk), -1e30)
                ex = jnp.exp(s - jnp.max(s, axis=-1, keepdims=True))
                p = (ex / jnp.sum(ex, axis=-1, keepdims=True)).astype(BF16)
                probs[g, i, h] = p
                outs.append(dot_nn(p, v))
            mix = jnp.concatenate(outs, axis=1).astype(BF16)
            mixed[g, rows, :] = mix
            acc = acc + dot_nn(mix, wp[g * WH : (g + 1) * WH, :])
        resid[rows, :] = acc
        e2[rows, :] = (norm_rows(acc)[0] * gain2 + shift2).astype(BF16)
        e2_copy(1, i, c, ypeer).start()
        e2_copy(0, i, c, core).start()
        part = pl.ds(i * IMG, IMG)
        cp = pltpu.make_async_copy(e2.at[part], e2_all.at[c, part], loc.at[4 + i])
        cp.start()
        locals_.append(cp)
        for n, (src, dst) in enumerate((
            (qkv.at[:, part], qkv_out.at[:, part]),
            (mixed.at[:, part], mixed_out.at[:, part]),
            (probs.at[:, i], probs_out.at[:, i]),
            (resid.at[part], resid_out.at[part]),
        )):
            cp = pltpu.make_async_copy(src, dst, keep_sem.at[n, i])
            cp.start()
            locals_.append(cp)
        if i % IMG_MB == IMG_MB - 1:
            h = i // IMG_MB
            blk = e2[h * BLK : (h + 1) * BLK, :]
            logits = jnp.where(exp_id < E, dot_nt(router_b, blk), -1e30)
            ex = jnp.exp(logits - jnp.max(logits, axis=0, keepdims=True))
            prob = ex / jnp.sum(ex, axis=0, keepdims=True)
            rprob[h] = prob
            named = rt[h]
            member = (named[0:1] == exp_id.astype(F32)) | (named[1:2] == exp_id.astype(F32))
            flags = jnp.where(member, 1.0, 0.0)
            rank = dot_nn(flags.astype(BF16), upper)
            info[h, 0:8, :] = jnp.where(member, rank, -1.0)
            info[h, 8:16, :] = jnp.where(member, prob, 0.0)
        if i == IMAGES - 1:
            cp = pltpu.make_async_copy(info, info_all.at[c], loc.at[4 + IMAGES])
            cp.start()
            locals_.append(cp)
            for n, peer in enumerate(peers):
                remote(info, info_all.at[c], inf_s.at[n], inf_r.at[n], (r, peer)).start()
        if i == 1:
            gather(0, 1)
        if i == 2:
            gather(1, 1)

    def relay(i):
        e2_copy(1, i, ypeer, ypeer).wait_recv()
        e2_copy(2, i, ypeer, core).start()

    relay(0)
    remote(cot, cot_all.at[ypeer], cot_s.at[1], cot_r.at[1], (r, ypeer)).wait_recv()
    remote(cot_all.at[ypeer], cot_all.at[ypeer], cot_s.at[2], cot_r.at[2], (r, core)).start()
    gather(0, 2)
    relay(1)
    gather(1, 2)
    for n in (1, 2):
        a2a_in(n).wait_recv()
    gather(2, 0)
    relay(2)
    gather(0, 3)
    gather(1, 3)
    relay(3)
    gather(2, 1)

    for n, who in ((0, core), (2, diag)):
        blk = cot_all.at[who]
        remote(blk, blk, cot_s.at[n], cot_r.at[n], (r, core)).wait_recv()
    for n in range(3):
        remote(cot, cot_all.at[c], cot_s.at[n], cot_r.at[n], (r, core)).wait_send()
    for i in range(IMAGES):
        e2_copy(0, i, core, core).wait_recv()
        e2_copy(2, i, diag, core).wait_recv()
        for n in range(3):
            e2_copy(n, i, c, core).wait_send()
    for n, peer in enumerate(peers):
        cp = remote(info, info_all.at[peer], inf_s.at[n], inf_r.at[n], (r, peer))
        cp.wait_recv()
        cp.wait_send()
        a2a(n).wait_send()
    for j in range(R):
        fan(0, j, c).wait_send()
        fan(1, j, c).wait_send()
    over_y(0, 0, c).wait_send()
    for d in range(2):
        for s in range(hops):
            own_ring(d, s, own).wait_send()
            far_ring(d, s, own).wait_send()
    for k in range(C):
        ring_finish(flow_buf(k), flow_s, flow_r, k, r, c, pos, R, 0, SPLIT[k])
    own_cot.wait()
    own_tok.wait()
    send_wg.wait()
    for cp in locals_:
        cp.wait()


def front(R, C, E, SPLIT, FFP, tok, cot, packed, smalls, wexp, rt):
    WH = D // C
    HB = D // R
    hops = R // 2
    vm = pl.BlockSpec(memory_space=pltpu.VMEM)
    hbm = pl.BlockSpec(memory_space=pl.ANY)
    sem = pltpu.SemaphoreType.DMA
    heads = WH // HEAD_DIM
    return pl.pallas_call(
        functools.partial(front_kernel, R, C, E, SPLIT, FFP),
        name="front",
        out_shape=(
            jax.ShapeDtypeStruct((C, R, 2, HB, D), BF16),
            jax.ShapeDtypeStruct((C, ROWS, D), BF16),
            jax.ShapeDtypeStruct((C, ROWS, D), BF16),
            jax.ShapeDtypeStruct((C, MICRO, 16, BLK), F32),
            jax.ShapeDtypeStruct((ROWS, D), BF16),
            jax.ShapeDtypeStruct((C, R, HB + SMALL, D), BF16),
            jax.ShapeDtypeStruct((C, ROWS, 3 * WH), BF16),
            jax.ShapeDtypeStruct((C, ROWS, WH), BF16),
            jax.ShapeDtypeStruct((C, IMAGES, heads, IMG, IMG), BF16),
            jax.ShapeDtypeStruct((ROWS, D), F32),
            jax.ShapeDtypeStruct((MICRO, 8, BLK), F32),
            jax.ShapeDtypeStruct((SMALL + 8, D), F32),
        ),
        in_specs=[vm] * (5 + len(smalls)),
        out_specs=(hbm,) * 10 + (vm, vm),
        scratch_shapes=[
            pltpu.VMEM((HB + SMALL, D), BF16),
            pltpu.VMEM(((IMAGES - 1) * SEQ + IMG + 1, D), F32),
            pltpu.VMEM((ROWS, D), BF16),
            pltpu.VMEM((ROWS, D), BF16),
            pltpu.VMEM((C, R, HB + SMALL, D), BF16),
            pltpu.VMEM((ROWS, D), F32),
            pltpu.VMEM((ROWS, D), BF16),
            pltpu.VMEM((D, D), BF16),
            pltpu.VMEM((MICRO, 16, BLK), F32),
            pltpu.VMEM((C, ROWS, 3 * WH), BF16),
            pltpu.VMEM((C, ROWS, WH), BF16),
            pltpu.VMEM((C, IMAGES, heads, IMG, IMG), BF16),
            pltpu.VMEM((ROWS, D), F32),
            sem((2, hops)), sem((2, hops)),
            sem((2, hops)), sem((2, hops)),
            sem((2, R)), sem((2, R)),
            sem((1,)), sem((1,)),
            sem((3,)), sem((3,)),
            sem((C, 2, hops)), sem((C, 2, hops)),
            sem((3,)), sem((3,)),
            sem((3, IMAGES)), sem((3, IMAGES)),
            sem((3,)), sem((3,)),
            sem((6 + IMAGES,)), sem((4, IMAGES)),
        ],
        compiler_params=pltpu.CompilerParams(
            collective_id=1, has_side_effects=True, vmem_limit_bytes=56 << 20
        ),
    )(tok, cot, packed, *smalls, wexp, rt)

def reduce_event(parts, rbuf, sends, recvs, slot, step, r, c, pos, R):
    right, left = ring_at(pos + 1, R), ring_at(pos - 1, R)
    hops = R // 2
    to_right, to_left = ring_at(pos + hops - step, R), ring_at(pos - hops + step, R)
    for d, (dest, peer) in enumerate(((to_right, right), (to_left, left))):
        if step > 0:
            got = rbuf(d, step - 1)
            if step == 1:
                got, mine = got.at[d], parts.at[dest, d]
            else:
                mine = parts.at[dest]
            remote(got, got, sends.at[slot, d, step - 1], recvs.at[slot, d, step - 1], (peer, c)).wait_recv()
            mine[...] = (mine[...].astype(F32) + got[...].astype(F32)).astype(BF16)
        src, dst = parts.at[dest], rbuf(d, step)
        if step == 0:
            src, dst = src.at[d], dst.at[d]
        remote(src, dst, sends.at[slot, d, step], recvs.at[slot, d, step], (peer, c)).start()


def reduce_finish(parts, rbuf, sends, recvs, slot, r, c, pos, R):
    hops = R // 2
    total = parts[r].astype(F32)
    for d in range(2):
        got = rbuf(d, hops - 1)
        remote(got, got, sends.at[slot, d, hops - 1], recvs.at[slot, d, hops - 1], (r, c)).wait_recv()
        total = total + got[...].astype(F32)
    for d in range(2):
        for step in range(hops):
            src, dst = parts.at[r], rbuf(d, step)
            if step == 0:
                src, dst = src.at[d], dst.at[d]
            remote(src, dst, sends.at[slot, d, step], recvs.at[slot, d, step], (r, c)).wait_send()
    return total


def expert_kernel(
    R, C, CAP, SPLIT,
    e2_all, cot_all, info_all, wbuf, sm,
    ge_parts, mix_parts, mix_out, gg_all, dexp, raw, wfar, bias_out,
    wv, eb, gb, info, X, GR, RES, GE, act, gh, stage, rbuf, corebuf, mixd, fin, ggs,
    w_sem, eb_sem, loc, flow_s, flow_r, red_s, red_r, fin_s, fin_r, core_s, core_r, ge_s, ge_r, mx_s, mx_r, gg_s, gg_r,
):
    r, c = lax.axis_index("row"), lax.axis_index("col")
    pos = ring_place(r, R)
    hops = R // 2
    HB = D // R
    right, left = ring_at(pos + 1, R), ring_at(pos - 1, R)
    core, ypeer, diag = col_core(c), col_y(c), col_diag(c)
    greet([(right, c), (left, c), (r, core), (r, ypeer), (r, diag)])
    NB = C * MICRO
    TR = NB * CAP

    def from_front(k):
        f = col_at(c, k)
        return lambda o: wbuf.at[f, o]

    def far_buf(k):
        return lambda o: wfar.at[k - 2, o]

    def gather(k, s):
        if s >= SPLIT[k]:
            ring_event(
                far_buf(k), flow_s, flow_r, k - 2, s, r, c, pos, R, from_front(k), SPLIT[k]
            )

    def more(k, s):
        if s > SPLIT[k]:
            gather(k, s)

    def weights(k):
        if k < 2:
            return [pltpu.make_async_copy(wbuf.at[col_at(c, k)], wv.at[k], w_sem.at[k, 0])]
        cps = []
        origins = [(r, 0)]
        for s in range(1, hops):
            origins += [(ring_at(pos - s, R), s), (ring_at(pos + s, R), s)]
        origins.append((ring_at(pos + hops, R), hops))
        for n, (o, s) in enumerate(origins):
            src = from_front(k)(o) if s <= SPLIT[k] else far_buf(k)(o)
            cps.append(pltpu.make_async_copy(src, wv.at[k - 2, o], w_sem.at[k, n]))
        return cps

    pending = {k: weights(k) for k in range(2)}
    for cp in pending[0] + pending[1]:
        cp.start()
    get_info = pltpu.make_async_copy(info_all, info, loc.at[0])
    get_info.start()
    gather(2, SPLIT[2])

    def place(p):
        return col_at(c, C - 1 - lax.div(p, MICRO)), lax.rem(p, MICRO)

    def fetch(p, slot, which):
        s, h = place(p)
        src, dst = (e2_all, eb) if which == 0 else (cot_all, gb)
        return pltpu.make_async_copy(
            src.at[s, pl.ds(pl.multiple_of(h * BLK, 16), BLK)], dst.at[slot], eb_sem.at[which, slot]
        )

    slot_id = lax.broadcasted_iota(jnp.int32, (CAP, BLK), 0).astype(F32)

    def pick(p):
        s, h = place(p)
        code = info[s, h, pl.ds(c, 1), :]
        gate = info[s, h, pl.ds(8 + c, 1), :]
        hot = jnp.where(slot_id == code, 1.0, 0.0)
        gate_slot = jnp.sum(hot * gate, axis=1, keepdims=True)
        return hot, gate_slot

    fetch(0, 0, 0).start()
    fetch(0, 0, 1).start()
    get_info.wait()

    def dispatch(p, bias):
        slot = lax.rem(p, 2)

        @pl.when(p + 1 < NB)
        def _():
            fetch(p + 1, 1 - slot, 0).start()
            fetch(p + 1, 1 - slot, 1).start()

        fetch(p, slot, 0).wait()
        fetch(p, slot, 1).wait()
        hot, gate_slot = pick(p)
        hot = hot.astype(BF16)
        rows = pl.ds(pl.multiple_of(p * CAP, 16), CAP)
        X[rows, :] = dot_nn(hot, eb[slot]).astype(BF16)
        g16 = (gate_slot * dot_nn(hot, gb[slot])).astype(BF16)
        GR[rows, :] = g16
        return bias + jnp.sum(g16.astype(F32), axis=0, keepdims=True)

    bias_out[...] = jnp.zeros_like(bias_out)
    out_bias = lax.fori_loop(0, NB // 2, dispatch, jnp.zeros((1, D), F32))
    gather(3, 0)
    bias_out[0:1, :] = lax.fori_loop(NB // 2, NB, dispatch, out_bias)
    more(2, 2)

    def red(k, step):
        reduce_event(stage.at[k], lambda d, s: rbuf.at[k, d, s], red_s, red_r, k, step, r, c, pos, R)

    def red_end(k):
        total = reduce_finish(stage.at[k], lambda d, s: rbuf.at[k, d, s], red_s, red_r, k, r, c, pos, R)
        fin[k] = total.astype(BF16)
        if k == 0:
            cp = pltpu.make_async_copy(fin.at[0], dexp.at[c], loc.at[1])
        else:
            cp = remote(fin.at[1], dexp.at[c], fin_s.at[0], fin_r.at[0], (r, core))
        cp.start()
        return cp

    MT = 512
    DT = D // 2
    HALFR = TR // 2

    def ffn(k, at, n):
        f = col_at(c, k)
        b1 = sm[pl.ds(9 + f, 1), :]
        slot = k % 2

        def tile(m, bias):
            rows = pl.ds(pl.multiple_of(at + m * MT, 16), MT)
            win = wv[slot, :, 0].reshape(D, D)
            wout = wv[slot, :, 1].reshape(D, D)
            hid = dot_nn(X[rows, :], win) + b1
            cdf = 0.5 * (1.0 + lax.erf(hid * (2.0 ** -0.5)))
            a16 = (hid * cdf).astype(BF16)
            act[slot, rows, :] = a16
            slope = cdf + hid * (jnp.exp(-0.5 * hid * hid) * ((2.0 * math.pi) ** -0.5))
            ga = dot_nn(GR[rows, :], wout)
            g16 = (ga * slope).astype(BF16)
            gh[slot, rows, :] = g16
            res = dot_nt(a16, wout)
            gen = dot_nt(g16, win)
            if k == 0:
                RES[rows, :] = res
                GE[rows, :] = gen
            else:
                RES[rows, :] = RES[rows, :] + res
                GE[rows, :] = GE[rows, :] + gen
            return bias + jnp.sum(g16.astype(F32), axis=0, keepdims=True)

        bsum = lax.fori_loop(0, n // MT, tile, jnp.zeros((1, D), F32))
        bias_out[pl.ds(1 + f, 1), :] = bias_out[pl.ds(1 + f, 1), :] + bsum

    def weight_grads(k, first, last):
        slot = k % 2

        def tile(j, _):
            cols = pl.ds(pl.multiple_of(j * DT, 128), DT)
            blocks = pl.ds(j * (R // 2), R // 2)
            stage[k, blocks, 0] = dot_tn(X[:, cols], gh[slot]).astype(BF16).reshape(R // 2, HB, D)
            stage[k, blocks, 1] = dot_tn(GR[:, cols], act[slot]).astype(BF16).reshape(R // 2, HB, D)
            return 0

        lax.fori_loop(first, last, tile, 0)

    order = [diag, ypeer, core, c]
    b2 = sm[8:9, :]
    sends = []

    def give_back(o):
        for h in range(MICRO):
            n = o * MICRO + h
            slot = n % 2
            if n + 1 < NB:
                fetch(n + 1, 1 - slot, 1).start()
            fetch(n, slot, 1).wait()
            if o == 0:
                ge_blk, mx_blk = eb.at[h], mixd.at[h]
            elif o == 1:
                ge_blk, mx_blk = corebuf.at[0, h], corebuf.at[1, h]
            else:
                at = pl.ds((o - 2) * MICRO * BLK + h * BLK, BLK)
                ge_blk, mx_blk = X.at[at], GR.at[at]
            hot, gate_slot = pick(n)
            hot_t = hot.T.astype(BF16)
            rows = slice(n * CAP, (n + 1) * CAP)
            res = (RES[rows, :] + b2).astype(BF16).astype(F32)
            g = dot_nn(hot.astype(BF16), gb[slot])
            gg = jnp.sum(g * res, axis=1, keepdims=True)
            gg_row = jnp.sum(hot * gg, axis=0, keepdims=True)
            mine = lax.broadcasted_iota(jnp.int32, (8, BLK), 0) == c
            ggs[o, h] = jnp.where(mine, gg_row, 0.0)
            ge = dot_nn(hot_t, GE[rows, :].astype(BF16))
            mx = dot_nn(hot_t, (gate_slot * res).astype(BF16))
            part = pl.ds(h * BLK, BLK)
            if o == 1:
                for t in range(2):
                    cb = corebuf.at[t, h]
                    remote(cb, cb, core_s.at[t, h], core_r.at[t, h], (r, core)).wait_recv()
                ge = ge + corebuf[0, h].astype(F32)
                mx = mx + corebuf[1, h].astype(F32)
            ge_blk[...] = ge.astype(BF16)
            mx_blk[...] = mx.astype(BF16)
            if o == 0:
                cps = [
                    remote(ge_blk, corebuf.at[0, h], core_s.at[0, h], core_r.at[0, h], (r, core)),
                    remote(mx_blk, corebuf.at[1, h], core_s.at[1, h], core_r.at[1, h], (r, core)),
                ]
            elif o == 1:
                cps = [
                    remote(ge_blk, ge_parts.at[2, part], ge_s.at[1, h], ge_r.at[1, h], (r, ypeer)),
                    pltpu.make_async_copy(mx_blk, mix_out.at[part], loc.at[4 + h]),
                ]
            elif o == 2:
                cps = [
                    remote(ge_blk, ge_parts.at[1, part], ge_s.at[0, h], ge_r.at[0, h], (r, core)),
                    remote(mx_blk, mix_parts.at[1, part], mx_s.at[h], mx_r.at[h], (r, core)),
                ]
            else:
                cps = [
                    pltpu.make_async_copy(ge_blk, ge_parts.at[0, part], loc.at[6 + h]),
                    pltpu.make_async_copy(mx_blk, mix_parts.at[0, part], loc.at[8 + h]),
                ]
            for cp in cps:
                cp.start()
            sends.append((o, cps))
        if o < 3:
            cp = remote(ggs.at[o], gg_all.at[c], gg_s.at[o], gg_r.at[o], (r, order[o]))
        else:
            cp = pltpu.make_async_copy(ggs.at[3], gg_all.at[c], loc.at[10])
        cp.start()
        sends.append((4 if o < 3 else 5, [cp]))

    def load(k):
        for cp in weights(k):
            cp.start()

    def loaded(k):
        for cp in weights(k):
            cp.wait()

    loaded(0)
    ffn(0, 0, HALFR)
    gather(3, 1)
    ffn(0, HALFR, HALFR)
    weight_grads(0, 0, 2)
    more(2, 3)
    loaded(1)
    ffn(1, 0, HALFR)
    gather(3, 2)
    ring_finish(far_buf(2), flow_s, flow_r, 0, r, c, pos, R, SPLIT[2], hops)
    load(2)
    ffn(1, HALFR, HALFR)
    weight_grads(1, 0, 1)
    gather(3, 3)
    weight_grads(1, 1, 2)
    red(0, 0)
    loaded(2)
    fetch(0, 0, 1).start()
    ffn(2, 0, HALFR)
    ring_finish(far_buf(3), flow_s, flow_r, 1, r, c, pos, R, SPLIT[3], hops)
    load(3)
    red(0, 1)
    red(1, 0)
    loaded(3)
    ffn(3, 0, HALFR)
    red(0, 2)
    give_back(0)
    give_back(1)
    red(1, 1)
    ffn(2, HALFR, HALFR)
    red(0, 3)
    ffn(3, HALFR, HALFR)
    red(1, 2)
    weight_grads(2, 0, 2)
    end0 = red_end(0)
    red(1, 3)
    raws = [pltpu.make_async_copy(stage.at[2], raw.at[0], loc.at[2])]
    raws[0].start()
    weight_grads(3, 0, 2)
    raws.append(pltpu.make_async_copy(stage.at[3], raw.at[1], loc.at[3]))
    raws[1].start()
    give_back(2)
    give_back(3)
    end1 = red_end(1)

    for o, cps in sends:
        for t, cp in enumerate(cps):
            if o == 3 or o == 5 or (o == 1 and t == 1):
                cp.wait()
            else:
                cp.wait_send()
    for h in range(MICRO):
        part = pl.ds(h * BLK, BLK)
        for n2, slot2 in enumerate((1, 2)):
            g_ref = ge_parts.at[slot2, part]
            remote(g_ref, g_ref, ge_s.at[n2, h], ge_r.at[n2, h], (r, core)).wait_recv()
        m_ref = mix_parts.at[1, part]
        remote(m_ref, m_ref, mx_s.at[h], mx_r.at[h], (r, core)).wait_recv()
    for o, peer in enumerate((diag, ypeer, core)):
        g_ref = gg_all.at[peer]
        remote(g_ref, g_ref, gg_s.at[o], gg_r.at[o], (r, peer)).wait_recv()
    end0.wait()
    end1.wait_send()
    d_ref = dexp.at[core]
    remote(d_ref, d_ref, fin_s.at[0], fin_r.at[0], (r, core)).wait_recv()
    for cp in raws:
        cp.wait()


def expert(R, C, CAP, SPLIT, e2_all, cot_all, info_all, wbuf, sm):
    HB = D // R
    hops = R // 2
    TR = C * MICRO * CAP
    vm = pl.BlockSpec(memory_space=pltpu.VMEM)
    hbm = pl.BlockSpec(memory_space=pl.ANY)
    sem = pltpu.SemaphoreType.DMA
    return pl.pallas_call(
        functools.partial(expert_kernel, R, C, CAP, SPLIT),
        name="expert",
        out_shape=(
            jax.ShapeDtypeStruct((3, ROWS, D), BF16),
            jax.ShapeDtypeStruct((2, ROWS, D), BF16),
            jax.ShapeDtypeStruct((ROWS, D), BF16),
            jax.ShapeDtypeStruct((C, MICRO, 8, BLK), F32),
            jax.ShapeDtypeStruct((C, 2, HB, D), BF16),
            jax.ShapeDtypeStruct((2, R, 2, HB, D), BF16),
            jax.ShapeDtypeStruct((2, R, 2, HB, D), BF16),
            jax.ShapeDtypeStruct((8, D), F32),
        ),
        in_specs=[hbm, hbm, hbm, hbm, vm],
        out_specs=(hbm, hbm, hbm, hbm, hbm, hbm, hbm, vm),
        scratch_shapes=[
            pltpu.VMEM((2, R, 2, HB, D), BF16),
            pltpu.VMEM((2, BLK, D), BF16),
            pltpu.VMEM((2, BLK, D), BF16),
            pltpu.VMEM((C, MICRO, 16, BLK), F32),
            pltpu.VMEM((TR, D), BF16),
            pltpu.VMEM((TR, D), BF16),
            pltpu.VMEM((TR, D), F32),
            pltpu.VMEM((TR, D), F32),
            pltpu.VMEM((2, TR, D), BF16),
            pltpu.VMEM((2, TR, D), BF16),
            pltpu.VMEM((C, R, 2, HB, D), BF16),
            pltpu.VMEM((2, 2, hops, 2, HB, D), BF16),
            pltpu.VMEM((2, MICRO, BLK, D), BF16),
            pltpu.VMEM((MICRO, BLK, D), BF16),
            pltpu.VMEM((2, 2, HB, D), BF16),
            pltpu.VMEM((C, MICRO, 8, BLK), F32),
            sem((C, R)), sem((2, 2)), sem((11,)),
            sem((2, 2, hops)), sem((2, 2, hops)),
            sem((2, 2, hops)), sem((2, 2, hops)),
            sem((1,)), sem((1,)),
            sem((2, MICRO)), sem((2, MICRO)),
            sem((2, MICRO)), sem((2, MICRO)),
            sem((MICRO,)), sem((MICRO,)),
            sem((3,)), sem((3,)),
        ],
        compiler_params=pltpu.CompilerParams(
            collective_id=2, has_side_effects=True, vmem_limit_bytes=62 << 20
        ),
    )(e2_all, cot_all, info_all, wbuf, sm)

def back_kernel(
    R, C, E, FFP,
    tok, cot_all, ge_parts, mix_parts, mix_out, gg, rprob, resid_in, qkv_in, mixed_in, probs_in, wg_in, sm, raw, bias_in,
    out, input_grad, attn_grad, dexp, mixy, n1_gain, n1_shift, n2_gain, n2_shift, router_out, pb_out, ab_out, eib_out, eob_out,
    cot, wg, gp, resid, qkv, mixed, probs, stage, rbuf, wp, gbr, dres, gm, e1t, dz, ge1, gblk, corein, yin, apart, abuf, early, late, sbuf, cbuf, rbuf2,
    loc, red_s, red_r, fin_s, fin_r, mix_s, mix_r, ag_s, ag_r, ar_s, ar_r, sm_s, sm_r, lc_s, lc_r, lr_s, lr_r,
):
    r, c = lax.axis_index("row"), lax.axis_index("col")
    pos = ring_place(r, R)
    hops = R // 2
    HB = D // R
    WH = D // C
    W3 = 3 * WH
    heads = WH // HEAD_DIM
    right, left = ring_at(pos + 1, R), ring_at(pos - 1, R)
    core, ypeer, diag = col_core(c), col_y(c), col_diag(c)

    copies = [
        pltpu.make_async_copy(raw, stage, loc.at[0]),
        pltpu.make_async_copy(ge_parts, gp, loc.at[1]),
        pltpu.make_async_copy(resid_in, resid, loc.at[4]),
        pltpu.make_async_copy(cot_all.at[c], cot, loc.at[8]),
        pltpu.make_async_copy(wg_in.at[:, :, pl.ds(0, HB)], wg, loc.at[2]),
    ]
    later = [
        pltpu.make_async_copy(mixed_in, mixed, loc.at[5]),
        pltpu.make_async_copy(qkv_in, qkv, loc.at[6]),
        pltpu.make_async_copy(probs_in, probs, loc.at[7]),
    ]
    for cp in copies:
        cp.start()
    pairs = [(r, core), (r, ypeer)]
    step_bit = 1
    while step_bit < R:
        bit = lax.rem(lax.div(r, step_bit), 2)
        pairs.append((r + step_bit - 2 * step_bit * bit, c))
        step_bit *= 2
    others = [(lax.rem(r + n, R), c) for n in range(1, R)]
    greet([(r, core), (r, ypeer), (r, diag)] + others)

    send_mix = remote(mix_out, mixy, mix_s.at[0], mix_r.at[0], (r, ypeer))
    send_mix.start()
    copies[0].wait()

    def red(k, step):
        reduce_event(stage.at[k], lambda d, s: rbuf.at[k, d, s], red_s, red_r, k, step, r, c, pos, R)

    red(0, 0)
    red(1, 0)
    for cp in copies[1:]:
        cp.wait()
    for cp in later:
        cp.start()
    gain1, shift1 = sm[0:1], sm[1:2]
    gain2, shift2 = sm[2:3], sm[3:4]
    router_b = sm[SMALL : SMALL + 8].astype(BF16)
    router3 = jnp.concatenate([router_b, router_b, router_b], axis=0)
    for g in range(C):
        wp[:, g * WH : (g + 1) * WH] = wg[g, :, :, W3:].reshape(D, WH)
    early[...] = jnp.zeros_like(early)
    late[...] = jnp.zeros_like(late)
    early[16:24, :] = bias_in[...]

    def pair(n):
        size = 16 if n < 2 else 24
        return remote(early.at[pl.ds(0, size)], sbuf.at[n, pl.ds(0, size)], sm_s.at[n], sm_r.at[n], pairs[n])

    def paired(n):
        size = 16 if n < 2 else 24
        pair(n).wait()
        early[0:size, :] = early[0:size, :] + sbuf[n, 0:size, :]
        if n + 1 < len(pairs):
            pair(n + 1).start()


    for h in range(MICRO):
        rp = rprob[h]
        p = gg[0, h]
        for e in range(1, E):
            p = p + gg[e, h]
        gl = rp * (p - jnp.sum(rp * p, axis=0, keepdims=True))
        hi = gl.astype(BF16)
        rest = gl - hi.astype(F32)
        mid = rest.astype(BF16)
        low = (rest - mid.astype(F32)).astype(BF16)
        gl3 = jnp.concatenate([hi.astype(F32), mid.astype(F32), low.astype(F32)], axis=0)
        gl3_t = gl3.T.astype(BF16)
        gl3 = gl3.astype(BF16)
        drt = jnp.zeros((24, D), F32)
        vecs = [jnp.zeros((1, D), F32) for _ in range(3)]
        for i in range(IMG_MB):
            at = h * BLK + i * IMG
            rows = slice(at, at + IMG)
            n2, inv2 = norm_rows(resid[rows, :])
            e2 = (n2 * gain2 + shift2).astype(BF16)
            drt = drt + dot_nn(gl3[:, i * IMG : (i + 1) * IMG], e2)
            ge2 = gp[0, rows, :].astype(F32) + gp[1, rows, :].astype(F32) + gp[2, rows, :].astype(F32)
            ge2 = ge2 + dot_nn(gl3_t[i * IMG : (i + 1) * IMG], router3)
            b = ge2 * gain2
            inner = b - jnp.mean(b, axis=-1, keepdims=True) - n2 * jnp.mean(b * n2, axis=-1, keepdims=True)
            gr = cot[rows, :].astype(F32) + inv2 * inner
            dres[rows, :] = gr
            g16 = gr.astype(BF16)
            gbr[rows, :] = g16
            vecs[0] = vecs[0] + jnp.sum(ge2 * n2, axis=0, keepdims=True)
            vecs[1] = vecs[1] + jnp.sum(ge2, axis=0, keepdims=True)
            vecs[2] = vecs[2] + jnp.sum(g16.astype(F32), axis=0, keepdims=True)
            for g in range(C):
                gm[g, rows, :] = dot_nt(g16, wp[g * WH : (g + 1) * WH, :]).astype(BF16)
            n1, _u = norm_rows(tok[rows, :].astype(F32))
            e1 = n1 * gain1 + shift1
            e1t[h * IMG_MB + i] = e1.T.astype(BF16)
        for n in range(3):
            early[n : n + 1, :] = early[n : n + 1, :] + vecs[n]
        early[8:16, :] = early[8:16, :] + drt[0:8] + drt[8:16] + drt[16:24]
        if h == 1:
            red(0, 1)
    get_mix = pltpu.make_async_copy(mix_parts, gp.at[pl.ds(0, 2)], loc.at[3])
    get_mix.start()
    pair(0).start()
    red(1, 1)
    for cp in later:
        cp.wait()
    for g in range(C):
        dp = dot_tn(mixed[g], gbr[...]).astype(BF16)
        for g2 in range(C):
            gblk[g2, g * WH : (g + 1) * WH, W3:] = dp[:, g2 * WH : (g2 + 1) * WH]

    order = [diag, ypeer, core, c]
    sends = []

    def close(k, peer):
        stage[k, r] = reduce_finish(
            stage.at[k], lambda d, s: rbuf.at[k, d, s], red_s, red_r, k, r, c, pos, R
        ).astype(BF16)
        cp = remote(stage.at[k, r], dexp.at[c], fin_s.at[k], fin_r.at[k], (r, peer))
        cp.start()
        sends.append(cp)

    for o in range(C):
        g = order[o]

        def image(i, vec, g=g):
            rows = pl.ds(pl.multiple_of(i * IMG, 16), IMG)
            z = qkv[g, rows, :]
            gmv = gm[g, rows, :]
            dq, dk, dv = [], [], []
            for h in range(heads):
                q = z[:, h * HEAD_DIM : (h + 1) * HEAD_DIM]
                kk = z[:, WH + h * HEAD_DIM : WH + (h + 1) * HEAD_DIM]
                v = z[:, 2 * WH + h * HEAD_DIM : 2 * WH + (h + 1) * HEAD_DIM]
                gmh = gmv[:, h * HEAD_DIM : (h + 1) * HEAD_DIM]
                p16 = probs[g, i, h]
                p = p16.astype(F32)
                w = dot_nt(gmh, v)
                ds = (p * (w - jnp.sum(p * w, axis=-1, keepdims=True))).astype(BF16)
                dq.append(dot_nn(ds, kk))
                dk.append(dot_tn(ds, q))
                dv.append(dot_tn(p16, gmh))
            d = jnp.concatenate(
                [v.astype(BF16).astype(F32) * SCALE for v in dq] + [v.astype(BF16).astype(F32) for v in dk + dv],
                axis=1,
            )
            dz[rows, :] = d.astype(BF16)
            w = wg[g, :, :, 0:W3].reshape(D, W3)
            part = dot_nt(d.astype(BF16), w)
            ge1[rows, :] = part if o == 0 else ge1[rows, :] + part
            return vec + jnp.sum(d, axis=0, keepdims=True)

        vec = lax.fori_loop(0, IMAGES, image, jnp.zeros((1, W3), F32))
        late[pl.ds(2 + g, 1), 0:W3] = vec
        for j in range(2):
            half = slice(j * (D // 2), (j + 1) * (D // 2))
            acc = jnp.zeros((D // 2, W3), F32)
            for i in range(IMAGES):
                acc = acc + dot_nn(e1t[i, half, :], dz[i * IMG : (i + 1) * IMG, :])
            gblk[g, half, 0:W3] = acc.astype(BF16)
        blk = gblk.at[g]
        if o == 0:
            cp = remote(blk, corein.at[0], ag_s.at[0], ag_r.at[0], (r, core))
            cp.start()
            sends.append(cp)
        elif o == 1:
            remote(blk, corein.at[0], ag_s.at[0], ag_r.at[0], (r, core)).wait_recv()
            blk[...] = (blk[...].astype(F32) + corein[0].astype(F32)).astype(BF16)
            cp = remote(blk, yin, ag_s.at[1], ag_r.at[1], (r, ypeer))
            cp.start()
            sends.append(cp)
        elif o == 2:
            cp = remote(blk, corein.at[1], ag_s.at[2], ag_r.at[2], (r, core))
            cp.start()
            sends.append(cp)
        paired(o)
        if o == 1:
            red(0, 2)
        elif o == 2:
            red(1, 2)
        elif o == 3:
            red(0, 3)
            red(1, 3)
            close(0, ypeer)
            close(1, diag)

    remote(gblk.at[c], corein.at[1], ag_s.at[2], ag_r.at[2], (r, core)).wait_recv()
    remote(gblk.at[c], yin, ag_s.at[1], ag_r.at[1], (r, ypeer)).wait_recv()
    for o in range(R):
        rows = slice(o * HB, (o + 1) * HB)
        tot = gblk[c, rows, :].astype(F32) + corein[1, rows, :].astype(F32) + yin[rows, :].astype(F32)
        apart[o, 0] = tot[0 : HB // 2].astype(BF16)
        apart[o, 1] = tot[HB // 2 :].astype(BF16)

    def ring(step):
        reduce_event(apart, lambda d, s: abuf.at[d, s], ar_s, ar_r, 0, step, r, c, pos, R)

    ring(0)

    def tight(dst, src):
        even = dst.shape[0] // 16 * 16
        dst[0:even, :] = src[0:even, :].astype(BF16)
        dst[even : dst.shape[0], :] = src[even : dst.shape[0], :].astype(BF16)

    dg = jnp.zeros((1, D), F32)
    dsh = jnp.zeros((1, D), F32)
    for i in range(IMAGES):
        rows = slice(i * IMG, (i + 1) * IMG)
        n1, inv1 = norm_rows(tok[rows, :].astype(F32))
        a = ge1[rows, :]
        b = a * gain1
        inner = b - jnp.mean(b, axis=-1, keepdims=True) - n1 * jnp.mean(b * n1, axis=-1, keepdims=True)
        full = dres[rows, :] + inv1 * inner
        dres[i * SEQ : (i + 1) * SEQ, :] = full[:SEQ]
        dg = dg + jnp.sum(a * n1, axis=0, keepdims=True)
        dsh = dsh + jnp.sum(a, axis=0, keepdims=True)
    tight(input_grad, dres)
    late[0:1, :] = dg
    late[1:2, :] = dsh
    cbuf[c] = late[...]
    firsts = [
        remote(late, cbuf.at[c], lc_s.at[n], lc_r.at[n], (r, peer)) for n, peer in enumerate((core, ypeer, diag))
    ]
    for cp in firsts:
        cp.start()
    for n in range(len(order), len(pairs)):
        paired(n)
    turned = pltpu.roll(early[...], lax.rem(D - r * HB, D), 1)
    early_id = lax.broadcasted_iota(jnp.int32, (24, 1), 0)
    n2_gain[...] = turned[0:1, :HB]
    n2_shift[...] = turned[1:2, :HB]
    router_out[...] = jnp.sum(jnp.where(early_id == 8 + c, turned, 0.0), axis=0, keepdims=True)[:, :HB]
    eob_out[...] = turned[16:17, :HB]
    pb_out[...] = pltpu.roll(early[...], lax.rem(D - c * WH, D), 1)[2:3, :WH]
    ff_row = jnp.where(early_id == 17 + lax.div(r * FFP, D), early[...], 0.0)
    ff_row = jnp.broadcast_to(jnp.sum(ff_row, axis=0, keepdims=True), (8, D))
    eib_out[...] = pltpu.roll(ff_row, lax.rem(D - lax.rem(r * FFP, D), D), 1)[0:1, :FFP]
    ring(1)
    for cp in firsts:
        cp.wait()
    tot = cbuf[0]
    for n in range(1, C):
        tot = tot + cbuf[n]
    late[...] = tot
    rbuf2[r] = tot
    seconds = [
        remote(late, rbuf2.at[r], lr_s.at[n], lr_r.at[n], peer) for n, peer in enumerate(others)
    ]
    for cp in seconds:
        cp.start()

    send_mix.wait()
    get_far = pltpu.make_async_copy(mixy, gp.at[2], loc.at[1])
    get_far.start()
    get_mix.wait()
    get_far.wait()
    for i in range(IMAGES):
        rows = slice(i * IMG, (i + 1) * IMG)
        o = resid[rows, :] + gp[0, rows, :].astype(F32) + gp[1, rows, :].astype(F32) + gp[2, rows, :].astype(F32)
        resid[i * SEQ : (i + 1) * SEQ, :] = o[:SEQ]
    tight(out, resid)
    ring(2)
    for cp in seconds:
        cp.wait()
    tot = rbuf2[0]
    for n in range(1, R):
        tot = tot + rbuf2[n]
    turned = pltpu.roll(tot, lax.rem(D - r * HB, D), 1)
    n1_gain[...] = turned[0:1, :HB]
    n1_shift[...] = turned[1:2, :HB]
    mine = jnp.sum(jnp.where(lax.broadcasted_iota(jnp.int32, (8, 1), 0) == 2 + c, tot, 0.0), axis=0, keepdims=True)
    ab_out[0:1, :] = mine[:, :WH]
    ab_out[1:2, :] = mine[:, 2 * WH : W3]
    ring(3)

    total = reduce_finish(apart, lambda d, s: abuf.at[d, s], ar_s, ar_r, 0, r, c, pos, R)
    attn_grad[...] = total.reshape(HB, D)
    for cp in sends:
        cp.wait_send()
    for k, peer in enumerate((ypeer, diag)):
        d_ref = dexp.at[peer]
        remote(d_ref, d_ref, fin_s.at[k], fin_r.at[k], (r, peer)).wait_recv()


def back(R, C, E, FFP, tok, cot, ge_parts, mix_parts, mix_out, gg, rprob, resid, qkv, mixed, probs, wg, sm, raw, bias):
    HB = D // R
    WH = D // C
    hops = R // 2
    vm = pl.BlockSpec(memory_space=pltpu.VMEM)
    hbm = pl.BlockSpec(memory_space=pl.ANY)
    sem = pltpu.SemaphoreType.DMA
    steps = 2 + int(math.log2(R))
    heads = WH // HEAD_DIM
    return pl.pallas_call(
        functools.partial(back_kernel, R, C, E, FFP),
        name="back",
        out_shape=(
            jax.ShapeDtypeStruct((IMAGES * SEQ, D), BF16),
            jax.ShapeDtypeStruct((IMAGES * SEQ, D), BF16),
            jax.ShapeDtypeStruct((HB, D), F32),
            jax.ShapeDtypeStruct((C, 2, HB, D), BF16),
            jax.ShapeDtypeStruct((ROWS, D), BF16),
            *[jax.ShapeDtypeStruct((1, HB), F32)] * 5,
            jax.ShapeDtypeStruct((1, WH), F32),
            jax.ShapeDtypeStruct((2, WH), F32),
            jax.ShapeDtypeStruct((1, FFP), F32),
            jax.ShapeDtypeStruct((1, HB), F32),
        ),
        in_specs=[vm, hbm, hbm, hbm, hbm, vm, vm, hbm, hbm, hbm, hbm, hbm, vm, hbm, vm],
        out_specs=(vm, vm, vm, hbm, hbm) + (vm,) * 9,
        scratch_shapes=[
            pltpu.VMEM((ROWS, D), BF16),
            pltpu.VMEM((C, R, HB, D), BF16),
            pltpu.VMEM((3, ROWS, D), BF16),
            pltpu.VMEM((ROWS, D), F32),
            pltpu.VMEM((C, ROWS, 3 * WH), BF16),
            pltpu.VMEM((C, ROWS, WH), BF16),
            pltpu.VMEM((C, IMAGES, heads, IMG, IMG), BF16),
            pltpu.VMEM((2, R, 2, HB, D), BF16),
            pltpu.VMEM((2, 2, hops, 2, HB, D), BF16),
            pltpu.VMEM((D, D), BF16),
            pltpu.VMEM((ROWS, D), BF16),
            pltpu.VMEM((ROWS, D), F32),
            pltpu.VMEM((C, ROWS, WH), BF16),
            pltpu.VMEM((IMAGES, D, IMG), BF16),
            pltpu.VMEM((ROWS, 3 * WH), BF16),
            pltpu.VMEM((ROWS, D), F32),
            pltpu.VMEM((C, D, D), BF16),
            pltpu.VMEM((2, D, D), BF16),
            pltpu.VMEM((D, D), BF16),
            pltpu.VMEM((R, 2, HB // 2, D), BF16),
            pltpu.VMEM((2, hops, 2, HB // 2, D), BF16),
            pltpu.VMEM((24, D), F32),
            pltpu.VMEM((8, D), F32),
            pltpu.VMEM((steps, 24, D), F32),
            pltpu.VMEM((C, 8, D), F32),
            pltpu.VMEM((R, 8, D), F32),
            sem((9,)),
            sem((2, 2, hops)), sem((2, 2, hops)),
            sem((2,)), sem((2,)),
            sem((1,)), sem((1,)),
            sem((3,)), sem((3,)),
            sem((1, 2, hops)), sem((1, 2, hops)),
            sem((steps,)), sem((steps,)),
            sem((C - 1,)), sem((C - 1,)),
            sem((R - 1,)), sem((R - 1,)),
        ],
        compiler_params=pltpu.CompilerParams(
            collective_id=3, has_side_effects=True, vmem_limit_bytes=62 << 20
        ),
    )(tok, cot, ge_parts, mix_parts, mix_out, gg, rprob, resid, qkv, mixed, probs, wg, sm, raw, bias)

def prepare(R, C, tokens, cotangent, routes, norm1_gain, norm1_shift, attn_in, attn_bias, attn_proj,
            proj_bias, norm2_gain, norm2_shift, router, expert_in, expert_in_bias, expert_out, expert_out_bias):
    HB, WH = D // R, D // C
    smalls = (
        norm1_gain[None], norm1_shift[None], norm2_gain[None], norm2_shift[None], attn_bias, proj_bias[None],
        router.reshape(1, HB), expert_out_bias, expert_in_bias,
    )
    packed = jnp.concatenate([attn_in.reshape(HB, 3 * WH), attn_proj], axis=1)
    wexp = jnp.stack([expert_in, jnp.swapaxes(expert_out, 1, 2)], axis=1)
    named = routes.astype(F32).T.reshape(2, IMAGES, SEQ)
    named = jnp.pad(named, ((0, 6), (0, 0), (0, IMG - SEQ)), constant_values=-1.0)
    rt = jnp.swapaxes(named.reshape(8, MICRO, BLK), 0, 1)
    return packed, smalls, wexp, rt

SPLIT = (4, 4, 1, 0)


def rings(
    tokens, cotangent, routes, norm1_gain, norm1_shift, attn_in, attn_bias, attn_proj, proj_bias,
    norm2_gain, norm2_shift, router, expert_in, expert_in_bias, expert_out, expert_out_bias,
):
    R, C = lax.axis_size("row"), lax.axis_size("col")
    E = expert_in.shape[0]
    HB, WH = D // R, D // C
    W3 = 3 * WH
    rows_mb = IMG_MB * SEQ
    cap = (2 * rows_mb * 13 // (10 * E) + 7) // 8 * 8
    cap = (cap + 15) // 16 * 16
    packed, smalls, wexp, rt = prepare(
        R, C, tokens, cotangent, routes, norm1_gain, norm1_shift, attn_in, attn_bias, attn_proj, proj_bias,
        norm2_gain, norm2_shift, router, expert_in, expert_in_bias, expert_out, expert_out_bias,
    )
    wbuf, e2_all, cot_all, info_all, tok, wg, qkv, mixed, probs, resid, rprob, sm = front(
        R, C, E, SPLIT, expert_in_bias.shape[1], tokens, cotangent, packed, smalls, wexp, rt
    )
    ge_parts, mix_parts, mix_out, gg, dexp_a, raw, _, bias = expert(
        R, C, cap, SPLIT, e2_all, cot_all, info_all, wbuf, sm
    )
    out, input_grad, attn_grad, dexp_b, _, n1g, n1s, n2g, n2s, grad_router, grad_pb, grad_ab, grad_eib, grad_eob = back(
        R, C, E, expert_in_bias.shape[1], tok, cot_all, ge_parts, mix_parts, mix_out, gg, rprob, resid, qkv, mixed, probs, wg, sm, raw, bias
    )
    c = lax.axis_index("col")
    e = lax.broadcasted_iota(jnp.int32, (E, 1, 1, 1), 0)
    near = lax.div(e, 2) == lax.div(c, 2)
    dexp = jnp.where(near, dexp_a, dexp_b).astype(F32)
    return (
        out,
        input_grad,
        n1g.reshape(HB),
        n1s.reshape(HB),
        attn_grad[:, :W3].reshape(HB, 3, WH),
        grad_ab,
        attn_grad[:, W3:],
        grad_pb.reshape(WH),
        n2g.reshape(HB),
        n2s.reshape(HB),
        grad_router.reshape(HB, 1),
        dexp[:, 0],
        grad_eib,
        jnp.swapaxes(dexp[:, 1], 1, 2),
        grad_eob,
    )


def solution(mesh):
    in_specs = (
        P(("row", "col"), None),
        P(("row", "col"), None),
        P(("row", "col"), None),
        P("row"),
        P("row"),
        P("row", None, "col"),
        P(None, "col"),
        P("row", "col"),
        P("col"),
        P("row"),
        P("row"),
        P("row", "col"),
        P(None, "row", "col"),
        P("col", "row"),
        P(None, "col", "row"),
        P("col", "row"),
    )
    out_specs = (
        P(("row", "col"), None),
        P(("row", "col"), None),
        P("row"),
        P("row"),
        P("row", None, "col"),
        P(None, "col"),
        P("row", "col"),
        P("col"),
        P("row"),
        P("row"),
        P("row", "col"),
        P(None, "row", "col"),
        P("col", "row"),
        P(None, "col", "row"),
        P("col", "row"),
    )
    body = rings if (mesh.shape["row"], mesh.shape["col"]) == (8, 4) else shards
    return jax.shard_map(body, mesh=mesh, in_specs=in_specs, out_specs=out_specs, check_vma=False)
```

```python
import functools
import math

import jax
import jax.numpy as jnp
from jax import lax
from jax.experimental import pallas as pl
from jax.experimental.pallas import tpu as pltpu
from jax.sharding import PartitionSpec as P

D = 768
HEADS = 12
HEAD_DIM = 64
SEQ = 197
IMG_MB = 2
MICRO = 2
IMAGES = IMG_MB * MICRO
IMG = (SEQ + 15) // 16 * 16
BLK = IMG_MB * IMG
ROWS = IMAGES * IMG
SCALE = HEAD_DIM ** (-0.5)
SMALL = 16
epsilon = 1e-06

MESH = pl.DeviceIdType.MESH
F32 = jnp.float32
BF16 = jnp.bfloat16
NT = (((1,), (1,)), ((), ()))
TN = (((0,), (0,)), ((), ()))


def dot_nn(a, b):
    return jnp.dot(a, b, preferred_element_type=F32)


def dot_nt(a, b):
    return lax.dot_general(a, b, NT, preferred_element_type=F32)


def dot_tn(a, b):
    return lax.dot_general(a, b, TN, preferred_element_type=F32)


def norm_rows(vals):
    centred = vals - jnp.mean(vals, axis=-1, keepdims=True)
    inv_std = lax.rsqrt(jnp.mean(centred * centred, axis=-1, keepdims=True) + epsilon)
    return centred * inv_std, inv_std


def ring_place(r, R):
    half = lax.rem(r, 2)
    return lax.div(r, 2) * (1 - half) + half * (R - 1 - lax.div(r, 2))


def ring_at(p, R):
    p = lax.rem(p + 2 * R, R)
    back = lax.div(p, R // 2)
    return (1 - back) * (2 * p) + back * (2 * (R - 1 - p) + 1)


def col_core(c):
    return c + 1 - 2 * lax.rem(c, 2)


def col_y(c):
    return c + 2 - 4 * lax.div(c, 2)


def col_diag(c):
    return 3 - c


def col_at(c, k):
    low = lax.rem(lax.rem(c, 2) + lax.rem(k, 2), 2)
    high = lax.rem(lax.div(c, 2) + lax.div(k, 2), 2)
    return low + 2 * high


def remote(src, dst, send, recv, dev):
    return pltpu.make_async_remote_copy(
        src_ref=src, dst_ref=dst, send_sem=send, recv_sem=recv, device_id=dev, device_id_type=MESH
    )


def greet(devs):
    bar = pltpu.get_barrier_semaphore()
    for dev in devs:
        pl.semaphore_signal(bar, inc=1, device_id=dev, device_id_type=MESH)
    pl.semaphore_wait(bar, len(devs))

def norm_forward(row_vals, norm_gain, norm_shift):
    centred = row_vals - jnp.mean(row_vals, axis=-1, keepdims=True)
    inv_std = lax.rsqrt(jnp.mean(centred * centred, axis=-1, keepdims=True) + epsilon)
    normed = centred * inv_std
    return (normed * norm_gain + norm_shift, normed, inv_std)


def norm_backward(grad_rows, normed, inv_std, norm_gain):
    scaled = grad_rows * norm_gain
    inner = (
        scaled
        - jnp.mean(scaled, axis=-1, keepdims=True)
        - normed * jnp.mean(scaled * normed, axis=-1, keepdims=True)
    )
    return (inv_std * inner, jnp.sum(grad_rows * normed, axis=0), jnp.sum(grad_rows, axis=0))


def gelu_exact(values):
    return jax.nn.gelu(values, approximate=False)


def shards(
    tokens,
    cotangent,
    routes,
    norm1_gain,
    norm1_shift,
    attn_in,
    attn_bias,
    attn_proj,
    proj_bias,
    norm2_gain,
    norm2_shift,
    router,
    expert_in,
    expert_in_bias,
    expert_out,
    expert_out_bias,
):
    experts_all = expert_in.shape[0]
    rows_mb = IMG_MB * SEQ
    capacity = (2 * rows_mb * 13 // (10 * experts_all) + 7) // 8 * 8
    scaling = HEAD_DIM ** (-0.5)
    head_shape = (IMG_MB, SEQ, HEADS, HEAD_DIM)
    stacked = jnp.stack([jnp.swapaxes(expert_in, 1, 2), expert_out])
    owned_cols = lax.all_to_all(stacked, "col", split_axis=1, concat_axis=2, tiled=True)
    norm_pack = jnp.stack([norm1_gain, norm1_shift, norm2_gain, norm2_shift])
    qkv_rows, proj_rows, router_rows, norm_full, owned, first_bias, second_bias = (
        lax.all_gather(attn_in, "row", axis=0, tiled=True),
        lax.all_gather(attn_proj, "row", axis=0, tiled=True),
        lax.all_gather(router, "row", axis=0, tiled=True),
        lax.all_gather(norm_pack, "row", axis=1, tiled=True),
        lax.all_gather(owned_cols, "row", axis=3, tiled=True),
        lax.all_gather(expert_in_bias, "row", axis=1, tiled=True),
        lax.all_gather(expert_out_bias, "row", axis=1, tiled=True),
    )
    qkv_full, proj_full, router_full, qv_bias, out_bias_vec = (
        lax.all_gather(qkv_rows, "col", axis=2, tiled=True),
        lax.all_gather(proj_rows, "col", axis=1, tiled=True),
        lax.all_gather(router_rows, "col", axis=1, tiled=True),
        lax.all_gather(attn_bias, "col", axis=1, tiled=True),
        lax.all_gather(proj_bias, "col", axis=0, tiled=True),
    )
    norms_wide = norm_full.astype(jnp.float32)
    gain_one, shift_one, gain_two, shift_two = (
        norms_wide[0],
        norms_wide[1],
        norms_wide[2],
        norms_wide[3],
    )
    qv_bias_wide = qv_bias.astype(jnp.float32)
    out_bias_wide = out_bias_vec.astype(jnp.float32)
    first_w = owned[0]
    second_w = owned[1]
    first_bias_wide = first_bias.astype(jnp.float32)[:, None, :]
    second_bias_wide = second_bias.astype(jnp.float32)[:, None, :]
    router_wide = router_full.astype(jnp.float32)
    expert_ids = jnp.arange(experts_all, dtype=jnp.int32)
    column_scale = jnp.array([scaling, 1.0, 1.0], jnp.float32)[None, :, None]
    exp_dev = owned.shape[1]
    acc_qkv = jnp.zeros(qkv_full.shape, jnp.float32)
    acc_proj = jnp.zeros(proj_full.shape, jnp.float32)
    acc_router = jnp.zeros(router_full.shape, jnp.float32)
    acc_qv = jnp.zeros(qv_bias.shape, jnp.float32)
    acc_out_bias = jnp.zeros(out_bias_vec.shape, jnp.float32)
    acc_norms = jnp.zeros(norm_full.shape, jnp.float32)
    acc_experts = (
        jnp.zeros((2, exp_dev, owned.shape[2], expert_in.shape[1]), jnp.float32),
        jnp.zeros(expert_in_bias.shape, jnp.float32),
        jnp.zeros(expert_out_bias.shape, jnp.float32),
    )
    outputs = []
    input_grads = []
    for batch_index in range(MICRO):
        offset = batch_index * rows_mb
        row_vals = tokens[offset : offset + rows_mb].astype(jnp.float32)
        grad_out = cotangent[offset : offset + rows_mb].astype(jnp.float32)
        route_mb = routes[offset : offset + rows_mb]
        normed_out1, normed1, inv_std1 = norm_forward(row_vals, gain_one, shift_one)
        entry1 = normed_out1.astype(jnp.bfloat16)
        projected = jnp.einsum("td,dje->tje", entry1, qkv_full, preferred_element_type=jnp.float32)
        query_rows = (
            ((projected[:, 0] + qv_bias_wide[0]) * scaling).astype(jnp.bfloat16).reshape(head_shape)
        )
        key_rows = projected[:, 1].astype(jnp.bfloat16).reshape(head_shape)
        value_rows = (projected[:, 2] + qv_bias_wide[1]).astype(jnp.bfloat16).reshape(head_shape)
        scores = jnp.einsum(
            "ishd,ijhd->ihsj", query_rows, key_rows, preferred_element_type=jnp.float32
        )
        row_peak = jnp.max(scores, axis=-1, keepdims=True)
        exp_scores = jnp.exp(scores - row_peak)
        totals = jnp.sum(exp_scores, axis=-1, keepdims=True)
        attn_probs = exp_scores / totals
        log_totals = row_peak + jnp.log(totals)
        attn_mixed = (
            jnp.einsum(
                "ihsj,ijhd->ishd",
                attn_probs.astype(jnp.bfloat16),
                value_rows,
                preferred_element_type=jnp.float32,
            )
            .reshape(rows_mb, D)
            .astype(jnp.bfloat16)
        )
        branch = jnp.dot(attn_mixed, proj_full, preferred_element_type=jnp.float32) + out_bias_wide
        resid = row_vals + branch
        normed_out2, normed2, inv_std2 = norm_forward(resid, gain_two, shift_two)
        entry2 = normed_out2.astype(jnp.bfloat16)
        logits = jnp.dot(entry2, router_full, preferred_element_type=jnp.float32)
        router_probs = jax.nn.softmax(logits, axis=-1)
        chosen = route_mb[:, :, None] == expert_ids[None, None, :]
        gate_values = jnp.sum(jnp.where(chosen, router_probs[:, None, :], 0.0), axis=-1)
        route_flags = chosen.reshape(2 * rows_mb, experts_all).astype(jnp.int32)
        before = jnp.cumsum(route_flags, axis=0) - route_flags
        target = route_mb.reshape(-1) * capacity + jnp.sum(before * route_flags, axis=-1)
        outgoing = (
            jnp.zeros((experts_all * capacity, D), jnp.bfloat16)
            .at[target]
            .set(jnp.repeat(entry2, 2, axis=0))
        )
        arrived = lax.all_to_all(
            outgoing.reshape(experts_all, capacity, D),
            "col",
            split_axis=0,
            concat_axis=1,
            tiled=True,
        )
        pre_act = (
            jnp.einsum("erd,efd->erf", arrived, first_w, preferred_element_type=jnp.float32)
            + first_bias_wide
        )
        active = gelu_exact(pre_act).astype(jnp.bfloat16)
        result = (
            jnp.einsum("erf,efd->erd", active, second_w, preferred_element_type=jnp.float32)
            + second_bias_wide
        ).astype(jnp.bfloat16)
        returned = lax.all_to_all(result, "col", split_axis=1, concat_axis=0, tiled=True).reshape(
            experts_all * capacity, D
        )
        picked = returned[target].reshape(rows_mb, 2, D).astype(jnp.float32)
        outputs.append(
            (resid + jnp.sum(gate_values[:, :, None] * picked, axis=1)).astype(jnp.bfloat16)
        )
        grad_gates = jnp.sum(grad_out[:, None, :] * picked, axis=-1)
        grad_sent = (
            (gate_values[:, :, None] * grad_out[:, None, :])
            .astype(jnp.bfloat16)
            .reshape(2 * rows_mb, D)
        )
        grad_outgoing = (
            jnp.zeros((experts_all * capacity, D), jnp.bfloat16).at[target].set(grad_sent)
        )
        grad_result = lax.all_to_all(
            grad_outgoing.reshape(experts_all, capacity, D),
            "col",
            split_axis=0,
            concat_axis=1,
            tiled=True,
        )
        grad_active = jnp.einsum(
            "erd,efd->erf", grad_result, second_w, preferred_element_type=jnp.float32
        )
        grad_pre = jax.vjp(gelu_exact, pre_act)[1](grad_active)[0].astype(jnp.bfloat16)
        weight_terms = jnp.stack(
            [
                jnp.einsum("erf,erd->efd", grad_pre, arrived, preferred_element_type=jnp.float32),
                jnp.einsum("erf,erd->efd", active, grad_result, preferred_element_type=jnp.float32),
            ]
        )
        in_bias_terms = jnp.sum(grad_pre.astype(jnp.float32), axis=1)
        out_bias_terms = jnp.sum(grad_result.astype(jnp.float32), axis=1)
        weight_piece, in_bias_piece, out_bias_piece = (
            lax.psum_scatter(
                weight_terms.astype(jnp.bfloat16), "row", scatter_dimension=3, tiled=True
            ).astype(jnp.float32),
            lax.psum_scatter(
                in_bias_terms.astype(jnp.bfloat16), "row", scatter_dimension=1, tiled=True
            ).astype(jnp.float32),
            lax.psum_scatter(
                out_bias_terms.astype(jnp.bfloat16), "row", scatter_dimension=1, tiled=True
            ).astype(jnp.float32),
        )
        acc_experts = (
            acc_experts[0] + weight_piece,
            acc_experts[1] + in_bias_piece,
            acc_experts[2] + out_bias_piece,
        )
        grad_entry = jnp.einsum(
            "erf,efd->erd", grad_pre, first_w, preferred_element_type=jnp.float32
        ).astype(jnp.bfloat16)
        grad_back = lax.all_to_all(
            grad_entry, "col", split_axis=1, concat_axis=0, tiled=True
        ).reshape(experts_all * capacity, D)
        grad_entry2 = jnp.sum(grad_back[target].reshape(rows_mb, 2, D).astype(jnp.float32), axis=1)
        grad_probs = jnp.sum(jnp.where(chosen, grad_gates[:, :, None], 0.0), axis=1)
        grad_logits = router_probs * (
            grad_probs - jnp.sum(router_probs * grad_probs, axis=-1, keepdims=True)
        )
        grad_entry2 = grad_entry2 + jnp.dot(
            grad_logits, router_wide.T, precision=lax.Precision.HIGHEST
        )
        acc_router = acc_router + jnp.dot(
            entry2.astype(jnp.float32).T, grad_logits, precision=lax.Precision.HIGHEST
        )
        grad_norm2, gain_two_grad, shift_two_grad = norm_backward(
            grad_entry2, normed2, inv_std2, gain_two
        )
        grad_resid = grad_out + grad_norm2
        grad_branch = grad_resid.astype(jnp.bfloat16)
        acc_proj = acc_proj + jnp.einsum(
            "td,te->de", attn_mixed, grad_branch, preferred_element_type=jnp.float32
        )
        acc_out_bias = acc_out_bias + jnp.sum(grad_branch.astype(jnp.float32), axis=0)
        grad_mixed = (
            jnp.einsum("te,de->td", grad_branch, proj_full, preferred_element_type=jnp.float32)
            .astype(jnp.bfloat16)
            .reshape(head_shape)
        )
        scores_again = jnp.einsum(
            "ishd,ijhd->ihsj", query_rows, key_rows, preferred_element_type=jnp.float32
        )
        probs_again = jnp.exp(scores_again - log_totals)
        grad_weights = jnp.einsum(
            "ishd,ijhd->ihsj", grad_mixed, value_rows, preferred_element_type=jnp.float32
        )
        grad_values = jnp.einsum(
            "ihsj,ishd->ijhd",
            probs_again.astype(jnp.bfloat16),
            grad_mixed,
            preferred_element_type=jnp.float32,
        )
        inner_sum = jnp.sum(probs_again * grad_weights, axis=-1, keepdims=True)
        grad_scores = (probs_again * (grad_weights - inner_sum)).astype(jnp.bfloat16)
        grad_query = jnp.einsum(
            "ihsj,ijhd->ishd", grad_scores, key_rows, preferred_element_type=jnp.float32
        )
        grad_keys = jnp.einsum(
            "ihsj,ishd->ijhd", grad_scores, query_rows, preferred_element_type=jnp.float32
        )
        grad_qkv = jnp.stack(
            [
                grad_query.reshape(rows_mb, D),
                grad_keys.reshape(rows_mb, D),
                grad_values.reshape(rows_mb, D),
            ],
            axis=1,
        ).astype(jnp.bfloat16)
        acc_qkv = (
            acc_qkv
            + jnp.einsum("td,tje->dje", entry1, grad_qkv, preferred_element_type=jnp.float32)
            * column_scale
        )
        grad_sums = jnp.sum(grad_qkv.astype(jnp.float32), axis=0)
        acc_qv = acc_qv + jnp.stack([grad_sums[0] * scaling, grad_sums[2]])
        grad_entry1 = jnp.sum(
            jnp.einsum("tje,dje->tjd", grad_qkv, qkv_full, preferred_element_type=jnp.float32)
            * column_scale,
            axis=1,
        )
        grad_norm1, gain_one_grad, shift_one_grad = norm_backward(
            grad_entry1, normed1, inv_std1, gain_one
        )
        input_grads.append((grad_resid + grad_norm1).astype(jnp.bfloat16))
        acc_norms = acc_norms + jnp.stack(
            [gain_one_grad, shift_one_grad, gain_two_grad, shift_two_grad]
        )
    qkv_grad, proj_grad, router_grad, qv_grad, out_bias_grad = (
        lax.psum_scatter(acc_qkv, "col", scatter_dimension=2, tiled=True),
        lax.psum_scatter(acc_proj, "col", scatter_dimension=1, tiled=True),
        lax.psum_scatter(acc_router, "col", scatter_dimension=1, tiled=True),
        lax.psum_scatter(acc_qv, "col", scatter_dimension=1, tiled=True),
        lax.psum_scatter(acc_out_bias, "col", scatter_dimension=0, tiled=True),
    )
    qv_grad, out_bias_grad = lax.psum((qv_grad, out_bias_grad), "row")
    qkv_grad, proj_grad, router_grad, norm_grad = (
        lax.psum_scatter(
            qkv_grad.astype(jnp.bfloat16), "row", scatter_dimension=0, tiled=True
        ).astype(jnp.float32),
        lax.psum_scatter(
            proj_grad.astype(jnp.bfloat16), "row", scatter_dimension=0, tiled=True
        ).astype(jnp.float32),
        lax.psum_scatter(
            router_grad.astype(jnp.bfloat16), "row", scatter_dimension=0, tiled=True
        ).astype(jnp.float32),
        lax.psum_scatter(
            acc_norms.astype(jnp.bfloat16), "row", scatter_dimension=1, tiled=True
        ).astype(jnp.float32),
    )
    expert_stack, in_bias_grad, out_bias_expert = acc_experts
    norm_grad = lax.psum(norm_grad, "col")
    expert_blocks = lax.all_to_all(
        expert_stack.astype(jnp.bfloat16), "col", split_axis=2, concat_axis=1, tiled=True
    ).astype(expert_stack.dtype)
    return (
        jnp.concatenate(outputs, axis=0),
        jnp.concatenate(input_grads, axis=0),
        norm_grad[0],
        norm_grad[1],
        qkv_grad,
        qv_grad,
        proj_grad,
        out_bias_grad,
        norm_grad[2],
        norm_grad[3],
        router_grad,
        jnp.swapaxes(expert_blocks[0], 1, 2),
        in_bias_grad,
        expert_blocks[1],
        out_bias_expert,
    )

def ring_event(buf_of, sends, recvs, flow, step, r, c, pos, R, source_of=None, first=0):
    right, left = ring_at(pos + 1, R), ring_at(pos - 1, R)
    hops = R // 2
    from_left, from_right = ring_at(pos - step, R), ring_at(pos + step, R)
    a, b = buf_of(from_left), buf_of(from_right)
    if step > first:
        remote(a, a, sends.at[flow, 0, step - 1], recvs.at[flow, 0, step - 1], (right, c)).wait_recv()
        remote(b, b, sends.at[flow, 1, step - 1], recvs.at[flow, 1, step - 1], (left, c)).wait_recv()
    at_a, at_b = a, b
    if step == first and source_of is not None:
        at_a, at_b = source_of(from_left), source_of(from_right)
    if step == hops - 1:
        a, b, at_a, at_b = a.at[0], b.at[1], at_a.at[0], at_b.at[1]
    remote(at_a, a, sends.at[flow, 0, step], recvs.at[flow, 0, step], (right, c)).start()
    remote(at_b, b, sends.at[flow, 1, step], recvs.at[flow, 1, step], (left, c)).start()


def ring_finish(buf_of, sends, recvs, flow, r, c, pos, R, first, last):
    right, left = ring_at(pos + 1, R), ring_at(pos - 1, R)
    hops = R // 2
    if last > first:
        a, b = buf_of(ring_at(pos - last, R)), buf_of(ring_at(pos + last, R))
        if last == hops:
            a, b = a.at[0], b.at[1]
        remote(a, a, sends.at[flow, 0, last - 1], recvs.at[flow, 0, last - 1], (right, c)).wait_recv()
        remote(b, b, sends.at[flow, 1, last - 1], recvs.at[flow, 1, last - 1], (left, c)).wait_recv()
    own = buf_of(r)
    for step in range(first, last):
        a, b = (own, own) if step < hops - 1 else (own.at[0], own.at[1])
        remote(a, a, sends.at[flow, 0, step], recvs.at[flow, 0, step], (right, c)).wait_send()
        remote(b, b, sends.at[flow, 1, step], recvs.at[flow, 1, step], (left, c)).wait_send()


def front_kernel(
    R, C, E, SPLIT, FFP,
    tok, cot_in, packed, g1, s1, g2, s2, qv_bias, p_bias, router_col, out_bias, in_bias, wexp, rt,
    wbuf, e2_all, cot_all, info_all, tok_out, wg_out, qkv_out, mixed_out, probs_out, resid_out, rprob, sm_out,
    pack, flat, tokp, cot, wg, norm1, e2, wp, info, qkv, mixed, probs, resid,
    ring_s, ring_r, yring_s, yring_r, fan_s, fan_r, y_s, y_r,
    a2a_s, a2a_r, flow_s, flow_r, cot_s, cot_r, e2_s, e2_r, inf_s, inf_r, loc, keep_sem,
):
    r, c = lax.axis_index("row"), lax.axis_index("col")
    pos = ring_place(r, R)
    hops = R // 2
    right, left = ring_at(pos + 1, R), ring_at(pos - 1, R)
    core, ypeer, diag = col_core(c), col_y(c), col_diag(c)
    HB = D // R
    pack[0:HB, :] = packed[...]
    wide = []
    for ref in (g1, s1, g2, s2, qv_bias, p_bias, router_col, out_bias, in_bias):
        v = ref[...].astype(F32)
        wide.append(jnp.concatenate([v, jnp.zeros((v.shape[0], D - v.shape[1]), F32)], axis=1))
    wide.append(jnp.zeros((SMALL - 10, D), F32))
    vecs = jnp.concatenate(wide, axis=0)
    row_id = lax.broadcasted_iota(jnp.int32, (SMALL, D), 0)
    turned = pltpu.roll(vecs, r * HB, 1)
    inner = jnp.sum(jnp.where(row_id == 9, vecs, 0.0), axis=0, keepdims=True)
    inner = pltpu.roll(jnp.broadcast_to(inner, (SMALL, D)), lax.rem(r * FFP, D), 1)
    placed = jnp.where((row_id >= 4) & (row_id < 7), vecs, turned)
    placed = jnp.where(row_id < 9, placed, jnp.where(row_id == 9 + lax.div(r * FFP, D), inner, 0.0))
    pack[HB : HB + SMALL, :] = placed.astype(BF16)
    greet([(right, c), (left, c), (r, core), (r, ypeer), (r, diag)])
    HALF = 64
    TAIL = pack.shape[0] - HALF
    HB, WH = D // R, D // C
    W3 = 3 * WH
    heads = WH // HEAD_DIM

    at_l = [ring_at(pos - s, R) for s in range(hops + 1)]
    at_r = [ring_at(pos + s, R) for s in range(hops + 1)]
    rows_by = [r]
    for s in range(1, hops):
        rows_by += [at_l[s], at_r[s]]
    rows_by.append(at_l[hops])

    def fan(kind, j, col):
        blk = wg.at[col, rows_by[j]]
        return remote(blk, blk, fan_s.at[kind, j], fan_r.at[kind, j], (r, core))

    def over_y(n, j, col):
        blk = wg.at[col, rows_by[j]]
        return remote(blk, blk, y_s.at[n], y_r.at[n], (r, ypeer))

    def own_ring(d, s, blk):
        if s == hops - 1:
            blk = blk.at[pl.ds(0, HALF)] if d == 0 else blk.at[pl.ds(HALF, TAIL)]
        return remote(blk, blk, ring_s.at[d, s], ring_r.at[d, s], (right if d == 0 else left, c))

    def far_ring(d, s, blk):
        if s == hops - 1:
            blk = blk.at[pl.ds(0, HALF)] if d == 0 else blk.at[pl.ds(HALF, TAIL)]
        return remote(blk, blk, yring_s.at[d, s], yring_r.at[d, s], (right if d == 0 else left, c))

    own = wg.at[c, r]
    remote(pack, own, ring_s.at[0, 0], ring_r.at[0, 0], (right, c)).start()
    remote(pack, own, ring_s.at[1, 0], ring_r.at[1, 0], (left, c)).start()
    remote(pack, own, y_s.at[0], y_r.at[0], (r, ypeer)).start()
    remote(pack, own, fan_s.at[0, 0], fan_r.at[0, 0], (r, core)).start()
    own_pack = pltpu.make_async_copy(pack, own, loc.at[0])
    own_pack.start()
    own_exp = pltpu.make_async_copy(wexp.at[c], wbuf.at[c, r], loc.at[1])
    own_exp.start()
    peers = [core, ypeer, diag]

    def a2a(n):
        return remote(wexp.at[peers[n]], wbuf.at[c, r], a2a_s.at[n], a2a_r.at[n], (r, peers[n]))

    def a2a_in(n):
        blk = wbuf.at[peers[n], r]
        return remote(blk, blk, a2a_s.at[n], a2a_r.at[n], (r, peers[n]))

    a2a(0).start()

    real = lax.broadcasted_iota(jnp.int32, (IMG, 1), 0) < SEQ
    even = tok.shape[0] // 16 * 16

    def images(src):
        flat[0:even, :] = src[0:even, :].astype(F32)
        flat[even : src.shape[0], :] = src[even : src.shape[0], :].astype(F32)
        for i in range(IMAGES):
            yield i, jnp.where(real, flat[i * SEQ : i * SEQ + IMG, :], 0.0)

    for i, rows in images(cot_in):
        cot[i * IMG : (i + 1) * IMG, :] = rows.astype(BF16)
    own_cot = pltpu.make_async_copy(cot, cot_all.at[c], loc.at[2])
    own_cot.start()
    for i, rows in images(tok):
        tokp[i * IMG : (i + 1) * IMG, :] = rows.astype(BF16)
        norm1[i * IMG : (i + 1) * IMG, :] = norm_rows(rows)[0]
    own_tok = pltpu.make_async_copy(tokp, tok_out, loc.at[5 + IMAGES])
    own_tok.start()

    over_y(0, 0, ypeer).wait_recv()
    far_ring(0, 0, wg.at[ypeer, r]).start()
    far_ring(1, 0, wg.at[ypeer, r]).start()
    fan(1, 0, ypeer).start()
    remote(cot, cot_all.at[c], cot_s.at[1], cot_r.at[1], (r, ypeer)).start()
    for s in range(1, hops + 1):
        for ring, col, kind in ((own_ring, c, 0), (far_ring, ypeer, 1)):
            for d, o in enumerate((at_l[s], at_r[s])):
                blk = wg.at[col, o]
                ring(d, s - 1, blk).wait_recv()
                if s < hops:
                    ring(d, s, blk).start()
            fan(kind, 2 * s - 1, col).start()
            if s < hops:
                fan(kind, 2 * s, col).start()
        if s == 2:
            a2a(1).start()
            a2a(2).start()
    own_pack.wait()
    own_exp.wait()

    def flow_buf(k):
        f = col_at(c, k)
        return lambda o: wbuf.at[f, o]

    def gather(k, s):
        if s < SPLIT[k]:
            ring_event(flow_buf(k), flow_s, flow_r, k, s, r, c, pos, R)

    gather(0, 0)
    a2a_in(0).wait_recv()
    gather(1, 0)
    remote(cot, cot_all.at[c], cot_s.at[0], cot_r.at[0], (r, core)).start()
    for j in range(R):
        fan(0, j, core).wait_recv()
        fan(1, j, diag).wait_recv()
    send_wg = pltpu.make_async_copy(wg, wg_out, loc.at[3])
    send_wg.start()

    own_small = jnp.zeros((SMALL, D), F32)
    for o in range(R):
        own_small = own_small + wg[c, o, HB : HB + SMALL, :].astype(F32)
    gain1, shift1 = own_small[0:1], own_small[1:2]
    gain2, shift2 = own_small[2:3], own_small[3:4]
    lane = lax.broadcasted_iota(jnp.int32, (1, W3), 1)
    col_scale = jnp.where(lane < WH, SCALE, 1.0).astype(F32)
    keep = lax.broadcasted_iota(jnp.int32, (1, IMG), 1) < SEQ
    rtr, pb, biases = [], [], []
    for g in range(C):
        wp[:, g * WH : (g + 1) * WH] = wg[g, :, 0:HB, W3:].reshape(D, WH)
        small = wg[g, 0, HB : HB + SMALL, :].astype(F32)
        bq, bv = small[4:5, :WH], small[5:6, :WH]
        biases.append(jnp.concatenate([bq, jnp.zeros_like(bq), bv], axis=1))
        pb.append(small[6:7, :WH])
        acc = jnp.zeros((1, D), F32)
        for o in range(R):
            acc = acc + wg[g, o, HB : HB + SMALL, :].astype(F32)[7:8]
        rtr.append(acc)
    pbias = jnp.concatenate(pb, axis=1)
    router_t = jnp.concatenate(rtr + [jnp.zeros((8 - C, D), F32)], axis=0)
    sm_out[0:SMALL, :] = own_small
    sm_out[SMALL : SMALL + 8, :] = router_t
    router_b = router_t.astype(BF16)
    upper = (
        lax.broadcasted_iota(jnp.int32, (BLK, BLK), 0) < lax.broadcasted_iota(jnp.int32, (BLK, BLK), 1)
    ).astype(BF16)
    exp_id = lax.broadcasted_iota(jnp.int32, (8, BLK), 0)

    def e2_copy(n, i, who, peer):
        part = pl.ds(i * IMG, IMG)
        src = e2.at[part] if n < 2 else e2_all.at[who, part]
        return remote(src, e2_all.at[who, part], e2_s.at[n, i], e2_r.at[n, i], (r, peer))

    locals_ = []
    for i in range(IMAGES):
        rows = slice(i * IMG, (i + 1) * IMG)
        entry1 = (norm1[rows, :] * gain1 + shift1).astype(BF16)
        acc = tokp[rows, :].astype(F32) + pbias
        for g in range(C):
            w = wg[g, :, 0:HB, 0:W3].reshape(D, W3)
            z = ((dot_nn(entry1, w) + biases[g]) * col_scale).astype(BF16)
            qkv[g, rows, :] = z
            outs = []
            for h in range(heads):
                q = z[:, h * HEAD_DIM : (h + 1) * HEAD_DIM]
                kk = z[:, WH + h * HEAD_DIM : WH + (h + 1) * HEAD_DIM]
                v = z[:, 2 * WH + h * HEAD_DIM : 2 * WH + (h + 1) * HEAD_DIM]
                s = jnp.where(keep, dot_nt(q, kk), -1e30)
                ex = jnp.exp(s - jnp.max(s, axis=-1, keepdims=True))
                p = (ex / jnp.sum(ex, axis=-1, keepdims=True)).astype(BF16)
                probs[g, i, h] = p
                outs.append(dot_nn(p, v))
            mix = jnp.concatenate(outs, axis=1).astype(BF16)
            mixed[g, rows, :] = mix
            acc = acc + dot_nn(mix, wp[g * WH : (g + 1) * WH, :])
        resid[rows, :] = acc
        e2[rows, :] = (norm_rows(acc)[0] * gain2 + shift2).astype(BF16)
        e2_copy(1, i, c, ypeer).start()
        e2_copy(0, i, c, core).start()
        part = pl.ds(i * IMG, IMG)
        cp = pltpu.make_async_copy(e2.at[part], e2_all.at[c, part], loc.at[4 + i])
        cp.start()
        locals_.append(cp)
        for n, (src, dst) in enumerate((
            (qkv.at[:, part], qkv_out.at[:, part]),
            (mixed.at[:, part], mixed_out.at[:, part]),
            (probs.at[:, i], probs_out.at[:, i]),
            (resid.at[part], resid_out.at[part]),
        )):
            cp = pltpu.make_async_copy(src, dst, keep_sem.at[n, i])
            cp.start()
            locals_.append(cp)
        if i % IMG_MB == IMG_MB - 1:
            h = i // IMG_MB
            blk = e2[h * BLK : (h + 1) * BLK, :]
            logits = jnp.where(exp_id < E, dot_nt(router_b, blk), -1e30)
            ex = jnp.exp(logits - jnp.max(logits, axis=0, keepdims=True))
            prob = ex / jnp.sum(ex, axis=0, keepdims=True)
            rprob[h] = prob
            named = rt[h]
            member = (named[0:1] == exp_id.astype(F32)) | (named[1:2] == exp_id.astype(F32))
            flags = jnp.where(member, 1.0, 0.0)
            rank = dot_nn(flags.astype(BF16), upper)
            info[h, 0:8, :] = jnp.where(member, rank, -1.0)
            info[h, 8:16, :] = jnp.where(member, prob, 0.0)
        if i == IMAGES - 1:
            cp = pltpu.make_async_copy(info, info_all.at[c], loc.at[4 + IMAGES])
            cp.start()
            locals_.append(cp)
            for n, peer in enumerate(peers):
                remote(info, info_all.at[c], inf_s.at[n], inf_r.at[n], (r, peer)).start()
        if i == 1:
            gather(0, 1)
        if i == 2:
            gather(1, 1)

    def relay(i):
        e2_copy(1, i, ypeer, ypeer).wait_recv()
        e2_copy(2, i, ypeer, core).start()

    relay(0)
    remote(cot, cot_all.at[ypeer], cot_s.at[1], cot_r.at[1], (r, ypeer)).wait_recv()
    remote(cot_all.at[ypeer], cot_all.at[ypeer], cot_s.at[2], cot_r.at[2], (r, core)).start()
    gather(0, 2)
    relay(1)
    gather(1, 2)
    for n in (1, 2):
        a2a_in(n).wait_recv()
    gather(2, 0)
    relay(2)
    gather(0, 3)
    gather(1, 3)
    relay(3)
    gather(2, 1)

    for n, who in ((0, core), (2, diag)):
        blk = cot_all.at[who]
        remote(blk, blk, cot_s.at[n], cot_r.at[n], (r, core)).wait_recv()
    for n in range(3):
        remote(cot, cot_all.at[c], cot_s.at[n], cot_r.at[n], (r, core)).wait_send()
    for i in range(IMAGES):
        e2_copy(0, i, core, core).wait_recv()
        e2_copy(2, i, diag, core).wait_recv()
        for n in range(3):
            e2_copy(n, i, c, core).wait_send()
    for n, peer in enumerate(peers):
        cp = remote(info, info_all.at[peer], inf_s.at[n], inf_r.at[n], (r, peer))
        cp.wait_recv()
        cp.wait_send()
        a2a(n).wait_send()
    for j in range(R):
        fan(0, j, c).wait_send()
        fan(1, j, c).wait_send()
    over_y(0, 0, c).wait_send()
    for d in range(2):
        for s in range(hops):
            own_ring(d, s, own).wait_send()
            far_ring(d, s, own).wait_send()
    for k in range(C):
        ring_finish(flow_buf(k), flow_s, flow_r, k, r, c, pos, R, 0, SPLIT[k])
    own_cot.wait()
    own_tok.wait()
    send_wg.wait()
    for cp in locals_:
        cp.wait()


def front(R, C, E, SPLIT, FFP, tok, cot, packed, smalls, wexp, rt):
    WH = D // C
    HB = D // R
    hops = R // 2
    vm = pl.BlockSpec(memory_space=pltpu.VMEM)
    hbm = pl.BlockSpec(memory_space=pl.ANY)
    sem = pltpu.SemaphoreType.DMA
    heads = WH // HEAD_DIM
    return pl.pallas_call(
        functools.partial(front_kernel, R, C, E, SPLIT, FFP),
        name="front",
        out_shape=(
            jax.ShapeDtypeStruct((C, R, 2, HB, D), BF16),
            jax.ShapeDtypeStruct((C, ROWS, D), BF16),
            jax.ShapeDtypeStruct((C, ROWS, D), BF16),
            jax.ShapeDtypeStruct((C, MICRO, 16, BLK), F32),
            jax.ShapeDtypeStruct((ROWS, D), BF16),
            jax.ShapeDtypeStruct((C, R, HB + SMALL, D), BF16),
            jax.ShapeDtypeStruct((C, ROWS, 3 * WH), BF16),
            jax.ShapeDtypeStruct((C, ROWS, WH), BF16),
            jax.ShapeDtypeStruct((C, IMAGES, heads, IMG, IMG), BF16),
            jax.ShapeDtypeStruct((ROWS, D), F32),
            jax.ShapeDtypeStruct((MICRO, 8, BLK), F32),
            jax.ShapeDtypeStruct((SMALL + 8, D), F32),
        ),
        in_specs=[vm] * (5 + len(smalls)),
        out_specs=(hbm,) * 10 + (vm, vm),
        scratch_shapes=[
            pltpu.VMEM((HB + SMALL, D), BF16),
            pltpu.VMEM(((IMAGES - 1) * SEQ + IMG + 1, D), F32),
            pltpu.VMEM((ROWS, D), BF16),
            pltpu.VMEM((ROWS, D), BF16),
            pltpu.VMEM((C, R, HB + SMALL, D), BF16),
            pltpu.VMEM((ROWS, D), F32),
            pltpu.VMEM((ROWS, D), BF16),
            pltpu.VMEM((D, D), BF16),
            pltpu.VMEM((MICRO, 16, BLK), F32),
            pltpu.VMEM((C, ROWS, 3 * WH), BF16),
            pltpu.VMEM((C, ROWS, WH), BF16),
            pltpu.VMEM((C, IMAGES, heads, IMG, IMG), BF16),
            pltpu.VMEM((ROWS, D), F32),
            sem((2, hops)), sem((2, hops)),
            sem((2, hops)), sem((2, hops)),
            sem((2, R)), sem((2, R)),
            sem((1,)), sem((1,)),
            sem((3,)), sem((3,)),
            sem((C, 2, hops)), sem((C, 2, hops)),
            sem((3,)), sem((3,)),
            sem((3, IMAGES)), sem((3, IMAGES)),
            sem((3,)), sem((3,)),
            sem((6 + IMAGES,)), sem((4, IMAGES)),
        ],
        compiler_params=pltpu.CompilerParams(
            collective_id=1, has_side_effects=True, vmem_limit_bytes=56 << 20
        ),
    )(tok, cot, packed, *smalls, wexp, rt)

def reduce_event(parts, rbuf, sends, recvs, slot, step, r, c, pos, R):
    right, left = ring_at(pos + 1, R), ring_at(pos - 1, R)
    hops = R // 2
    to_right, to_left = ring_at(pos + hops - step, R), ring_at(pos - hops + step, R)
    for d, (dest, peer) in enumerate(((to_right, right), (to_left, left))):
        if step > 0:
            got = rbuf(d, step - 1)
            if step == 1:
                got, mine = got.at[d], parts.at[dest, d]
            else:
                mine = parts.at[dest]
            remote(got, got, sends.at[slot, d, step - 1], recvs.at[slot, d, step - 1], (peer, c)).wait_recv()
            mine[...] = (mine[...].astype(F32) + got[...].astype(F32)).astype(BF16)
        src, dst = parts.at[dest], rbuf(d, step)
        if step == 0:
            src, dst = src.at[d], dst.at[d]
        remote(src, dst, sends.at[slot, d, step], recvs.at[slot, d, step], (peer, c)).start()


def reduce_finish(parts, rbuf, sends, recvs, slot, r, c, pos, R):
    hops = R // 2
    total = parts[r].astype(F32)
    for d in range(2):
        got = rbuf(d, hops - 1)
        remote(got, got, sends.at[slot, d, hops - 1], recvs.at[slot, d, hops - 1], (r, c)).wait_recv()
        total = total + got[...].astype(F32)
    for d in range(2):
        for step in range(hops):
            src, dst = parts.at[r], rbuf(d, step)
            if step == 0:
                src, dst = src.at[d], dst.at[d]
            remote(src, dst, sends.at[slot, d, step], recvs.at[slot, d, step], (r, c)).wait_send()
    return total


def expert_kernel(
    R, C, CAP, SPLIT,
    e2_all, cot_all, info_all, wbuf, sm,
    ge_parts, mix_parts, mix_out, gg_all, dexp, raw, wfar, bias_out,
    wv, eb, gb, info, X, GR, RES, GE, act, gh, stage, rbuf, corebuf, mixd, fin, ggs,
    w_sem, eb_sem, loc, flow_s, flow_r, red_s, red_r, fin_s, fin_r, core_s, core_r, ge_s, ge_r, mx_s, mx_r, gg_s, gg_r,
):
    r, c = lax.axis_index("row"), lax.axis_index("col")
    pos = ring_place(r, R)
    hops = R // 2
    HB = D // R
    right, left = ring_at(pos + 1, R), ring_at(pos - 1, R)
    core, ypeer, diag = col_core(c), col_y(c), col_diag(c)
    greet([(right, c), (left, c), (r, core), (r, ypeer), (r, diag)])
    NB = C * MICRO
    TR = NB * CAP

    def from_front(k):
        f = col_at(c, k)
        return lambda o: wbuf.at[f, o]

    def far_buf(k):
        return lambda o: wfar.at[k - 2, o]

    def gather(k, s):
        if s >= SPLIT[k]:
            ring_event(
                far_buf(k), flow_s, flow_r, k - 2, s, r, c, pos, R, from_front(k), SPLIT[k]
            )

    def more(k, s):
        if s > SPLIT[k]:
            gather(k, s)

    def weights(k):
        if k < 2:
            return [pltpu.make_async_copy(wbuf.at[col_at(c, k)], wv.at[k], w_sem.at[k, 0])]
        cps = []
        origins = [(r, 0)]
        for s in range(1, hops):
            origins += [(ring_at(pos - s, R), s), (ring_at(pos + s, R), s)]
        origins.append((ring_at(pos + hops, R), hops))
        for n, (o, s) in enumerate(origins):
            src = from_front(k)(o) if s <= SPLIT[k] else far_buf(k)(o)
            cps.append(pltpu.make_async_copy(src, wv.at[k - 2, o], w_sem.at[k, n]))
        return cps

    pending = {k: weights(k) for k in range(2)}
    for cp in pending[0] + pending[1]:
        cp.start()
    get_info = pltpu.make_async_copy(info_all, info, loc.at[0])
    get_info.start()
    gather(2, SPLIT[2])

    def place(p):
        return col_at(c, C - 1 - lax.div(p, MICRO)), lax.rem(p, MICRO)

    def fetch(p, slot, which):
        s, h = place(p)
        src, dst = (e2_all, eb) if which == 0 else (cot_all, gb)
        return pltpu.make_async_copy(
            src.at[s, pl.ds(pl.multiple_of(h * BLK, 16), BLK)], dst.at[slot], eb_sem.at[which, slot]
        )

    slot_id = lax.broadcasted_iota(jnp.int32, (CAP, BLK), 0).astype(F32)

    def pick(p):
        s, h = place(p)
        code = info[s, h, pl.ds(c, 1), :]
        gate = info[s, h, pl.ds(8 + c, 1), :]
        hot = jnp.where(slot_id == code, 1.0, 0.0)
        gate_slot = jnp.sum(hot * gate, axis=1, keepdims=True)
        return hot, gate_slot

    fetch(0, 0, 0).start()
    fetch(0, 0, 1).start()
    get_info.wait()

    def dispatch(p, bias):
        slot = lax.rem(p, 2)

        @pl.when(p + 1 < NB)
        def _():
            fetch(p + 1, 1 - slot, 0).start()
            fetch(p + 1, 1 - slot, 1).start()

        fetch(p, slot, 0).wait()
        fetch(p, slot, 1).wait()
        hot, gate_slot = pick(p)
        hot = hot.astype(BF16)
        rows = pl.ds(pl.multiple_of(p * CAP, 16), CAP)
        X[rows, :] = dot_nn(hot, eb[slot]).astype(BF16)
        g16 = (gate_slot * dot_nn(hot, gb[slot])).astype(BF16)
        GR[rows, :] = g16
        return bias + jnp.sum(g16.astype(F32), axis=0, keepdims=True)

    bias_out[...] = jnp.zeros_like(bias_out)
    out_bias = lax.fori_loop(0, NB // 2, dispatch, jnp.zeros((1, D), F32))
    gather(3, 0)
    bias_out[0:1, :] = lax.fori_loop(NB // 2, NB, dispatch, out_bias)
    more(2, 2)

    def red(k, step):
        reduce_event(stage.at[k], lambda d, s: rbuf.at[k, d, s], red_s, red_r, k, step, r, c, pos, R)

    def red_end(k):
        total = reduce_finish(stage.at[k], lambda d, s: rbuf.at[k, d, s], red_s, red_r, k, r, c, pos, R)
        fin[k] = total.astype(BF16)
        if k == 0:
            cp = pltpu.make_async_copy(fin.at[0], dexp.at[c], loc.at[1])
        else:
            cp = remote(fin.at[1], dexp.at[c], fin_s.at[0], fin_r.at[0], (r, core))
        cp.start()
        return cp

    MT = 512
    DT = D // 2
    HALFR = TR // 2

    def ffn(k, at, n):
        f = col_at(c, k)
        b1 = sm[pl.ds(9 + f, 1), :]
        slot = k % 2

        def tile(m, bias):
            rows = pl.ds(pl.multiple_of(at + m * MT, 16), MT)
            win = wv[slot, :, 0].reshape(D, D)
            wout = wv[slot, :, 1].reshape(D, D)
            hid = dot_nn(X[rows, :], win) + b1
            cdf = 0.5 * (1.0 + lax.erf(hid * (2.0 ** -0.5)))
            a16 = (hid * cdf).astype(BF16)
            act[slot, rows, :] = a16
            slope = cdf + hid * (jnp.exp(-0.5 * hid * hid) * ((2.0 * math.pi) ** -0.5))
            ga = dot_nn(GR[rows, :], wout)
            g16 = (ga * slope).astype(BF16)
            gh[slot, rows, :] = g16
            res = dot_nt(a16, wout)
            gen = dot_nt(g16, win)
            if k == 0:
                RES[rows, :] = res
                GE[rows, :] = gen
            else:
                RES[rows, :] = RES[rows, :] + res
                GE[rows, :] = GE[rows, :] + gen
            return bias + jnp.sum(g16.astype(F32), axis=0, keepdims=True)

        bsum = lax.fori_loop(0, n // MT, tile, jnp.zeros((1, D), F32))
        bias_out[pl.ds(1 + f, 1), :] = bias_out[pl.ds(1 + f, 1), :] + bsum

    def weight_grads(k, first, last):
        slot = k % 2

        def tile(j, _):
            cols = pl.ds(pl.multiple_of(j * DT, 128), DT)
            blocks = pl.ds(j * (R // 2), R // 2)
            stage[k, blocks, 0] = dot_tn(X[:, cols], gh[slot]).astype(BF16).reshape(R // 2, HB, D)
            stage[k, blocks, 1] = dot_tn(GR[:, cols], act[slot]).astype(BF16).reshape(R // 2, HB, D)
            return 0

        lax.fori_loop(first, last, tile, 0)

    order = [diag, ypeer, core, c]
    b2 = sm[8:9, :]
    sends = []

    def give_back(o):
        for h in range(MICRO):
            n = o * MICRO + h
            slot = n % 2
            if n + 1 < NB:
                fetch(n + 1, 1 - slot, 1).start()
            fetch(n, slot, 1).wait()
            if o == 0:
                ge_blk, mx_blk = eb.at[h], mixd.at[h]
            elif o == 1:
                ge_blk, mx_blk = corebuf.at[0, h], corebuf.at[1, h]
            else:
                at = pl.ds((o - 2) * MICRO * BLK + h * BLK, BLK)
                ge_blk, mx_blk = X.at[at], GR.at[at]
            hot, gate_slot = pick(n)
            hot_t = hot.T.astype(BF16)
            rows = slice(n * CAP, (n + 1) * CAP)
            res = (RES[rows, :] + b2).astype(BF16).astype(F32)
            g = dot_nn(hot.astype(BF16), gb[slot])
            gg = jnp.sum(g * res, axis=1, keepdims=True)
            gg_row = jnp.sum(hot * gg, axis=0, keepdims=True)
            mine = lax.broadcasted_iota(jnp.int32, (8, BLK), 0) == c
            ggs[o, h] = jnp.where(mine, gg_row, 0.0)
            ge = dot_nn(hot_t, GE[rows, :].astype(BF16))
            mx = dot_nn(hot_t, (gate_slot * res).astype(BF16))
            part = pl.ds(h * BLK, BLK)
            if o == 1:
                for t in range(2):
                    cb = corebuf.at[t, h]
                    remote(cb, cb, core_s.at[t, h], core_r.at[t, h], (r, core)).wait_recv()
                ge = ge + corebuf[0, h].astype(F32)
                mx = mx + corebuf[1, h].astype(F32)
            ge_blk[...] = ge.astype(BF16)
            mx_blk[...] = mx.astype(BF16)
            if o == 0:
                cps = [
                    remote(ge_blk, corebuf.at[0, h], core_s.at[0, h], core_r.at[0, h], (r, core)),
                    remote(mx_blk, corebuf.at[1, h], core_s.at[1, h], core_r.at[1, h], (r, core)),
                ]
            elif o == 1:
                cps = [
                    remote(ge_blk, ge_parts.at[2, part], ge_s.at[1, h], ge_r.at[1, h], (r, ypeer)),
                    pltpu.make_async_copy(mx_blk, mix_out.at[part], loc.at[4 + h]),
                ]
            elif o == 2:
                cps = [
                    remote(ge_blk, ge_parts.at[1, part], ge_s.at[0, h], ge_r.at[0, h], (r, core)),
                    remote(mx_blk, mix_parts.at[1, part], mx_s.at[h], mx_r.at[h], (r, core)),
                ]
            else:
                cps = [
                    pltpu.make_async_copy(ge_blk, ge_parts.at[0, part], loc.at[6 + h]),
                    pltpu.make_async_copy(mx_blk, mix_parts.at[0, part], loc.at[8 + h]),
                ]
            for cp in cps:
                cp.start()
            sends.append((o, cps))
        if o < 3:
            cp = remote(ggs.at[o], gg_all.at[c], gg_s.at[o], gg_r.at[o], (r, order[o]))
        else:
            cp = pltpu.make_async_copy(ggs.at[3], gg_all.at[c], loc.at[10])
        cp.start()
        sends.append((4 if o < 3 else 5, [cp]))

    def load(k):
        for cp in weights(k):
            cp.start()

    def loaded(k):
        for cp in weights(k):
            cp.wait()

    loaded(0)
    ffn(0, 0, HALFR)
    gather(3, 1)
    ffn(0, HALFR, HALFR)
    weight_grads(0, 0, 2)
    more(2, 3)
    loaded(1)
    ffn(1, 0, HALFR)
    gather(3, 2)
    ring_finish(far_buf(2), flow_s, flow_r, 0, r, c, pos, R, SPLIT[2], hops)
    load(2)
    ffn(1, HALFR, HALFR)
    weight_grads(1, 0, 1)
    gather(3, 3)
    weight_grads(1, 1, 2)
    red(0, 0)
    loaded(2)
    fetch(0, 0, 1).start()
    ffn(2, 0, HALFR)
    ring_finish(far_buf(3), flow_s, flow_r, 1, r, c, pos, R, SPLIT[3], hops)
    load(3)
    red(0, 1)
    red(1, 0)
    loaded(3)
    ffn(3, 0, HALFR)
    red(0, 2)
    give_back(0)
    give_back(1)
    red(1, 1)
    ffn(2, HALFR, HALFR)
    red(0, 3)
    ffn(3, HALFR, HALFR)
    red(1, 2)
    weight_grads(2, 0, 2)
    end0 = red_end(0)
    red(1, 3)
    raws = [pltpu.make_async_copy(stage.at[2], raw.at[0], loc.at[2])]
    raws[0].start()
    weight_grads(3, 0, 2)
    raws.append(pltpu.make_async_copy(stage.at[3], raw.at[1], loc.at[3]))
    raws[1].start()
    give_back(2)
    give_back(3)
    end1 = red_end(1)

    for o, cps in sends:
        for t, cp in enumerate(cps):
            if o == 3 or o == 5 or (o == 1 and t == 1):
                cp.wait()
            else:
                cp.wait_send()
    for h in range(MICRO):
        part = pl.ds(h * BLK, BLK)
        for n2, slot2 in enumerate((1, 2)):
            g_ref = ge_parts.at[slot2, part]
            remote(g_ref, g_ref, ge_s.at[n2, h], ge_r.at[n2, h], (r, core)).wait_recv()
        m_ref = mix_parts.at[1, part]
        remote(m_ref, m_ref, mx_s.at[h], mx_r.at[h], (r, core)).wait_recv()
    for o, peer in enumerate((diag, ypeer, core)):
        g_ref = gg_all.at[peer]
        remote(g_ref, g_ref, gg_s.at[o], gg_r.at[o], (r, peer)).wait_recv()
    end0.wait()
    end1.wait_send()
    d_ref = dexp.at[core]
    remote(d_ref, d_ref, fin_s.at[0], fin_r.at[0], (r, core)).wait_recv()
    for cp in raws:
        cp.wait()


def expert(R, C, CAP, SPLIT, e2_all, cot_all, info_all, wbuf, sm):
    HB = D // R
    hops = R // 2
    TR = C * MICRO * CAP
    vm = pl.BlockSpec(memory_space=pltpu.VMEM)
    hbm = pl.BlockSpec(memory_space=pl.ANY)
    sem = pltpu.SemaphoreType.DMA
    return pl.pallas_call(
        functools.partial(expert_kernel, R, C, CAP, SPLIT),
        name="expert",
        out_shape=(
            jax.ShapeDtypeStruct((3, ROWS, D), BF16),
            jax.ShapeDtypeStruct((2, ROWS, D), BF16),
            jax.ShapeDtypeStruct((ROWS, D), BF16),
            jax.ShapeDtypeStruct((C, MICRO, 8, BLK), F32),
            jax.ShapeDtypeStruct((C, 2, HB, D), BF16),
            jax.ShapeDtypeStruct((2, R, 2, HB, D), BF16),
            jax.ShapeDtypeStruct((2, R, 2, HB, D), BF16),
            jax.ShapeDtypeStruct((8, D), F32),
        ),
        in_specs=[hbm, hbm, hbm, hbm, vm],
        out_specs=(hbm, hbm, hbm, hbm, hbm, hbm, hbm, vm),
        scratch_shapes=[
            pltpu.VMEM((2, R, 2, HB, D), BF16),
            pltpu.VMEM((2, BLK, D), BF16),
            pltpu.VMEM((2, BLK, D), BF16),
            pltpu.VMEM((C, MICRO, 16, BLK), F32),
            pltpu.VMEM((TR, D), BF16),
            pltpu.VMEM((TR, D), BF16),
            pltpu.VMEM((TR, D), F32),
            pltpu.VMEM((TR, D), F32),
            pltpu.VMEM((2, TR, D), BF16),
            pltpu.VMEM((2, TR, D), BF16),
            pltpu.VMEM((C, R, 2, HB, D), BF16),
            pltpu.VMEM((2, 2, hops, 2, HB, D), BF16),
            pltpu.VMEM((2, MICRO, BLK, D), BF16),
            pltpu.VMEM((MICRO, BLK, D), BF16),
            pltpu.VMEM((2, 2, HB, D), BF16),
            pltpu.VMEM((C, MICRO, 8, BLK), F32),
            sem((C, R)), sem((2, 2)), sem((11,)),
            sem((2, 2, hops)), sem((2, 2, hops)),
            sem((2, 2, hops)), sem((2, 2, hops)),
            sem((1,)), sem((1,)),
            sem((2, MICRO)), sem((2, MICRO)),
            sem((2, MICRO)), sem((2, MICRO)),
            sem((MICRO,)), sem((MICRO,)),
            sem((3,)), sem((3,)),
        ],
        compiler_params=pltpu.CompilerParams(
            collective_id=2, has_side_effects=True, vmem_limit_bytes=62 << 20
        ),
    )(e2_all, cot_all, info_all, wbuf, sm)

def back_kernel(
    R, C, E, FFP,
    tok, cot_all, ge_parts, mix_parts, mix_out, gg, rprob, resid_in, qkv_in, mixed_in, probs_in, wg_in, sm, raw, bias_in,
    out, input_grad, attn_grad, proj_grad, dexp, mixy, n1_gain, n1_shift, n2_gain, n2_shift, router_out, pb_out, ab_out, eib_out, eob_out,
    cot, wg, gp, resid, qkv, mixed, probs, stage, rbuf, wp, gbr, dres, gm, e1t, dz, ge1, gblk, corein, yin, apart, abuf, early, late, sbuf, cbuf, rbuf2,
    loc, red_s, red_r, fin_s, fin_r, mix_s, mix_r, ag_s, ag_r, ar_s, ar_r, sm_s, sm_r, lc_s, lc_r, lr_s, lr_r,
):
    r, c = lax.axis_index("row"), lax.axis_index("col")
    pos = ring_place(r, R)
    hops = R // 2
    HB = D // R
    WH = D // C
    W3 = 3 * WH
    heads = WH // HEAD_DIM
    right, left = ring_at(pos + 1, R), ring_at(pos - 1, R)
    core, ypeer, diag = col_core(c), col_y(c), col_diag(c)

    copies = [
        pltpu.make_async_copy(raw, stage, loc.at[0]),
        pltpu.make_async_copy(ge_parts, gp, loc.at[1]),
        pltpu.make_async_copy(resid_in, resid, loc.at[4]),
        pltpu.make_async_copy(cot_all.at[c], cot, loc.at[8]),
        pltpu.make_async_copy(wg_in.at[:, :, pl.ds(0, HB)], wg, loc.at[2]),
    ]
    later = [
        pltpu.make_async_copy(mixed_in, mixed, loc.at[5]),
        pltpu.make_async_copy(qkv_in, qkv, loc.at[6]),
        pltpu.make_async_copy(probs_in, probs, loc.at[7]),
    ]
    for cp in copies:
        cp.start()
    pairs = [(r, core), (r, ypeer)]
    step_bit = 1
    while step_bit < R:
        bit = lax.rem(lax.div(r, step_bit), 2)
        pairs.append((r + step_bit - 2 * step_bit * bit, c))
        step_bit *= 2
    others = [(lax.rem(r + n, R), c) for n in range(1, R)]
    greet([(r, core), (r, ypeer), (r, diag)] + others)

    send_mix = remote(mix_out, mixy, mix_s.at[0], mix_r.at[0], (r, ypeer))
    send_mix.start()
    copies[0].wait()

    def red(k, step):
        reduce_event(stage.at[k], lambda d, s: rbuf.at[k, d, s], red_s, red_r, k, step, r, c, pos, R)

    red(0, 0)
    red(1, 0)
    for cp in copies[1:]:
        cp.wait()
    for cp in later:
        cp.start()
    gain1, shift1 = sm[0:1], sm[1:2]
    gain2, shift2 = sm[2:3], sm[3:4]
    router_b = sm[SMALL : SMALL + 8].astype(BF16)
    router3 = jnp.concatenate([router_b, router_b, router_b], axis=0)
    for g in range(C):
        wp[:, g * WH : (g + 1) * WH] = wg[g, :, :, W3:].reshape(D, WH)
    early[...] = jnp.zeros_like(early)
    late[...] = jnp.zeros_like(late)
    early[16:24, :] = bias_in[...]

    def pair(n):
        size = 16 if n < 2 else 24
        return remote(early.at[pl.ds(0, size)], sbuf.at[n, pl.ds(0, size)], sm_s.at[n], sm_r.at[n], pairs[n])

    def paired(n):
        size = 16 if n < 2 else 24
        pair(n).wait()
        early[0:size, :] = early[0:size, :] + sbuf[n, 0:size, :]
        if n + 1 < len(pairs):
            pair(n + 1).start()


    for h in range(MICRO):
        rp = rprob[h]
        p = gg[0, h]
        for e in range(1, E):
            p = p + gg[e, h]
        gl = rp * (p - jnp.sum(rp * p, axis=0, keepdims=True))
        hi = gl.astype(BF16)
        rest = gl - hi.astype(F32)
        mid = rest.astype(BF16)
        low = (rest - mid.astype(F32)).astype(BF16)
        gl3 = jnp.concatenate([hi.astype(F32), mid.astype(F32), low.astype(F32)], axis=0)
        gl3_t = gl3.T.astype(BF16)
        gl3 = gl3.astype(BF16)
        drt = jnp.zeros((24, D), F32)
        vecs = [jnp.zeros((1, D), F32) for _ in range(3)]
        for i in range(IMG_MB):
            at = h * BLK + i * IMG
            rows = slice(at, at + IMG)
            n2, inv2 = norm_rows(resid[rows, :])
            e2 = (n2 * gain2 + shift2).astype(BF16)
            drt = drt + dot_nn(gl3[:, i * IMG : (i + 1) * IMG], e2)
            ge2 = gp[0, rows, :].astype(F32) + gp[1, rows, :].astype(F32) + gp[2, rows, :].astype(F32)
            ge2 = ge2 + dot_nn(gl3_t[i * IMG : (i + 1) * IMG], router3)
            b = ge2 * gain2
            inner = b - jnp.mean(b, axis=-1, keepdims=True) - n2 * jnp.mean(b * n2, axis=-1, keepdims=True)
            gr = cot[rows, :].astype(F32) + inv2 * inner
            dres[rows, :] = gr
            g16 = gr.astype(BF16)
            gbr[rows, :] = g16
            vecs[0] = vecs[0] + jnp.sum(ge2 * n2, axis=0, keepdims=True)
            vecs[1] = vecs[1] + jnp.sum(ge2, axis=0, keepdims=True)
            vecs[2] = vecs[2] + jnp.sum(g16.astype(F32), axis=0, keepdims=True)
            for g in range(C):
                gm[g, rows, :] = dot_nt(g16, wp[g * WH : (g + 1) * WH, :]).astype(BF16)
            n1, _u = norm_rows(tok[rows, :].astype(F32))
            e1 = n1 * gain1 + shift1
            e1t[h * IMG_MB + i] = e1.T.astype(BF16)
        for n in range(3):
            early[n : n + 1, :] = early[n : n + 1, :] + vecs[n]
        early[8:16, :] = early[8:16, :] + drt[0:8] + drt[8:16] + drt[16:24]
        if h == 1:
            red(0, 1)
    get_mix = pltpu.make_async_copy(mix_parts, gp.at[pl.ds(0, 2)], loc.at[3])
    get_mix.start()
    pair(0).start()
    red(1, 1)
    for cp in later:
        cp.wait()
    for g in range(C):
        dp = dot_tn(mixed[g], gbr[...]).astype(BF16)
        for g2 in range(C):
            gblk[g2, g * WH : (g + 1) * WH, W3:] = dp[:, g2 * WH : (g2 + 1) * WH]

    order = [diag, ypeer, core, c]
    sends = []

    def close(k, peer):
        stage[k, r] = reduce_finish(
            stage.at[k], lambda d, s: rbuf.at[k, d, s], red_s, red_r, k, r, c, pos, R
        ).astype(BF16)
        cp = remote(stage.at[k, r], dexp.at[c], fin_s.at[k], fin_r.at[k], (r, peer))
        cp.start()
        sends.append(cp)

    for o in range(C):
        g = order[o]

        def image(i, vec, g=g):
            rows = pl.ds(pl.multiple_of(i * IMG, 16), IMG)
            z = qkv[g, rows, :]
            gmv = gm[g, rows, :]
            mixv = mixed[g, rows, :]
            dq, dk, dv = [], [], []
            for h in range(heads):
                q = z[:, h * HEAD_DIM : (h + 1) * HEAD_DIM]
                kk = z[:, WH + h * HEAD_DIM : WH + (h + 1) * HEAD_DIM]
                v = z[:, 2 * WH + h * HEAD_DIM : 2 * WH + (h + 1) * HEAD_DIM]
                gmh = gmv[:, h * HEAD_DIM : (h + 1) * HEAD_DIM]
                p16 = probs[g, i, h]
                p = p16.astype(F32)
                w = dot_nt(gmh, v)
                mixh = mixv[:, h * HEAD_DIM : (h + 1) * HEAD_DIM]
                inner = jnp.sum(gmh.astype(F32) * mixh.astype(F32), axis=-1, keepdims=True)
                ds = (p * (w - inner)).astype(BF16)
                dq.append(dot_nn(ds, kk))
                dk.append(dot_tn(ds, q))
                dv.append(dot_tn(p16, gmh))
            d = jnp.concatenate(
                [v.astype(BF16).astype(F32) * SCALE for v in dq] + [v.astype(BF16).astype(F32) for v in dk + dv],
                axis=1,
            )
            dz[rows, :] = d.astype(BF16)
            w = wg[g, :, :, 0:W3].reshape(D, W3)
            part = dot_nt(d.astype(BF16), w)
            ge1[rows, :] = part if o == 0 else ge1[rows, :] + part
            return vec + jnp.sum(d, axis=0, keepdims=True)

        vec = lax.fori_loop(0, IMAGES, image, jnp.zeros((1, W3), F32))
        late[pl.ds(2 + g, 1), 0:W3] = vec
        for j in range(2):
            half = slice(j * (D // 2), (j + 1) * (D // 2))
            acc = jnp.zeros((D // 2, W3), F32)
            for i in range(IMAGES):
                acc = acc + dot_nn(e1t[i, half, :], dz[i * IMG : (i + 1) * IMG, :])
            gblk[g, half, 0:W3] = acc.astype(BF16)
        blk = gblk.at[g]
        if o == 0:
            cp = remote(blk, corein.at[0], ag_s.at[0], ag_r.at[0], (r, core))
            cp.start()
            sends.append(cp)
        elif o == 1:
            remote(blk, corein.at[0], ag_s.at[0], ag_r.at[0], (r, core)).wait_recv()
            blk[...] = (blk[...].astype(F32) + corein[0].astype(F32)).astype(BF16)
            cp = remote(blk, yin, ag_s.at[1], ag_r.at[1], (r, ypeer))
            cp.start()
            sends.append(cp)
        elif o == 2:
            cp = remote(blk, corein.at[1], ag_s.at[2], ag_r.at[2], (r, core))
            cp.start()
            sends.append(cp)
        paired(o)
        if o == 1:
            red(0, 2)
        elif o == 2:
            red(1, 2)
        elif o == 3:
            red(0, 3)
            red(1, 3)
            close(0, ypeer)
            close(1, diag)

    remote(gblk.at[c], corein.at[1], ag_s.at[2], ag_r.at[2], (r, core)).wait_recv()
    remote(gblk.at[c], yin, ag_s.at[1], ag_r.at[1], (r, ypeer)).wait_recv()
    for o in range(R):
        rows = slice(o * HB, (o + 1) * HB)
        tot = gblk[c, rows, :].astype(F32) + corein[1, rows, :].astype(F32) + yin[rows, :].astype(F32)
        apart[o, 0] = tot[0 : HB // 2].astype(BF16)
        apart[o, 1] = tot[HB // 2 :].astype(BF16)

    def ring(step):
        reduce_event(apart, lambda d, s: abuf.at[d, s], ar_s, ar_r, 0, step, r, c, pos, R)

    ring(0)

    def tight(dst, src):
        even = dst.shape[0] // 16 * 16
        dst[0:even, :] = src[0:even, :].astype(BF16)
        dst[even : dst.shape[0], :] = src[even : dst.shape[0], :].astype(BF16)

    dg = jnp.zeros((1, D), F32)
    dsh = jnp.zeros((1, D), F32)
    for i in range(IMAGES):
        rows = slice(i * IMG, (i + 1) * IMG)
        n1, inv1 = norm_rows(tok[rows, :].astype(F32))
        a = ge1[rows, :]
        b = a * gain1
        inner = b - jnp.mean(b, axis=-1, keepdims=True) - n1 * jnp.mean(b * n1, axis=-1, keepdims=True)
        full = dres[rows, :] + inv1 * inner
        dres[i * SEQ : (i + 1) * SEQ, :] = full[:SEQ]
        dg = dg + jnp.sum(a * n1, axis=0, keepdims=True)
        dsh = dsh + jnp.sum(a, axis=0, keepdims=True)
    tight(input_grad, dres)
    late[0:1, :] = dg
    late[1:2, :] = dsh
    cbuf[c] = late[...]
    firsts = [
        remote(late, cbuf.at[c], lc_s.at[n], lc_r.at[n], (r, peer)) for n, peer in enumerate((core, ypeer, diag))
    ]
    for cp in firsts:
        cp.start()
    for n in range(len(order), len(pairs)):
        paired(n)
    turned = pltpu.roll(early[...], lax.rem(D - r * HB, D), 1)
    early_id = lax.broadcasted_iota(jnp.int32, (24, 1), 0)
    n2_gain[...] = turned[0:1, :HB]
    n2_shift[...] = turned[1:2, :HB]
    router_out[...] = jnp.sum(jnp.where(early_id == 8 + c, turned, 0.0), axis=0, keepdims=True)[:, :HB]
    eob_out[...] = turned[16:17, :HB]
    pb_out[...] = pltpu.roll(early[...], lax.rem(D - c * WH, D), 1)[2:3, :WH]
    ff_row = jnp.where(early_id == 17 + lax.div(r * FFP, D), early[...], 0.0)
    ff_row = jnp.broadcast_to(jnp.sum(ff_row, axis=0, keepdims=True), (8, D))
    eib_out[...] = pltpu.roll(ff_row, lax.rem(D - lax.rem(r * FFP, D), D), 1)[0:1, :FFP]
    ring(1)
    for cp in firsts:
        cp.wait()
    tot = cbuf[0]
    for n in range(1, C):
        tot = tot + cbuf[n]
    late[...] = tot
    rbuf2[r] = tot
    seconds = [
        remote(late, rbuf2.at[r], lr_s.at[n], lr_r.at[n], peer) for n, peer in enumerate(others)
    ]
    for cp in seconds:
        cp.start()

    send_mix.wait()
    get_far = pltpu.make_async_copy(mixy, gp.at[2], loc.at[1])
    get_far.start()
    get_mix.wait()
    get_far.wait()
    for i in range(IMAGES):
        rows = slice(i * IMG, (i + 1) * IMG)
        o = resid[rows, :] + gp[0, rows, :].astype(F32) + gp[1, rows, :].astype(F32) + gp[2, rows, :].astype(F32)
        resid[i * SEQ : (i + 1) * SEQ, :] = o[:SEQ]
    tight(out, resid)
    ring(2)
    for cp in seconds:
        cp.wait()
    tot = rbuf2[0]
    for n in range(1, R):
        tot = tot + rbuf2[n]
    turned = pltpu.roll(tot, lax.rem(D - r * HB, D), 1)
    n1_gain[...] = turned[0:1, :HB]
    n1_shift[...] = turned[1:2, :HB]
    mine = jnp.sum(jnp.where(lax.broadcasted_iota(jnp.int32, (8, 1), 0) == 2 + c, tot, 0.0), axis=0, keepdims=True)
    ab_out[0:1, :] = mine[:, :WH]
    ab_out[1:2, :] = mine[:, 2 * WH : W3]
    ring(3)

    total = reduce_finish(apart, lambda d, s: abuf.at[d, s], ar_s, ar_r, 0, r, c, pos, R)
    total = total.reshape(HB, D)
    attn_grad[...] = total[:, :W3]
    proj_grad[...] = total[:, W3:]
    for cp in sends:
        cp.wait_send()
    for k, peer in enumerate((ypeer, diag)):
        d_ref = dexp.at[peer]
        remote(d_ref, d_ref, fin_s.at[k], fin_r.at[k], (r, peer)).wait_recv()


def back(R, C, E, FFP, tok, cot, ge_parts, mix_parts, mix_out, gg, rprob, resid, qkv, mixed, probs, wg, sm, raw, bias):
    HB = D // R
    WH = D // C
    hops = R // 2
    vm = pl.BlockSpec(memory_space=pltpu.VMEM)
    hbm = pl.BlockSpec(memory_space=pl.ANY)
    sem = pltpu.SemaphoreType.DMA
    steps = 2 + int(math.log2(R))
    heads = WH // HEAD_DIM
    return pl.pallas_call(
        functools.partial(back_kernel, R, C, E, FFP),
        name="back",
        out_shape=(
            jax.ShapeDtypeStruct((IMAGES * SEQ, D), BF16),
            jax.ShapeDtypeStruct((IMAGES * SEQ, D), BF16),
            jax.ShapeDtypeStruct((HB, 3 * WH), F32),
            jax.ShapeDtypeStruct((HB, WH), F32),
            jax.ShapeDtypeStruct((C, 2, HB, D), BF16),
            jax.ShapeDtypeStruct((ROWS, D), BF16),
            *[jax.ShapeDtypeStruct((1, HB), F32)] * 5,
            jax.ShapeDtypeStruct((1, WH), F32),
            jax.ShapeDtypeStruct((2, WH), F32),
            jax.ShapeDtypeStruct((1, FFP), F32),
            jax.ShapeDtypeStruct((1, HB), F32),
        ),
        in_specs=[vm, hbm, hbm, hbm, hbm, vm, vm, hbm, hbm, hbm, hbm, hbm, vm, hbm, vm],
        out_specs=(vm, vm, vm, vm, hbm, hbm) + (vm,) * 9,
        scratch_shapes=[
            pltpu.VMEM((ROWS, D), BF16),
            pltpu.VMEM((C, R, HB, D), BF16),
            pltpu.VMEM((3, ROWS, D), BF16),
            pltpu.VMEM((ROWS, D), F32),
            pltpu.VMEM((C, ROWS, 3 * WH), BF16),
            pltpu.VMEM((C, ROWS, WH), BF16),
            pltpu.VMEM((C, IMAGES, heads, IMG, IMG), BF16),
            pltpu.VMEM((2, R, 2, HB, D), BF16),
            pltpu.VMEM((2, 2, hops, 2, HB, D), BF16),
            pltpu.VMEM((D, D), BF16),
            pltpu.VMEM((ROWS, D), BF16),
            pltpu.VMEM((ROWS, D), F32),
            pltpu.VMEM((C, ROWS, WH), BF16),
            pltpu.VMEM((IMAGES, D, IMG), BF16),
            pltpu.VMEM((ROWS, 3 * WH), BF16),
            pltpu.VMEM((ROWS, D), F32),
            pltpu.VMEM((C, D, D), BF16),
            pltpu.VMEM((2, D, D), BF16),
            pltpu.VMEM((D, D), BF16),
            pltpu.VMEM((R, 2, HB // 2, D), BF16),
            pltpu.VMEM((2, hops, 2, HB // 2, D), BF16),
            pltpu.VMEM((24, D), F32),
            pltpu.VMEM((8, D), F32),
            pltpu.VMEM((steps, 24, D), F32),
            pltpu.VMEM((C, 8, D), F32),
            pltpu.VMEM((R, 8, D), F32),
            sem((9,)),
            sem((2, 2, hops)), sem((2, 2, hops)),
            sem((2,)), sem((2,)),
            sem((1,)), sem((1,)),
            sem((3,)), sem((3,)),
            sem((1, 2, hops)), sem((1, 2, hops)),
            sem((steps,)), sem((steps,)),
            sem((C - 1,)), sem((C - 1,)),
            sem((R - 1,)), sem((R - 1,)),
        ],
        compiler_params=pltpu.CompilerParams(
            collective_id=3, has_side_effects=True, vmem_limit_bytes=62 << 20
        ),
    )(tok, cot, ge_parts, mix_parts, mix_out, gg, rprob, resid, qkv, mixed, probs, wg, sm, raw, bias)

def prepare(R, C, tokens, cotangent, routes, norm1_gain, norm1_shift, attn_in, attn_bias, attn_proj,
            proj_bias, norm2_gain, norm2_shift, router, expert_in, expert_in_bias, expert_out, expert_out_bias):
    HB, WH = D // R, D // C
    smalls = (
        norm1_gain[None], norm1_shift[None], norm2_gain[None], norm2_shift[None], attn_bias, proj_bias[None],
        router.reshape(1, HB), expert_out_bias, expert_in_bias,
    )
    packed = jnp.concatenate([attn_in.reshape(HB, 3 * WH), attn_proj], axis=1)
    wexp = jnp.stack([expert_in, jnp.swapaxes(expert_out, 1, 2)], axis=1)
    named = routes.astype(F32).T.reshape(2, IMAGES, SEQ)
    named = jnp.pad(named, ((0, 6), (0, 0), (0, IMG - SEQ)), constant_values=-1.0)
    rt = jnp.swapaxes(named.reshape(8, MICRO, BLK), 0, 1)
    return packed, smalls, wexp, rt

SPLIT = (4, 4, 1, 0)


def rings(
    tokens, cotangent, routes, norm1_gain, norm1_shift, attn_in, attn_bias, attn_proj, proj_bias,
    norm2_gain, norm2_shift, router, expert_in, expert_in_bias, expert_out, expert_out_bias,
):
    R, C = lax.axis_size("row"), lax.axis_size("col")
    E = expert_in.shape[0]
    HB, WH = D // R, D // C
    rows_mb = IMG_MB * SEQ
    cap = (2 * rows_mb * 13 // (10 * E) + 7) // 8 * 8
    cap = (cap + 15) // 16 * 16
    packed, smalls, wexp, rt = prepare(
        R, C, tokens, cotangent, routes, norm1_gain, norm1_shift, attn_in, attn_bias, attn_proj, proj_bias,
        norm2_gain, norm2_shift, router, expert_in, expert_in_bias, expert_out, expert_out_bias,
    )
    wbuf, e2_all, cot_all, info_all, tok, wg, qkv, mixed, probs, resid, rprob, sm = front(
        R, C, E, SPLIT, expert_in_bias.shape[1], tokens, cotangent, packed, smalls, wexp, rt
    )
    ge_parts, mix_parts, mix_out, gg, dexp_a, raw, _, bias = expert(
        R, C, cap, SPLIT, e2_all, cot_all, info_all, wbuf, sm
    )
    out, input_grad, attn_grad, proj_grad, dexp_b, _, n1g, n1s, n2g, n2s, grad_router, grad_pb, grad_ab, grad_eib, grad_eob = back(
        R, C, E, expert_in_bias.shape[1], tok, cot_all, ge_parts, mix_parts, mix_out, gg, rprob, resid, qkv, mixed, probs, wg, sm, raw, bias
    )
    c = lax.axis_index("col")
    e = lax.broadcasted_iota(jnp.int32, (E, 1, 1, 1), 0)
    near = lax.div(e, 2) == lax.div(c, 2)
    dexp = jnp.where(near, dexp_a, dexp_b).astype(F32)
    return (
        out,
        input_grad,
        n1g.reshape(HB),
        n1s.reshape(HB),
        attn_grad.reshape(HB, 3, WH),
        grad_ab,
        proj_grad,
        grad_pb.reshape(WH),
        n2g.reshape(HB),
        n2s.reshape(HB),
        grad_router.reshape(HB, 1),
        dexp[:, 0],
        grad_eib,
        jnp.swapaxes(dexp[:, 1], 1, 2),
        grad_eob,
    )


def solution(mesh):
    in_specs = (
        P(("row", "col"), None),
        P(("row", "col"), None),
        P(("row", "col"), None),
        P("row"),
        P("row"),
        P("row", None, "col"),
        P(None, "col"),
        P("row", "col"),
        P("col"),
        P("row"),
        P("row"),
        P("row", "col"),
        P(None, "row", "col"),
        P("col", "row"),
        P(None, "col", "row"),
        P("col", "row"),
    )
    out_specs = (
        P(("row", "col"), None),
        P(("row", "col"), None),
        P("row"),
        P("row"),
        P("row", None, "col"),
        P(None, "col"),
        P("row", "col"),
        P("col"),
        P("row"),
        P("row"),
        P("row", "col"),
        P(None, "row", "col"),
        P("col", "row"),
        P(None, "col", "row"),
        P("col", "row"),
    )
    body = rings if (mesh.shape["row"], mesh.shape["col"]) == (8, 4) else shards
    return jax.shard_map(body, mesh=mesh, in_specs=in_specs, out_specs=out_specs, check_vma=False)
```
